128 devices in a mesh: owner: 128 (over y, z, x, core).
Axes of the slice: x: 4, y: 4, z: 4, core: 2. Of those that a mesh axis runs over, the one named last changes fastest.
Arguments:
- coarse: float32 [128, 3, 256, 256], P('owner'), may hold values from 0 to 1.5
- parents: int32 [256], P('owner'), may hold values from 0 to 3, as said below
- new_counts: int32 [128], replicated, may hold values from 1 to 3, as said below
- neighbours: int32 [256, 4], replicated, may hold values from -1 to 255, as said below
- land_cover: int32 [384, 256, 256], P('owner'), may hold values from 0 to 10
- class_diffusivity: float32 [11], replicated, may hold values from 0.05 to 0.25
- class_growth: float32 [11], replicated, may hold values from 0.2 to 1
Outputs:
- fields: float32 [384, 3, 256, 256], P('owner')
The draws below stay inside these ranges and needn't reach their ends.
Inputs may be any that keep to these rules, and one draw needn't show every extreme that they name: `parents`: within the 2 entries of one old owner the values differ; value p names quadrant p % 4 of the owner's local coarse patch p // 4. `new_counts`: each aligned block of 2 owners holds 4 patches in all; every owner holds at least one. The table is symmetric: if h = neighbours[g, f] is not -1, then neighbours[h, f ^ 1] = g. A neighbour's index differs from g by at most 3; -1 marks the domain's edge.
All inputs are finite; a program needn't handle non-finite values.
Results may differ from the reference program's by a relative error of at most 0.00005.
Values sent between devices are 32-bit elements; how exact they have to be, the bound alone decides.
A program may use at most 128 MiB of HBM per device.

```python
import math
import jax
import jax.numpy as jnp
from jax import lax

P_SIZE = 256
HALF = 128
CLASSES = 11
ROWS_P = 2
GROUP = 2
NEW_DEV = 2
CAP = 3
COARSE_DEV = 1
NPATCH = 256
N_OWNER = 128


def draw_new_counts(key, part):
    key = jax.random.fold_in(key, 11)
    groups = N_OWNER // GROUP
    first_counts = 1 + jax.random.randint(key, (groups,), 0, CAP)
    first_counts = first_counts.at[0].set(CAP)
    first_counts = first_counts.at[groups - 2].set(CAP)
    first_counts = first_counts.at[groups - 1].set(1)
    first_counts = first_counts.at[N_OWNER // 4].set(CAP)
    second_counts = GROUP * NEW_DEV - first_counts
    return jnp.stack([first_counts, second_counts], axis=1).reshape(N_OWNER).astype(jnp.int32)


def draw_neighbours(key, part):
    key = jax.random.fold_in(key, 23)
    columns = NPATCH // ROWS_P
    upward = jax.random.randint(key, (columns,), 0, 2)
    upward = upward.at[0].set(0).at[1].set(1)
    column_ids = jnp.arange(columns)[:, None]
    row_ids = jnp.arange(ROWS_P)[None, :]

    def curve_index(column, row):
        reversed_col = upward[jnp.clip(column, 0, columns - 1)]
        return column * ROWS_P + jnp.where(reversed_col == 1, ROWS_P - 1 - row, row)
    shape_full = (columns, ROWS_P)
    own_ids = jnp.broadcast_to(curve_index(column_ids, row_ids), shape_full)
    west_ids = jnp.broadcast_to(jnp.where(column_ids > 0, curve_index(column_ids - 1, row_ids), -1), shape_full)
    east_ids = jnp.broadcast_to(jnp.where(column_ids < columns - 1, curve_index(column_ids + 1, row_ids), -1), shape_full)
    south_ids = jnp.broadcast_to(jnp.where(row_ids > 0, curve_index(column_ids, row_ids - 1), -1), shape_full)
    north_ids = jnp.broadcast_to(jnp.where(row_ids < ROWS_P - 1, curve_index(column_ids, row_ids + 1), -1), shape_full)
    listing = jnp.stack([west_ids, east_ids, south_ids, north_ids], axis=-1).reshape(NPATCH, 4)
    return jnp.zeros((NPATCH, 4), jnp.int32).at[own_ids.reshape(NPATCH)].set(listing.astype(jnp.int32))


def draw_parents(key, part):
    key = jax.random.fold_in(key, 37)
    owner_keys = jax.random.split(key, N_OWNER)

    def one_owner(owner_key):
        return jax.random.permutation(owner_key, 4 * COARSE_DEV)[:NEW_DEV]
    return jax.vmap(one_owner)(owner_keys).reshape(NPATCH).astype(jnp.int32)


def with_ends(drawn, rng, smallest, high):
    place = [jax.random.randint(jax.random.fold_in(rng, axis), (), 0, length) for axis, length in enumerate(drawn.shape)]
    longest = drawn.shape.index(max(drawn.shape))
    next_to = place[:longest] + [(place[longest] + 1) % drawn.shape[longest]] + place[longest + 1:]
    return drawn.at[tuple(place)].set(smallest).at[tuple(next_to)].set(high)


def block_levels(stream_key, dims, cuts, least, largest):
    factor_of = 1.0
    for position, shards_of in cuts:
        heights = jax.random.uniform(jax.random.fold_in(jax.random.fold_in(stream_key, 6), position), (shards_of,), jnp.float32, least / len(cuts), largest / len(cuts))
        factor_of = factor_of * jnp.repeat(jnp.exp(heights), dims[position] // shards_of).reshape((-1,) + (1,) * (len(dims) - 1 - position))
    return factor_of


def setup_inputs(seed: int = 0) -> dict:
    keys = jax.random.split(jax.random.key(seed), 8)
    return {
        "coarse": jnp.clip(1.5 * jax.random.uniform(keys[0], (N_OWNER * COARSE_DEV, 3, P_SIZE, P_SIZE), jnp.float32) ** block_levels(keys[0], (N_OWNER * COARSE_DEV, 3, P_SIZE, P_SIZE), ((0, 128),), -0.2, 0.2), 0.0, 1.5),
        "parents": draw_parents(jax.random.fold_in(keys[7], 71), 0),
        "new_counts": draw_new_counts(jax.random.fold_in(keys[7], 71), 0),
        "neighbours": draw_neighbours(jax.random.fold_in(keys[7], 71), 0),
        "land_cover": with_ends(jax.random.randint(keys[4], (N_OWNER * CAP, P_SIZE, P_SIZE), 0, CLASSES), jax.random.fold_in(keys[4], 1), 0, CLASSES - 1).astype(jnp.int32),
        "class_diffusivity": jnp.clip(jnp.exp(jax.random.uniform(keys[5], (CLASSES,), jnp.float32, math.log(0.05), math.log(0.25))), 0.05, 0.25),
        "class_growth": jnp.clip(jnp.exp(jax.random.uniform(keys[6], (CLASSES,), jnp.float32, math.log(0.2), math.log(1.0))), 0.2, 1.0),
    }


full_precision = lax.Precision.HIGHEST


def prolong_table(fine_len):
    coarse_len = fine_len // 2
    fine_index = jnp.arange(fine_len, dtype=jnp.int32)
    nearest = fine_index // 2
    second = jnp.clip(jnp.where(fine_index % 2 == 0, nearest - 1, nearest + 1), 0, coarse_len - 1)
    column = jnp.arange(coarse_len, dtype=jnp.int32)
    heavy = (column[None, :] == nearest[:, None]).astype(jnp.float32)
    light = (column[None, :] == second[:, None]).astype(jnp.float32)
    return 0.75 * heavy + 0.25 * light


def prolong(quarter_blocks):
    table = prolong_table(2 * quarter_blocks.shape[-1])
    rows_done = jnp.einsum("ia,ncab->ncib", table, quarter_blocks, precision=full_precision)
    return jnp.einsum("ncib,jb->ncij", rows_done, table, precision=full_precision)


def edge_faces(fields_now):
    return jnp.stack([fields_now[:, :, :, 0], fields_now[:, :, :, -1], fields_now[:, :, 0, :], fields_now[:, :, -1, :]], axis=1)


def laplacian(fields_now, ghosts):
    sideways = jnp.concatenate([ghosts[:, 0][:, :, :, None], fields_now, ghosts[:, 1][:, :, :, None]], axis=3)
    upright = jnp.concatenate([ghosts[:, 2][:, :, None, :], fields_now, ghosts[:, 3][:, :, None, :]], axis=2)
    return (sideways[:, :, :, :-2] + sideways[:, :, :, 2:]) + (upright[:, :, :-2, :] + upright[:, :, 2:, :]) - 4.0 * fields_now


def tendency(fields_now, ghosts, diffus, growth):
    laplace_terms = laplacian(fields_now, ghosts)
    invader = fields_now[:, 0]
    resource = fields_now[:, 1]
    inhibitor = fields_now[:, 2]
    d_invader = diffus * laplace_terms[:, 0] + growth * invader * (resource - invader - inhibitor)
    d_resource = 0.5 * diffus * laplace_terms[:, 1] + 0.4 * (1.0 - resource) - invader * resource
    d_inhibitor = diffus * laplace_terms[:, 2] + invader - 0.3 * inhibitor
    return jnp.stack([d_invader, d_resource, d_inhibitor], axis=1)


def advance(fields_now, diffus, growth, ghost_fn):
    rate_one = tendency(fields_now, ghost_fn(fields_now), diffus, growth)
    section_two = fields_now + 0.5 * rate_one
    rate_two = tendency(section_two, ghost_fn(section_two), diffus, growth)
    section_three = fields_now + 0.5 * rate_two
    rate_three = tendency(section_three, ghost_fn(section_three), diffus, growth)
    section_four = fields_now + rate_three
    rate_four = tendency(section_four, ghost_fn(section_four), diffus, growth)
    return fields_now + (rate_one + 2.0 * rate_two + 2.0 * rate_three + rate_four) / 6.0


def reference(coarse, parents, new_counts, neighbours, land_cover, class_diffusivity, class_growth):
    patch_ids = jnp.arange(NPATCH, dtype=jnp.int32)
    slot_ends = jnp.cumsum(new_counts).astype(jnp.int32)
    starts = (slot_ends - new_counts).astype(jnp.int32)
    owner_new = jnp.sum((slot_ends[None, :] <= patch_ids[:, None]).astype(jnp.int32), axis=1).astype(jnp.int32)
    slot_index = (owner_new * CAP + patch_ids - starts[owner_new]).astype(jnp.int32)
    classes = land_cover[slot_index]
    diffus = class_diffusivity[classes]
    growth = class_growth[classes]
    local_coarse = ((patch_ids // NEW_DEV) * COARSE_DEV + parents // 4).astype(jnp.int32)
    quadrant = (parents % 4).astype(jnp.int32)
    coarse_split = coarse.reshape(N_OWNER * COARSE_DEV, 3, 2, HALF, 2, HALF)
    quarter_blocks = coarse_split[local_coarse, :, quadrant // 2, :, quadrant % 2, :]
    fine_fields = prolong(quarter_blocks)
    safe_rows = jnp.maximum(neighbours, 0).astype(jnp.int32)
    face_index = jnp.arange(4, dtype=jnp.int32)[None, :]
    has_peer = (neighbours >= 0)[:, :, None, None]

    def ghost_fn(fields_now):
        faces = edge_faces(fields_now)
        opposite = jnp.stack([faces[:, 1], faces[:, 0], faces[:, 3], faces[:, 2]], axis=1)
        return jnp.where(has_peer, opposite[safe_rows, face_index], faces)

    advanced = advance(fine_fields, diffus, growth, ghost_fn)
    result = jnp.zeros((N_OWNER * CAP, 3, P_SIZE, P_SIZE), advanced.dtype)
    return result.at[slot_index].set(advanced)
```

```python
import functools

import jax
import jax.numpy as jnp
from jax import lax
from jax.experimental import pallas as pl
from jax.experimental.pallas import tpu as pltpu
from jax.sharding import PartitionSpec as P

SIDE = 256
HALF = 128
CLASSES = 11
PAD = 8
WEIGHTS = (0.5, 0.5, 1.0, 1.0 / 6.0)
MESH = pl.DeviceIdType.MESH


def iota(shape, dim):
    return lax.broadcasted_iota(jnp.int32, shape, dim)


def prolong_weights(fine, coarse):
    near = fine >> 1
    second = jnp.clip(near + jnp.where((fine & 1) == 0, -1, 1), 0, HALF - 1)
    heavy = jnp.where(coarse == near, 0.75, 0.0)
    light = jnp.where(coarse == second, 0.25, 0.0)
    return (heavy + light).astype(jnp.bfloat16)


def split(block, axis):
    high = block.astype(jnp.bfloat16)
    low = (block - high.astype(jnp.float32)).astype(jnp.bfloat16)
    return jnp.concatenate([high, low], axis=axis)


def dot(a, b):
    return jnp.dot(a, b, preferred_element_type=jnp.float32)


def dot_t(a, b):
    return lax.dot_general(a, b, (((1,), (1,)), ((), ())), preferred_element_type=jnp.float32)


def look_up(classes, diff_ref, grow_ref):
    diffus = jnp.full(classes.shape, diff_ref[0], jnp.float32)
    growth = jnp.full(classes.shape, grow_ref[0], jnp.float32)
    for number in range(1, CLASSES):
        hit = classes == jnp.asarray(number, classes.dtype)
        diffus = jnp.where(hit, diff_ref[number], diffus)
        growth = jnp.where(hit, grow_ref[number], growth)
    return diffus, growth


def scaled_rates(weight, x0, x1, x2, lap0, lap1, lap2, diffus, growth):
    dw = diffus * weight
    gw = growth * weight
    xw = x0 * weight
    r0 = dw * lap0 + (gw * x0) * (x1 - x0 - x2)
    r1 = (0.5 * dw) * lap1 + (0.4 * weight - x1 * (0.4 * weight + xw))
    r2 = dw * lap2 + (xw - (0.3 * weight) * x2)
    return r0, r1, r2


def combine(x, s2, s3, s4, rate):
    return (s2 + 2.0 * s3 + s4 - x) * (1.0 / 3.0) + rate


def kernel(
    owners,
    parents_ref,
    counts_ref,
    nb_ref,
    diff_ref,
    grow_ref,
    coarse_ref,
    land_ref,
    out_ref,
    quads,
    land,
    x_buf,
    s2_buf,
    s3_buf,
    s4_buf,
    diffus_buf,
    growth_buf,
    result,
    ring,
    across,
    t0,
    t1,
    t2,
    t3,
    strip_diffus,
    strip_growth,
    f0,
    f1,
    f2,
    f3,
    load_sem,
    land_sem,
    face_send,
    face_recv,
    pair_send,
    pair_recv,
):
    me = lax.axis_index("owner")
    parity = me % 2
    partner = me + 1 - 2 * parity
    moving = 1 - parity
    up1, up2 = (me + 1) % owners, (me + 2) % owners
    dn1, dn2 = (me + owners - 1) % owners, (me + owners - 2) % owners
    stages = (x_buf, s2_buf, s3_buf, s4_buf)
    strips = (t0, t1, t2, t3)
    faces = (f0, f1, f2, f3)

    loads = []
    for q in range(4):
        block = coarse_ref.at[0, :, pl.ds((q // 2) * HALF, HALF), pl.ds((q % 2) * HALF, HALF)]
        loads.append(pltpu.make_async_copy(block, quads.at[q], load_sem.at[q]))
    for load in loads:
        load.start()
    land_load = pltpu.make_async_copy(land_ref, land.at[pl.ds(0, 3)], land_sem)
    land_load.start()
    barrier = pltpu.get_barrier_semaphore()
    for other in (up1, dn1, up2, dn2):
        pl.semaphore_signal(barrier, inc=1, device_id=(other,), device_id_type=MESH)

    shape = (SIDE, SIDE)
    columns_up = prolong_weights(iota(shape, 1), iota(shape, 0) & (HALF - 1))
    rows_up = prolong_weights(iota(shape, 0), iota(shape, 1) & (HALF - 1))
    edge = iota((16, SIDE), 0)
    edge = jnp.where(edge < 8, edge, edge + (SIDE - 16))
    edge_up = prolong_weights(edge, iota((16, SIDE), 1) & (HALF - 1))
    edge_pick = jnp.where(iota((16, SIDE), 1) == edge, 1.0, 0.0).astype(jnp.bfloat16)
    for buf in stages:
        for i in range(2):
            for c in range(3):
                for j in range(2):
                    buf[i, c, j, 0:PAD] = jnp.zeros((PAD, HALF), jnp.float32)
                    buf[i, c, j, PAD + SIDE :] = jnp.zeros((PAD, HALF), jnp.float32)

    def send_faces(s, start):
        f = faces[s]
        copies = [
            (f.at[pl.ds(3, 2)], f.at[pl.ds(1, 2)], up1),
            (f.at[pl.ds(3, 2)], f.at[pl.ds(5, 2)], dn1),
            (f.at[4], f.at[0], up2),
            (f.at[3], f.at[7], dn2),
        ]
        made = []
        for n, (src, dst, to) in enumerate(copies):
            made.append(
                pltpu.make_async_remote_copy(
                    src_ref=src,
                    dst_ref=dst,
                    send_sem=face_send.at[s, n],
                    recv_sem=face_recv.at[s, n],
                    device_id=(to,),
                    device_id_type=MESH,
                )
            )
        if start:
            for copy in made:
                copy.start()
        return made

    def put_faces(s, c, block):
        for i in range(2):
            for f in range(4):
                row = 7 * (f % 2)
                faces[s][3 + i, 4 * f + c : 4 * f + c + 1, :] = block[4 * i + f, row : row + 1, :]

    for load in loads:
        load.wait()
    parent = [parents_ref[i] % 4 for i in range(2)]
    edges = []
    for i in range(2):
        for c in range(3):
            block = quads[parent[i], c]
            edges.append(dot_t(edge_up, split(block, 1)))
            edges.append(dot(edge_up, split(block, 0)))
    edges = dot(split(jnp.concatenate(edges, axis=0), 1), columns_up).reshape(2, 3, 4, 8, SIDE)
    for c in range(3):
        block = jnp.concatenate([edges[0, c], edges[1, c]], axis=0)
        t0[c] = block
        put_faces(0, c, block)

    pl.semaphore_wait(barrier, 4)
    sent = send_faces(0, True)
    land_copy = pltpu.make_async_remote_copy(
        src_ref=land_ref.at[2 * (1 - parity)],
        dst_ref=land.at[3],
        send_sem=pair_send.at[0],
        recv_sem=pair_recv.at[0],
        device_id=(partner,),
        device_id_type=MESH,
    )
    land_copy.start()

    for i in range(2):
        for c in range(3):
            half_done = dot(split(quads[parent[i], c], 1), columns_up)
            fine = dot(rows_up, split(half_done, 0))
            for j in range(2):
                x_buf[i, c, j, PAD : PAD + SIDE] = fine[:, j * HALF : (j + 1) * HALF]

    land_load.wait()
    land_copy.wait_recv()
    count = counts_ref[me]
    slots = []
    for i in range(2):
        even_slot = jnp.where(i >= count, 3, i)
        odd_slot = jnp.where(i - 2 + count < 0, 3, i - 2 + count)
        slots.append(jnp.where(parity == 0, even_slot, odd_slot))
    for i in range(2):
        picked = dot_t(edge_pick, land[slots[i]].astype(jnp.float32).astype(jnp.bfloat16))
        across_d, across_g = look_up(picked, diff_ref, grow_ref)
        ends = jnp.concatenate(
            [land[slots[i], 0:8, :], land[slots[i], SIDE - 8 : SIDE, :]], axis=0
        )
        along_d, along_g = look_up(ends, diff_ref, grow_ref)
        for n in range(2):
            rows = slice(8 * n, 8 * n + 8)
            strip_diffus[4 * i + n] = across_d[rows]
            strip_growth[4 * i + n] = across_g[rows]
            strip_diffus[4 * i + 2 + n] = along_d[rows]
            strip_growth[4 * i + 2 + n] = along_g[rows]

        def fill(step, carry, i=i):
            r = pl.multiple_of(step * 8, 8)
            for j in range(2):
                d, g = look_up(
                    land[slots[i], pl.ds(r, 8), j * HALF : (j + 1) * HALF], diff_ref, grow_ref
                )
                diffus_buf[i, j, pl.ds(r, 8), :] = d
                growth_buf[i, j, pl.ds(r, 8), :] = g
            return carry

        lax.fori_loop(0, SIDE // 8, fill, 0)

    peers = []
    for i in range(2):
        for f in range(4):
            value = nb_ref[2 * me + i, f]
            peers.append((value >= 0, jnp.clip(value - (2 * me - 3), 0, 7)))

    strip = (8, 8, SIDE)
    sub = iota(strip, 1)
    lane = iota(strip, 2)
    sub_half = iota((8, 8, HALF), 1)
    lane_half = iota((8, 8, HALF), 2)

    def strip_laplacian(s, c):
        now = strips[s][c]
        f_ref = faces[s]
        ghosts = []
        for i in range(2):
            for f in range(4):
                has, where = peers[4 * i + f]
                theirs = 4 * (f ^ 1) + c
                ours = 4 * f + c
                row = jnp.where(
                    has, f_ref[where, theirs : theirs + 1, :], f_ref[3 + i, ours : ours + 1, :]
                )
                ghosts.append(jnp.broadcast_to(row, (8, SIDE)))
        ghost = jnp.stack(ghosts, axis=0)
        low = jnp.sum(
            jnp.where(lane_half == sub_half, ghost[:, :, :HALF], 0.0), axis=2, keepdims=True
        )
        high = jnp.sum(
            jnp.where(lane_half == sub_half + (HALF - 8), ghost[:, :, HALF:], 0.0),
            axis=2,
            keepdims=True,
        )
        ends = []
        for e in range(2):
            columns = []
            for i in range(2):
                for f in range(4):
                    source = (low, high)[f % 2]
                    face = 4 * i + (2 if f < 2 else 0) + e
                    columns.append(source[face])
            ends.append(jnp.stack(columns, axis=0))
        above = jnp.where(sub == 0, ghost, pltpu.roll(now, 1, 1))
        below = jnp.where(sub == 7, ghost, pltpu.roll(now, 7, 1))
        left = jnp.where(lane == 0, ends[0], pltpu.roll(now, 1, 2))
        right = jnp.where(lane == SIDE - 1, ends[1], pltpu.roll(now, SIDE - 1, 2))
        return now, (left + right) + (below + above) - 4.0 * now

    def strip_stage(s):
        values = [strip_laplacian(s, c) for c in range(3)]
        rates = scaled_rates(
            WEIGHTS[s],
            *[v[0] for v in values],
            *[v[1] for v in values],
            strip_diffus[...],
            strip_growth[...],
        )
        for c in range(3):
            if s < 3:
                block = t0[c] + rates[c]
                strips[s + 1][c] = block
                put_faces(s + 1, c, block)
            else:
                block = combine(t0[c], t1[c], t2[c], t3[c], rates[c])
                for i in range(2):
                    ring[i, c] = block[4 * i : 4 * i + 4]

    first_lane = iota((8, HALF), 1) == 0
    last_lane = iota((8, HALF), 1) == HALF - 1

    def bulk_stage(i, s):
        src = stages[s]

        def step_rows(step, carry):
            r = pl.multiple_of(step * 8, 8)
            at = PAD + r
            now = [[None, None] for _ in range(3)]
            lap = [[None, None] for _ in range(3)]
            for c in range(3):
                a = src[i, c, 0, pl.ds(at, 8), :]
                b = src[i, c, 1, pl.ds(at, 8), :]
                now[c] = [a, b]
                a_right, b_right = pltpu.roll(a, 1, 1), pltpu.roll(b, 1, 1)
                a_left, b_left = pltpu.roll(a, HALF - 1, 1), pltpu.roll(b, HALF - 1, 1)
                sides = [
                    a_right + jnp.where(last_lane, b_left, a_left),
                    jnp.where(first_lane, a_right, b_right) + b_left,
                ]
                for j in range(2):
                    above = src[i, c, j, pl.ds(at - 1, 8), :]
                    below = src[i, c, j, pl.ds(at + 1, 8), :]
                    lap[c][j] = sides[j] + (below + above) - 4.0 * now[c][j]
            for j in range(2):
                rates = scaled_rates(
                    WEIGHTS[s],
                    *[now[c][j] for c in range(3)],
                    *[lap[c][j] for c in range(3)],
                    diffus_buf[i, j, pl.ds(r, 8), :],
                    growth_buf[i, j, pl.ds(r, 8), :],
                )
                for c in range(3):
                    base = now[c][j] if s == 0 else x_buf[i, c, j, pl.ds(at, 8), :]
                    if s < 3:
                        stages[s + 1][i, c, j, pl.ds(at, 8), :] = base + rates[c]
                    else:
                        result[i, c, j, pl.ds(r, 8), :] = combine(
                            base,
                            s2_buf[i, c, j, pl.ds(at, 8), :],
                            s3_buf[i, c, j, pl.ds(at, 8), :],
                            now[c][j],
                            rates[c],
                        )
            return carry

        lax.fori_loop(0, SIDE // 8, step_rows, 0, unroll=2)

    result_copy = pltpu.make_async_remote_copy(
        src_ref=result.at[moving],
        dst_ref=result.at[2],
        send_sem=pair_send.at[1],
        recv_sem=pair_recv.at[1],
        device_id=(partner,),
        device_id_type=MESH,
    )
    ring_copy = pltpu.make_async_remote_copy(
        src_ref=ring.at[moving],
        dst_ref=ring.at[2],
        send_sem=pair_send.at[2],
        recv_sem=pair_recv.at[2],
        device_id=(partner,),
        device_id_type=MESH,
    )
    gaps = (((moving, 0), (moving, 1), (moving, 2)), ((moving, 3), (parity, 0), (parity, 1)), ((parity, 2), (parity, 3)))
    for s in range(4):
        for copy in sent[4 * s : 4 * s + 4]:
            copy.wait_recv()
        strip_stage(s)
        if s < 3:
            sent = sent + send_faces(s + 1, True)
            for i, stage in gaps[s]:
                bulk_stage(i, stage)
                if s == 1 and stage == 3:
                    result_copy.start()
    ring_copy.start()

    def turn(e):
        for c in range(3):
            block = jnp.concatenate(
                [ring[e, c, 0], jnp.zeros((HALF - 16, SIDE), jnp.float32), ring[e, c, 1]], axis=0
            )
            across[e, c, 0:HALF] = block[:, :HALF].T
            across[e, c, HALF:SIDE] = block[:, HALF:].T

    turn(0)
    turn(1)
    result_copy.wait_recv()
    ring_copy.wait_recv()
    turn(2)

    low_lanes = iota((8, HALF), 1) < 4
    high_lanes = iota((8, HALF), 1) >= HALF - 4
    sub_rows = iota((8, SIDE), 0)
    sources = []
    for s in range(3):
        from_even = s
        from_odd = (5 - count + s) % 3
        sources.append((jnp.where(parity == 0, from_even, from_odd), s < count))

    def place(step, carry):
        r = pl.multiple_of(step * 8, 8)
        for s in range(3):
            e, held = sources[s]
            for c in range(3):
                side = across[e, c, pl.ds(r, 8), :]
                left = jnp.where(low_lanes, side, result[e, c, 0, pl.ds(r, 8), :])
                right = jnp.where(high_lanes, side, result[e, c, 1, pl.ds(r, 8), :])
                out_ref[s, c, pl.ds(r, 8), 0:HALF] = jnp.where(held, left, 0.0)
                out_ref[s, c, pl.ds(r, 8), HALF:SIDE] = jnp.where(held, right, 0.0)
        return carry

    lax.fori_loop(0, SIDE // 8, place, 0)
    for s in range(3):
        e, held = sources[s]
        for c in range(3):
            for n, rows in ((0, slice(0, 8)), (1, slice(SIDE - 8, SIDE))):
                inside = sub_rows < 4 if n == 0 else sub_rows >= 4
                merged = jnp.where(inside, ring[e, c, 2 + n], out_ref[s, c, rows, :])
                out_ref[s, c, rows, :] = jnp.where(held, merged, 0.0)

    for copy in sent:
        copy.wait_send()
    land_copy.wait_send()
    result_copy.wait_send()
    ring_copy.wait_send()


def body(coarse, parents, new_counts, neighbours, land_cover, class_diffusivity, class_growth):
    owners = lax.axis_size("owner")
    f32 = jnp.float32
    smem = pl.BlockSpec(memory_space=pltpu.SMEM)
    hbm = pl.BlockSpec(memory_space=pl.ANY)
    stage_buf = pltpu.VMEM((2, 3, 2, SIDE + 2 * PAD, HALF), f32)
    strip_buf = pltpu.VMEM((3, 8, 8, SIDE), f32)
    face_buf = pltpu.VMEM((8, 16, SIDE), f32)
    return pl.pallas_call(
        functools.partial(kernel, owners),
        out_shape=jax.ShapeDtypeStruct((3, 3, SIDE, SIDE), f32),
        in_specs=[smem] * 5 + [hbm] * 2,
        out_specs=pl.BlockSpec(memory_space=pltpu.VMEM),
        scratch_shapes=[
            pltpu.VMEM((4, 3, HALF, HALF), f32),
            pltpu.VMEM((4, SIDE, SIDE), jnp.int32),
            stage_buf,
            stage_buf,
            stage_buf,
            stage_buf,
            pltpu.VMEM((2, 2, SIDE, HALF), f32),
            pltpu.VMEM((2, 2, SIDE, HALF), f32),
            pltpu.VMEM((3, 3, 2, SIDE, HALF), f32),
            pltpu.VMEM((3, 3, 4, 8, SIDE), f32),
            pltpu.VMEM((3, 3, SIDE, HALF), f32),
            strip_buf,
            strip_buf,
            strip_buf,
            strip_buf,
            pltpu.VMEM((8, 8, SIDE), f32),
            pltpu.VMEM((8, 8, SIDE), f32),
            face_buf,
            face_buf,
            face_buf,
            face_buf,
            pltpu.SemaphoreType.DMA((4,)),
            pltpu.SemaphoreType.DMA,
            pltpu.SemaphoreType.DMA((4, 4)),
            pltpu.SemaphoreType.DMA((4, 4)),
            pltpu.SemaphoreType.DMA((3,)),
            pltpu.SemaphoreType.DMA((3,)),
        ],
        compiler_params=pltpu.CompilerParams(
            collective_id=0, has_side_effects=True, vmem_limit_bytes=40 * 1024 * 1024
        ),
        name="regrid_step",
    )(parents, new_counts, neighbours, class_diffusivity, class_growth, coarse, land_cover)


def solution(mesh):
    return jax.shard_map(
        body,
        mesh=mesh,
        in_specs=(
            P("owner", None, None, None),
            P("owner"),
            P(),
            P(),
            P("owner", None, None),
            P(),
            P(),
        ),
        out_specs=P("owner", None, None, None),
        check_vma=False,
    )
```

```python
import functools

import jax
import jax.numpy as jnp
from jax import lax
from jax.experimental import pallas as pl
from jax.experimental.pallas import tpu as pltpu
from jax.sharding import PartitionSpec as P

SIDE = 256
HALF = 128
CLASSES = 11
PAD = 8
WEIGHTS = (0.5, 0.5, 1.0, 1.0 / 6.0)
MESH = pl.DeviceIdType.MESH


def iota(shape, dim):
    return lax.broadcasted_iota(jnp.int32, shape, dim)


def phased(index):
    return 2 * (index & (HALF - 1)) + (index >> 7)


def prolong_weights(fine, coarse):
    near = fine >> 1
    second = jnp.clip(near + jnp.where((fine & 1) == 0, -1, 1), 0, HALF - 1)
    heavy = jnp.where(coarse == near, 0.75, 0.0)
    light = jnp.where(coarse == second, 0.25, 0.0)
    return (heavy + light).astype(jnp.bfloat16)


def split(block, axis):
    high = block.astype(jnp.bfloat16)
    low = (block - high.astype(jnp.float32)).astype(jnp.bfloat16)
    return jnp.concatenate([high, low], axis=axis)


def dot(a, b):
    return jnp.dot(a, b, preferred_element_type=jnp.float32)


def dot_t(a, b):
    return lax.dot_general(a, b, (((1,), (1,)), ((), ())), preferred_element_type=jnp.float32)


def look_up(classes, diff_ref, grow_ref):
    diffus = jnp.full(classes.shape, diff_ref[0], jnp.float32)
    growth = jnp.full(classes.shape, grow_ref[0], jnp.float32)
    for number in range(1, CLASSES):
        hit = classes == jnp.asarray(number, classes.dtype)
        diffus = jnp.where(hit, diff_ref[number], diffus)
        growth = jnp.where(hit, grow_ref[number], growth)
    return diffus, growth


def scaled_rates(weight, x0, x1, x2, lap0, lap1, lap2, diffus, growth):
    dw = diffus * weight
    gw = growth * weight
    xw = x0 * weight
    r0 = dw * lap0 + (gw * x0) * (x1 - x0 - x2)
    r1 = (0.5 * dw) * lap1 + (0.4 * weight - x1 * (0.4 * weight + xw))
    r2 = dw * lap2 + (xw - (0.3 * weight) * x2)
    return r0, r1, r2


def combine(x, s2, s3, s4, rate):
    return (s2 + 2.0 * s3 + s4 - x) * (1.0 / 3.0) + rate


def kernel(
    owners,
    parents_hbm,
    counts_hbm,
    nb_hbm,
    diff_hbm,
    grow_hbm,
    coarse_ref,
    land_ref,
    out_ref,
    parents_ref,
    counts_ref,
    nb_ref,
    diff_ref,
    grow_ref,
    quads,
    land,
    x_buf,
    s2_buf,
    s3_buf,
    s4_buf,
    diffus_buf,
    growth_buf,
    result,
    ring,
    across,
    t0,
    t1,
    t2,
    t3,
    strip_diffus,
    strip_growth,
    f0,
    f1,
    f2,
    f3,
    load_sem,
    small_sem,
    land_sem,
    face_send,
    face_recv,
    pair_send,
    pair_recv,
):
    me = lax.axis_index("owner")
    parity = me % 2
    partner = me + 1 - 2 * parity
    moving = 1 - parity
    up1, up2 = (me + 1) % owners, (me + 2) % owners
    dn1, dn2 = (me + owners - 1) % owners, (me + owners - 2) % owners
    stages = (x_buf, s2_buf, s3_buf, s4_buf)
    strips = (t0, t1, t2, t3)
    faces = (f0, f1, f2, f3)

    loads = []
    for q in range(4):
        block = coarse_ref.at[0, :, pl.ds((q // 2) * HALF, HALF), pl.ds((q % 2) * HALF, HALF)]
        loads.append(pltpu.make_async_copy(block, quads.at[q], load_sem.at[q]))
    for load in loads:
        load.start()
    small = []
    pairs = (
        (parents_hbm, parents_ref),
        (counts_hbm, counts_ref),
        (nb_hbm, nb_ref),
        (diff_hbm, diff_ref),
        (grow_hbm, grow_ref),
    )
    for n, (src, dst) in enumerate(pairs):
        small.append(pltpu.make_async_copy(src, dst, small_sem.at[n]))
        small[n].start()
    land_load = pltpu.make_async_copy(land_ref, land.at[pl.ds(0, 3)], land_sem)
    land_load.start()
    barrier = pltpu.get_barrier_semaphore()
    for other in (up1, dn1, up2, dn2):
        pl.semaphore_signal(barrier, inc=1, device_id=(other,), device_id_type=MESH)

    shape = (SIDE, SIDE)
    columns_up = prolong_weights(iota(shape, 1), iota(shape, 0) & (HALF - 1))
    phases_across = prolong_weights(phased(iota(shape, 1)), iota(shape, 0) & (HALF - 1))
    phases_along = prolong_weights(phased(iota(shape, 0)), iota(shape, 1) & (HALF - 1))
    weave = jnp.where(phased(iota(shape, 0)) == iota(shape, 1), 1.0, 0.0).astype(jnp.bfloat16)
    unweave = jnp.where(phased(iota(shape, 1)) == iota(shape, 0), 1.0, 0.0).astype(jnp.bfloat16)
    edge = iota((16, SIDE), 0)
    edge = jnp.where(edge < 8, edge, edge + (SIDE - 16))
    edge_up = prolong_weights(edge, iota((16, SIDE), 1) & (HALF - 1))
    edge_pick = jnp.where(iota((16, SIDE), 1) == edge, 1.0, 0.0).astype(jnp.bfloat16)
    for buf in stages:
        for i in range(2):
            for c in range(3):
                for y in range(2):
                    for x in range(2):
                        buf[i, c, y, x, 0:PAD] = jnp.zeros((PAD, HALF), jnp.float32)
                        buf[i, c, y, x, PAD + HALF :] = jnp.zeros((PAD, HALF), jnp.float32)

    def send_faces(s, start):
        f = faces[s]
        copies = [
            (f.at[pl.ds(3, 2)], f.at[pl.ds(1, 2)], up1),
            (f.at[pl.ds(3, 2)], f.at[pl.ds(5, 2)], dn1),
            (f.at[4], f.at[0], up2),
            (f.at[3], f.at[7], dn2),
        ]
        made = []
        for n, (src, dst, to) in enumerate(copies):
            made.append(
                pltpu.make_async_remote_copy(
                    src_ref=src,
                    dst_ref=dst,
                    send_sem=face_send.at[s, n],
                    recv_sem=face_recv.at[s, n],
                    device_id=(to,),
                    device_id_type=MESH,
                )
            )
        if start:
            for copy in made:
                copy.start()
        return made

    def put_faces(s, c, block):
        for i in range(2):
            for f in range(4):
                row = 7 * (f % 2)
                faces[s][3 + i, 4 * f + c : 4 * f + c + 1, :] = block[4 * i + f, row : row + 1, :]

    for load in loads + small:
        load.wait()
    parent = [parents_ref[i] % 4 for i in range(2)]
    edges = []
    for i in range(2):
        for c in range(3):
            block = quads[parent[i], c]
            edges.append(dot_t(edge_up, split(block, 1)))
            edges.append(dot(edge_up, split(block, 0)))
    edges = dot(split(jnp.concatenate(edges, axis=0), 1), columns_up).reshape(2, 3, 4, 8, SIDE)
    for c in range(3):
        block = jnp.concatenate([edges[0, c], edges[1, c]], axis=0)
        t0[c] = block
        put_faces(0, c, block)

    pl.semaphore_wait(barrier, 4)
    sent = send_faces(0, True)
    land_copy = pltpu.make_async_remote_copy(
        src_ref=land_ref.at[2 * (1 - parity)],
        dst_ref=land.at[3],
        send_sem=pair_send.at[0],
        recv_sem=pair_recv.at[0],
        device_id=(partner,),
        device_id_type=MESH,
    )
    land_copy.start()

    for i in range(2):
        for c in range(3):
            half_done = dot(split(quads[parent[i], c], 1), phases_across)
            fine = dot(phases_along, split(half_done, 0))
            for y in range(2):
                for x in range(2):
                    x_buf[i, c, y, x, PAD : PAD + HALF] = fine[
                        y * HALF : (y + 1) * HALF, x * HALF : (x + 1) * HALF
                    ]

    land_load.wait()
    land_copy.wait_recv()
    count = counts_ref[me]
    slots = []
    for i in range(2):
        even_slot = jnp.where(i >= count, 3, i)
        odd_slot = jnp.where(i - 2 + count < 0, 3, i - 2 + count)
        slots.append(jnp.where(parity == 0, even_slot, odd_slot))
    for i in range(2):
        classes = land[slots[i]].astype(jnp.float32).astype(jnp.bfloat16)
        picked = dot_t(edge_pick, classes)
        across_d, across_g = look_up(picked, diff_ref, grow_ref)
        ends = jnp.concatenate(
            [land[slots[i], 0:8, :], land[slots[i], SIDE - 8 : SIDE, :]], axis=0
        )
        along_d, along_g = look_up(ends, diff_ref, grow_ref)
        for n in range(2):
            rows = slice(8 * n, 8 * n + 8)
            strip_diffus[4 * i + n] = across_d[rows]
            strip_growth[4 * i + n] = across_g[rows]
            strip_diffus[4 * i + 2 + n] = along_d[rows]
            strip_growth[4 * i + 2 + n] = along_g[rows]

        classes = dot(classes, unweave).astype(jnp.bfloat16)
        for n in range(8):
            rows = slice(32 * n, 32 * n + 32)
            d, g = look_up(dot(weave[rows], classes), diff_ref, grow_ref)
            y, m = n // 4, 32 * (n % 4)
            for x in range(2):
                diffus_buf[i, y, x, m : m + 32] = d[:, x * HALF : (x + 1) * HALF]
                growth_buf[i, y, x, m : m + 32] = g[:, x * HALF : (x + 1) * HALF]

    peers = []
    for i in range(2):
        for f in range(4):
            value = nb_ref[f, 2 * me + i]
            peers.append((value >= 0, jnp.clip(value - (2 * me - 3), 0, 7)))

    strip = (8, 8, SIDE)
    sub = iota(strip, 1)
    lane = iota(strip, 2)
    sub_half = iota((8, 8, HALF), 1)
    lane_half = iota((8, 8, HALF), 2)

    def strip_laplacian(s, c):
        now = strips[s][c]
        f_ref = faces[s]
        ghosts = []
        for i in range(2):
            for f in range(4):
                has, where = peers[4 * i + f]
                theirs = 4 * (f ^ 1) + c
                ours = 4 * f + c
                row = jnp.where(
                    has, f_ref[where, theirs : theirs + 1, :], f_ref[3 + i, ours : ours + 1, :]
                )
                ghosts.append(jnp.broadcast_to(row, (8, SIDE)))
        ghost = jnp.stack(ghosts, axis=0)
        low = jnp.sum(
            jnp.where(lane_half == sub_half, ghost[:, :, :HALF], 0.0), axis=2, keepdims=True
        )
        high = jnp.sum(
            jnp.where(lane_half == sub_half + (HALF - 8), ghost[:, :, HALF:], 0.0),
            axis=2,
            keepdims=True,
        )
        ends = []
        for e in range(2):
            columns = []
            for i in range(2):
                for f in range(4):
                    source = (low, high)[f % 2]
                    face = 4 * i + (2 if f < 2 else 0) + e
                    columns.append(source[face])
            ends.append(jnp.stack(columns, axis=0))
        above = jnp.where(sub == 0, ghost, pltpu.roll(now, 1, 1))
        below = jnp.where(sub == 7, ghost, pltpu.roll(now, 7, 1))
        left = jnp.where(lane == 0, ends[0], pltpu.roll(now, 1, 2))
        right = jnp.where(lane == SIDE - 1, ends[1], pltpu.roll(now, SIDE - 1, 2))
        return now, (left + right) + (below + above) - 4.0 * now

    def strip_stage(s):
        values = [strip_laplacian(s, c) for c in range(3)]
        rates = scaled_rates(
            WEIGHTS[s],
            *[v[0] for v in values],
            *[v[1] for v in values],
            strip_diffus[...],
            strip_growth[...],
        )
        for c in range(3):
            if s < 3:
                block = t0[c] + rates[c]
                strips[s + 1][c] = block
                put_faces(s + 1, c, block)
            else:
                block = combine(t0[c], t1[c], t2[c], t3[c], rates[c])
                for i in range(2):
                    ring[i, c] = block[4 * i : 4 * i + 4]

    def bulk_stage(i, s):
        src = stages[s]
        dst = stages[(s + 1) % 4] if s < 3 else s2_buf

        def step_rows(step, carry):
            r = pl.multiple_of(step * 8, 8)
            at = PAD + r
            here = pl.ds(at, 8)
            now = [[src[i, c, n // 2, n % 2, here, :] for n in range(4)] for c in range(3)]
            lap = [[None] * 4 for _ in range(3)]
            for c in range(3):
                for n in range(4):
                    y, x = n // 2, n % 2
                    beside = now[c][2 * y + 1 - x]
                    beyond = pltpu.roll(beside, HALF - 1 if x else 1, 1)
                    upright = now[c][2 * (1 - y) + x]
                    further = src[i, c, 1 - y, x, pl.ds(at + 2 * y - 1, 8), :]
                    lap[c][n] = (beside + beyond) + (upright + further) - 4.0 * now[c][n]
            for n in range(4):
                y, x = n // 2, n % 2
                rates = scaled_rates(
                    WEIGHTS[s],
                    *[now[c][n] for c in range(3)],
                    *[lap[c][n] for c in range(3)],
                    diffus_buf[i, y, x, pl.ds(r, 8), :],
                    growth_buf[i, y, x, pl.ds(r, 8), :],
                )
                for c in range(3):
                    base = now[c][n] if s == 0 else x_buf[i, c, y, x, here, :]
                    if s < 3:
                        value = base + rates[c]
                    else:
                        value = combine(
                            base,
                            s2_buf[i, c, y, x, here, :],
                            s3_buf[i, c, y, x, here, :],
                            now[c][n],
                            rates[c],
                        )
                    dst[i, c, y, x, here, :] = value
            return carry

        lax.fori_loop(0, HALF // 8, step_rows, 0, unroll=4)

    def bulk_weave(i):
        for c in range(3):
            for y in range(2):
                both = jnp.concatenate(
                    [s2_buf[i, c, y, x, PAD : PAD + HALF, :] for x in range(2)], axis=1
                )
                high = both.astype(jnp.bfloat16)
                low = (both - high.astype(jnp.float32)).astype(jnp.bfloat16)
                woven = dot(high, weave) + dot(low, weave)
                for j in range(2):
                    result[i, c, j, pl.ds(y, HALF, stride=2), :] = woven[:, j * HALF : (j + 1) * HALF]

    result_copy = pltpu.make_async_remote_copy(
        src_ref=result.at[moving],
        dst_ref=result.at[2],
        send_sem=pair_send.at[1],
        recv_sem=pair_recv.at[1],
        device_id=(partner,),
        device_id_type=MESH,
    )
    ring_copy = pltpu.make_async_remote_copy(
        src_ref=ring.at[moving],
        dst_ref=ring.at[2],
        send_sem=pair_send.at[2],
        recv_sem=pair_recv.at[2],
        device_id=(partner,),
        device_id_type=MESH,
    )
    gaps = (
        ((moving, 0), (moving, 1), (moving, 2)),
        ((moving, 3), (moving, 4), (parity, 0)),
        ((parity, 1), (parity, 2), (parity, 3), (parity, 4)),
    )
    for s in range(4):
        for copy in sent[4 * s : 4 * s + 4]:
            copy.wait_recv()
        strip_stage(s)
        if s < 3:
            sent = sent + send_faces(s + 1, True)
            for i, stage in gaps[s]:
                if stage < 4:
                    bulk_stage(i, stage)
                else:
                    bulk_weave(i)
                if s == 1 and stage == 4:
                    result_copy.start()
    ring_copy.start()

    def turn(e):
        for c in range(3):
            block = jnp.concatenate(
                [ring[e, c, 0], jnp.zeros((HALF - 16, SIDE), jnp.float32), ring[e, c, 1]], axis=0
            )
            across[e, c, 0:HALF] = block[:, :HALF].T
            across[e, c, HALF:SIDE] = block[:, HALF:].T

    turn(0)
    turn(1)
    result_copy.wait_recv()
    ring_copy.wait_recv()
    turn(2)

    low_lanes = iota((8, HALF), 1) < 4
    high_lanes = iota((8, HALF), 1) >= HALF - 4
    sub_rows = iota((8, SIDE), 0)
    sources = []
    for s in range(3):
        from_even = s
        from_odd = (5 - count + s) % 3
        sources.append((jnp.where(parity == 0, from_even, from_odd), s < count))

    def place(step, carry):
        r = pl.multiple_of(step * 8, 8)
        for s in range(3):
            e, held = sources[s]
            for c in range(3):
                side = across[e, c, pl.ds(r, 8), :]
                left = jnp.where(low_lanes, side, result[e, c, 0, pl.ds(r, 8), :])
                right = jnp.where(high_lanes, side, result[e, c, 1, pl.ds(r, 8), :])
                out_ref[s, c, pl.ds(r, 8), 0:HALF] = jnp.where(held, left, 0.0)
                out_ref[s, c, pl.ds(r, 8), HALF:SIDE] = jnp.where(held, right, 0.0)
        return carry

    lax.fori_loop(0, SIDE // 8, place, 0)
    for s in range(3):
        e, held = sources[s]
        for c in range(3):
            for n, rows in ((0, slice(0, 8)), (1, slice(SIDE - 8, SIDE))):
                inside = sub_rows < 4 if n == 0 else sub_rows >= 4
                merged = jnp.where(inside, ring[e, c, 2 + n], out_ref[s, c, rows, :])
                out_ref[s, c, rows, :] = jnp.where(held, merged, 0.0)

    for copy in sent:
        copy.wait_send()
    land_copy.wait_send()
    result_copy.wait_send()
    ring_copy.wait_send()


def body(coarse, parents, new_counts, neighbours, land_cover, class_diffusivity, class_growth):
    owners = lax.axis_size("owner")
    f32 = jnp.float32
    hbm = pl.BlockSpec(memory_space=pltpu.HBM)
    stage_buf = pltpu.VMEM((2, 3, 2, 2, HALF + 2 * PAD, HALF), f32)
    strip_buf = pltpu.VMEM((3, 8, 8, SIDE), f32)
    face_buf = pltpu.VMEM((8, 16, SIDE), f32)
    return pl.pallas_call(
        functools.partial(kernel, owners),
        out_shape=jax.ShapeDtypeStruct((3, 3, SIDE, SIDE), f32),
        in_specs=[hbm] * 7,
        out_specs=pl.BlockSpec(memory_space=pltpu.VMEM),
        scratch_shapes=[
            pltpu.SMEM((2,), jnp.int32),
            pltpu.SMEM((owners,), jnp.int32),
            pltpu.SMEM((4, 2 * owners), jnp.int32),
            pltpu.SMEM((CLASSES,), f32),
            pltpu.SMEM((CLASSES,), f32),
            pltpu.VMEM((4, 3, HALF, HALF), f32),
            pltpu.VMEM((4, SIDE, SIDE), jnp.int32),
            stage_buf,
            stage_buf,
            stage_buf,
            stage_buf,
            pltpu.VMEM((2, 2, 2, HALF, HALF), f32),
            pltpu.VMEM((2, 2, 2, HALF, HALF), f32),
            pltpu.VMEM((3, 3, 2, SIDE, HALF), f32),
            pltpu.VMEM((3, 3, 4, 8, SIDE), f32),
            pltpu.VMEM((3, 3, SIDE, HALF), f32),
            strip_buf,
            strip_buf,
            strip_buf,
            strip_buf,
            pltpu.VMEM((8, 8, SIDE), f32),
            pltpu.VMEM((8, 8, SIDE), f32),
            face_buf,
            face_buf,
            face_buf,
            face_buf,
            pltpu.SemaphoreType.DMA((4,)),
            pltpu.SemaphoreType.DMA((5,)),
            pltpu.SemaphoreType.DMA,
            pltpu.SemaphoreType.DMA((4, 4)),
            pltpu.SemaphoreType.DMA((4, 4)),
            pltpu.SemaphoreType.DMA((3,)),
            pltpu.SemaphoreType.DMA((3,)),
        ],
        compiler_params=pltpu.CompilerParams(
            collective_id=0, has_side_effects=True, vmem_limit_bytes=62 * 1024 * 1024
        ),
        name="regrid_step",
    )(parents, new_counts, neighbours.T, class_diffusivity, class_growth, coarse, land_cover)


def solution(mesh):
    return jax.shard_map(
        body,
        mesh=mesh,
        in_specs=(
            P("owner", None, None, None),
            P("owner"),
            P(),
            P(),
            P("owner", None, None),
            P(),
            P(),
        ),
        out_specs=P("owner", None, None, None),
        check_vma=False,
    )
```

```python
import functools

import jax
import jax.numpy as jnp
from jax import lax
from jax.experimental import pallas as pl
from jax.experimental.pallas import tpu as pltpu
from jax.sharding import PartitionSpec as P

SIDE = 256
HALF = 128
CLASSES = 11
PAD = 8
WEIGHTS = (0.5, 0.5, 1.0, 1.0 / 6.0)
MESH = pl.DeviceIdType.MESH


def iota(shape, dim):
    return lax.broadcasted_iota(jnp.int32, shape, dim)


def phased(index):
    return 2 * (index & (HALF - 1)) + (index >> 7)


def prolong_weights(fine, coarse):
    near = fine >> 1
    second = jnp.clip(near + jnp.where((fine & 1) == 0, -1, 1), 0, HALF - 1)
    heavy = jnp.where(coarse == near, 0.75, 0.0)
    light = jnp.where(coarse == second, 0.25, 0.0)
    return (heavy + light).astype(jnp.bfloat16)


def split(block, axis):
    high = block.astype(jnp.bfloat16)
    low = (block - high.astype(jnp.float32)).astype(jnp.bfloat16)
    return jnp.concatenate([high, low], axis=axis)


def dot(a, b):
    return jnp.dot(a, b, preferred_element_type=jnp.float32)


def dot_t(a, b):
    return lax.dot_general(a, b, (((1,), (1,)), ((), ())), preferred_element_type=jnp.float32)


def look_up(classes, diff_ref, grow_ref):
    diffus = jnp.full(classes.shape, diff_ref[0], jnp.float32)
    growth = jnp.full(classes.shape, grow_ref[0], jnp.float32)
    for number in range(1, CLASSES):
        hit = classes == jnp.asarray(number, classes.dtype)
        diffus = jnp.where(hit, diff_ref[number], diffus)
        growth = jnp.where(hit, grow_ref[number], growth)
    return diffus, growth


def scaled_rates(weight, x0, x1, x2, lap0, lap1, lap2, diffus, growth):
    dw = diffus * weight
    gw = growth * weight
    xw = x0 * weight
    r0 = dw * lap0 + (gw * x0) * (x1 - x0 - x2)
    r1 = (0.5 * dw) * lap1 + (0.4 * weight - x1 * (0.4 * weight + xw))
    r2 = dw * lap2 + (xw - (0.3 * weight) * x2)
    return r0, r1, r2


def combine(x, s2, s3, s4, rate):
    return (s2 + 2.0 * s3 + s4 - x) * (1.0 / 3.0) + rate


def kernel(
    owners,
    parents_hbm,
    counts_hbm,
    nb_hbm,
    diff_hbm,
    grow_hbm,
    coarse_ref,
    land_ref,
    result_out,
    ring_out,
    parents_ref,
    counts_ref,
    nb_ref,
    diff_ref,
    grow_ref,
    quads,
    land,
    x_buf,
    s2_buf,
    s3_buf,
    s4_buf,
    diffus_buf,
    growth_buf,
    result,
    ring,
    t0,
    t1,
    t2,
    t3,
    strip_diffus,
    strip_growth,
    f0,
    f1,
    f2,
    f3,
    load_sem,
    small_sem,
    land_sem,
    face_send,
    face_recv,
    pair_send,
    pair_recv,
    own_sem,
):
    me = lax.axis_index("owner")
    parity = me % 2
    partner = me + 1 - 2 * parity
    moving = 1 - parity
    reach = [(me + by) % owners for by in (1, -1, 2, -2)]
    exists = [me + 1 < owners, me >= 1, me + 2 < owners, me >= 2]
    stages = (x_buf, s2_buf, s3_buf, s4_buf)
    strips = (t0, t1, t2, t3)
    faces = (f0, f1, f2, f3)

    loads = []
    for q in range(4):
        block = coarse_ref.at[0, :, pl.ds((q // 2) * HALF, HALF), pl.ds((q % 2) * HALF, HALF)]
        loads.append(pltpu.make_async_copy(block, quads.at[q], load_sem.at[q]))
    for load in loads:
        load.start()
    small = []
    pairs = (
        (parents_hbm, parents_ref),
        (counts_hbm, counts_ref),
        (nb_hbm, nb_ref),
        (diff_hbm, diff_ref),
        (grow_hbm, grow_ref),
    )
    for n, (src, dst) in enumerate(pairs):
        small.append(pltpu.make_async_copy(src, dst, small_sem.at[n]))
        small[n].start()
    land_load = pltpu.make_async_copy(land_ref, land.at[pl.ds(0, 3)], land_sem)
    land_load.start()
    barrier = pltpu.get_barrier_semaphore()
    for n in range(4):

        @pl.when(exists[n])
        def _(n=n):
            pl.semaphore_signal(barrier, inc=1, device_id=(reach[n],), device_id_type=MESH)


    shape = (SIDE, SIDE)
    columns_up = prolong_weights(iota(shape, 1), iota(shape, 0) & (HALF - 1))
    phases_across = prolong_weights(phased(iota(shape, 1)), iota(shape, 0) & (HALF - 1))
    phases_along = prolong_weights(phased(iota(shape, 0)), iota(shape, 1) & (HALF - 1))
    weave = jnp.where(phased(iota(shape, 0)) == iota(shape, 1), 1.0, 0.0).astype(jnp.bfloat16)
    unweave = jnp.where(phased(iota(shape, 1)) == iota(shape, 0), 1.0, 0.0).astype(jnp.bfloat16)
    edge = iota((16, SIDE), 0)
    edge = jnp.where(edge < 8, edge, edge + (SIDE - 16))
    edge_up = prolong_weights(edge, iota((16, SIDE), 1) & (HALF - 1))
    edge_pick = jnp.where(iota((16, SIDE), 1) == edge, 1.0, 0.0).astype(jnp.bfloat16)
    for buf in stages:
        for i in range(2):
            for c in range(3):
                for y in range(2):
                    for x in range(2):
                        buf[i, c, y, x, 0:PAD] = jnp.zeros((PAD, HALF), jnp.float32)
                        buf[i, c, y, x, PAD + HALF :] = jnp.zeros((PAD, HALF), jnp.float32)

    def face_copies(s):
        f = faces[s]
        ends = [
            (f.at[pl.ds(3, 2)], f.at[pl.ds(1, 2)]),
            (f.at[pl.ds(3, 2)], f.at[pl.ds(5, 2)]),
            (f.at[4], f.at[0]),
            (f.at[3], f.at[7]),
        ]
        made = []
        for n, (src, dst) in enumerate(ends):
            made.append(
                pltpu.make_async_remote_copy(
                    src_ref=src,
                    dst_ref=dst,
                    send_sem=face_send.at[s, n],
                    recv_sem=face_recv.at[s, n],
                    device_id=(reach[n],),
                    device_id_type=MESH,
                )
            )
        return made

    def send_faces(s):
        for n, copy in enumerate(face_copies(s)):
            pl.when(exists[n])(copy.start)

    def await_faces(s):
        for n, copy in enumerate(face_copies(s)):
            pl.when(exists[n ^ 1])(copy.wait_recv)

    def put_faces(s, c, block):
        for i in range(2):
            for f in range(4):
                row = 7 * (f % 2)
                faces[s][3 + i, 4 * f + c : 4 * f + c + 1, :] = block[4 * i + f, row : row + 1, :]

    for load in loads + small:
        load.wait()
    parent = [parents_ref[i] % 4 for i in range(2)]
    edges = []
    for i in range(2):
        for c in range(3):
            block = quads[parent[i], c]
            edges.append(dot_t(edge_up, split(block, 1)))
            edges.append(dot(edge_up, split(block, 0)))
    edges = dot(split(jnp.concatenate(edges, axis=0), 1), columns_up).reshape(2, 3, 4, 8, SIDE)
    for c in range(3):
        block = jnp.concatenate([edges[0, c], edges[1, c]], axis=0)
        t0[c] = block
        put_faces(0, c, block)

    pl.semaphore_wait(barrier, sum(jnp.where(there, 1, 0) for there in exists))
    send_faces(0)
    land_copy = pltpu.make_async_remote_copy(
        src_ref=land_ref.at[2 * (1 - parity)],
        dst_ref=land.at[3],
        send_sem=pair_send.at[0],
        recv_sem=pair_recv.at[0],
        device_id=(partner,),
        device_id_type=MESH,
    )
    land_copy.start()

    for i in range(2):
        for c in range(3):
            half_done = dot(split(quads[parent[i], c], 1), phases_across)
            fine = dot(phases_along, split(half_done, 0))
            for y in range(2):
                for x in range(2):
                    x_buf[i, c, y, x, PAD : PAD + HALF] = fine[
                        y * HALF : (y + 1) * HALF, x * HALF : (x + 1) * HALF
                    ]

    land_load.wait()
    land_copy.wait_recv()
    count = counts_ref[me]
    slots = []
    for i in range(2):
        even_slot = jnp.where(i >= count, 3, i)
        odd_slot = jnp.where(i - 2 + count < 0, 3, i - 2 + count)
        slots.append(jnp.where(parity == 0, even_slot, odd_slot))
    for i in range(2):
        classes = land[slots[i]].astype(jnp.float32).astype(jnp.bfloat16)
        picked = dot_t(edge_pick, classes)
        across_d, across_g = look_up(picked, diff_ref, grow_ref)
        ends = jnp.concatenate(
            [land[slots[i], 0:8, :], land[slots[i], SIDE - 8 : SIDE, :]], axis=0
        )
        along_d, along_g = look_up(ends, diff_ref, grow_ref)
        for n in range(2):
            rows = slice(8 * n, 8 * n + 8)
            strip_diffus[4 * i + n] = across_d[rows]
            strip_growth[4 * i + n] = across_g[rows]
            strip_diffus[4 * i + 2 + n] = along_d[rows]
            strip_growth[4 * i + 2 + n] = along_g[rows]

        classes = dot(classes, unweave).astype(jnp.bfloat16)
        for n in range(8):
            rows = slice(32 * n, 32 * n + 32)
            d, g = look_up(dot(weave[rows], classes), diff_ref, grow_ref)
            y, m = n // 4, 32 * (n % 4)
            for x in range(2):
                diffus_buf[i, y, x, m : m + 32] = d[:, x * HALF : (x + 1) * HALF]
                growth_buf[i, y, x, m : m + 32] = g[:, x * HALF : (x + 1) * HALF]

    peers = []
    for i in range(2):
        for f in range(4):
            value = nb_ref[f, 2 * me + i]
            peers.append((value >= 0, jnp.clip(value - (2 * me - 3), 0, 7)))

    strip = (8, 8, SIDE)
    sub = iota(strip, 1)
    lane = iota(strip, 2)
    sub_half = iota((8, 8, HALF), 1)
    lane_half = iota((8, 8, HALF), 2)

    def strip_laplacian(s, c):
        now = strips[s][c]
        f_ref = faces[s]
        ghosts = []
        for i in range(2):
            for f in range(4):
                has, where = peers[4 * i + f]
                theirs = 4 * (f ^ 1) + c
                ours = 4 * f + c
                row = jnp.where(
                    has, f_ref[where, theirs : theirs + 1, :], f_ref[3 + i, ours : ours + 1, :]
                )
                ghosts.append(jnp.broadcast_to(row, (8, SIDE)))
        ghost = jnp.stack(ghosts, axis=0)
        low = jnp.sum(
            jnp.where(lane_half == sub_half, ghost[:, :, :HALF], 0.0), axis=2, keepdims=True
        )
        high = jnp.sum(
            jnp.where(lane_half == sub_half + (HALF - 8), ghost[:, :, HALF:], 0.0),
            axis=2,
            keepdims=True,
        )
        ends = []
        for e in range(2):
            columns = []
            for i in range(2):
                for f in range(4):
                    source = (low, high)[f % 2]
                    face = 4 * i + (2 if f < 2 else 0) + e
                    columns.append(source[face])
            ends.append(jnp.stack(columns, axis=0))
        above = jnp.where(sub == 0, ghost, pltpu.roll(now, 1, 1))
        below = jnp.where(sub == 7, ghost, pltpu.roll(now, 7, 1))
        left = jnp.where(lane == 0, ends[0], pltpu.roll(now, 1, 2))
        right = jnp.where(lane == SIDE - 1, ends[1], pltpu.roll(now, SIDE - 1, 2))
        return now, (left + right) + (below + above) - 4.0 * now

    def strip_stage(s):
        values = [strip_laplacian(s, c) for c in range(3)]
        rates = scaled_rates(
            WEIGHTS[s],
            *[v[0] for v in values],
            *[v[1] for v in values],
            strip_diffus[...],
            strip_growth[...],
        )
        for c in range(3):
            if s < 3:
                block = t0[c] + rates[c]
                strips[s + 1][c] = block
                put_faces(s + 1, c, block)
            else:
                block = combine(t0[c], t1[c], t2[c], t3[c], rates[c])
                for i in range(2):
                    ring[i, c] = block[4 * i : 4 * i + 4]

    def bulk_stage(i, s):
        src = stages[s]
        dst = stages[(s + 1) % 4] if s < 3 else s2_buf

        def step_rows(step, carry):
            r = pl.multiple_of(step * 8, 8)
            at = PAD + r
            here = pl.ds(at, 8)
            now = [[src[i, c, n // 2, n % 2, here, :] for n in range(4)] for c in range(3)]
            lap = [[None] * 4 for _ in range(3)]
            for c in range(3):
                for n in range(4):
                    y, x = n // 2, n % 2
                    beside = now[c][2 * y + 1 - x]
                    beyond = pltpu.roll(beside, HALF - 1 if x else 1, 1)
                    upright = now[c][2 * (1 - y) + x]
                    further = src[i, c, 1 - y, x, pl.ds(at + 2 * y - 1, 8), :]
                    lap[c][n] = (beside + beyond) + (upright + further) - 4.0 * now[c][n]
            for n in range(4):
                y, x = n // 2, n % 2
                rates = scaled_rates(
                    WEIGHTS[s],
                    *[now[c][n] for c in range(3)],
                    *[lap[c][n] for c in range(3)],
                    diffus_buf[i, y, x, pl.ds(r, 8), :],
                    growth_buf[i, y, x, pl.ds(r, 8), :],
                )
                for c in range(3):
                    base = now[c][n] if s == 0 else x_buf[i, c, y, x, here, :]
                    if s < 3:
                        value = base + rates[c]
                    else:
                        value = combine(
                            base,
                            s2_buf[i, c, y, x, here, :],
                            s3_buf[i, c, y, x, here, :],
                            now[c][n],
                            rates[c],
                        )
                    dst[i, c, y, x, here, :] = value
            return carry

        lax.fori_loop(0, HALF // 8, step_rows, 0, unroll=4)

    def bulk_weave(i):
        for c in range(3):
            for y in range(2):
                both = jnp.concatenate(
                    [s2_buf[i, c, y, x, PAD : PAD + HALF, :] for x in range(2)], axis=1
                )
                high = both.astype(jnp.bfloat16)
                low = (both - high.astype(jnp.float32)).astype(jnp.bfloat16)
                woven = dot(high, weave) + dot(low, weave)
                for j in range(2):
                    result[i, c, j, pl.ds(y, HALF, stride=2), :] = woven[:, j * HALF : (j + 1) * HALF]

    def to_partner(n, src, dst):
        return pltpu.make_async_remote_copy(
            src_ref=src.at[moving],
            dst_ref=dst.at[2],
            send_sem=pair_send.at[n],
            recv_sem=pair_recv.at[n],
            device_id=(partner,),
            device_id_type=MESH,
        )

    result_copy = to_partner(1, result, result_out)
    ring_copy = to_partner(2, ring, ring_out)
    own_copies = []
    for i in range(2):
        own_copies.append(pltpu.make_async_copy(result.at[i], result_out.at[i], own_sem.at[i]))
    own_copies.append(pltpu.make_async_copy(ring, ring_out.at[pl.ds(0, 2)], own_sem.at[2]))
    gaps = (
        ((moving, 0), (moving, 1), (moving, 2)),
        ((moving, 3), (moving, 4), (parity, 0)),
        ((parity, 1), (parity, 2), (parity, 3), (parity, 4)),
    )
    for s in range(4):
        await_faces(s)
        strip_stage(s)
        if s < 3:
            send_faces(s + 1)
            for i, stage in gaps[s]:
                if stage < 4:
                    bulk_stage(i, stage)
                else:
                    bulk_weave(i)
                if s == 1 and stage == 4:
                    result_copy.start()
    ring_copy.start()
    for copy in own_copies:
        copy.start()
    for s in range(4):
        for n, copy in enumerate(face_copies(s)):
            pl.when(exists[n])(copy.wait_send)
    land_copy.wait_send()
    for copy in own_copies:
        copy.wait()
    result_copy.wait()
    ring_copy.wait()


def merge_kernel(
    counts_hbm,
    result_hbm,
    ring_hbm,
    out_hbm,
    counts_ref,
    result,
    ring,
    zeros,
    count_sem,
    ring_sem,
    result_sem,
    out_sem,
    zero_sem,
):
    me = lax.axis_index("owner")
    even = me % 2 == 0
    count_copy = pltpu.make_async_copy(counts_hbm, counts_ref, count_sem)
    ring_copy = pltpu.make_async_copy(ring_hbm, ring, ring_sem)
    count_copy.start()
    ring_copy.start()

    def load(e, c):
        return pltpu.make_async_copy(result_hbm.at[e, c], result.at[e, c], result_sem.at[e, c])

    for e in range(3):
        for c in range(3):
            load(e, c).start()
    zeros[...] = jnp.zeros_like(zeros)
    count_copy.wait()
    count = counts_ref[me]
    empties = []
    for s in (1, 2):
        empties.append(pltpu.make_async_copy(zeros, out_hbm.at[s], zero_sem.at[s - 1]))
        pl.when(s >= count)(empties[-1].start)

    slots = []
    for e in range(3):
        slot = jnp.where(even, e, (e + 1) % 3 + count - 3)
        slots.append((slot, (slot >= 0) & (slot < count)))
    low_lanes = iota((8, HALF), 1) < 4
    high_lanes = iota((8, HALF), 1) >= HALF - 4
    sub_rows = iota((8, HALF), 0)
    ring_copy.wait()

    def stores(e, c):
        made = []
        for j in range(2):
            made.append(
                pltpu.make_async_copy(
                    result.at[e, c, j],
                    out_hbm.at[jnp.maximum(slots[e][0], 0), c, :, pl.ds(j * HALF, HALF)],
                    out_sem.at[e, c, j],
                )
            )
        return made

    for e in range(3):
        for c in range(3):
            gap = jnp.zeros((HALF - 16, SIDE), jnp.float32)
            block = jnp.concatenate([ring[e, c, 0], gap, ring[e, c, 1]], axis=0)
            sides = (block[:, :HALF].T, block[:, HALF:].T)
            load(e, c).wait()
            for j in range(2):
                lanes = high_lanes if j else low_lanes
                for t in range(SIDE // 8):
                    rows = slice(8 * t, 8 * t + 8)
                    within = slice(8 * t % HALF, 8 * t % HALF + 8)
                    value = jnp.where(lanes, sides[t // 16][within], result[e, c, j, rows, :])
                    if t == 0:
                        value = jnp.where(
                            sub_rows < 4, ring[e, c, 2, :, j * HALF : (j + 1) * HALF], value
                        )
                    if t == SIDE // 8 - 1:
                        value = jnp.where(
                            sub_rows >= 4, ring[e, c, 3, :, j * HALF : (j + 1) * HALF], value
                        )
                    result[e, c, j, rows, :] = value

            @pl.when(slots[e][1])
            def _(e=e, c=c):
                for copy in stores(e, c):
                    copy.start()

    for e in range(3):

        @pl.when(slots[e][1])
        def _(e=e):
            for c in range(3):
                for copy in stores(e, c):
                    copy.wait()

    for s in (1, 2):
        pl.when(s >= count)(empties[s - 1].wait)


def body(coarse, parents, new_counts, neighbours, land_cover, class_diffusivity, class_growth):
    owners = lax.axis_size("owner")
    f32 = jnp.float32
    hbm = pl.BlockSpec(memory_space=pltpu.HBM)
    stage_buf = pltpu.VMEM((2, 3, 2, 2, HALF + 2 * PAD, HALF), f32)
    strip_buf = pltpu.VMEM((3, 8, 8, SIDE), f32)
    face_buf = pltpu.VMEM((8, 16, SIDE), f32)
    results = jax.ShapeDtypeStruct((3, 3, 2, SIDE, HALF), f32)
    rings = jax.ShapeDtypeStruct((3, 3, 4, 8, SIDE), f32)
    whole, outer = pl.pallas_call(
        functools.partial(kernel, owners),
        out_shape=(results, rings),
        in_specs=[hbm] * 7,
        out_specs=(hbm, hbm),
        scratch_shapes=[
            pltpu.SMEM((2,), jnp.int32),
            pltpu.SMEM((owners,), jnp.int32),
            pltpu.SMEM((4, 2 * owners), jnp.int32),
            pltpu.SMEM((CLASSES,), f32),
            pltpu.SMEM((CLASSES,), f32),
            pltpu.VMEM((4, 3, HALF, HALF), f32),
            pltpu.VMEM((4, SIDE, SIDE), jnp.int32),
            stage_buf,
            stage_buf,
            stage_buf,
            stage_buf,
            pltpu.VMEM((2, 2, 2, HALF, HALF), f32),
            pltpu.VMEM((2, 2, 2, HALF, HALF), f32),
            pltpu.VMEM((2, 3, 2, SIDE, HALF), f32),
            pltpu.VMEM((2, 3, 4, 8, SIDE), f32),
            strip_buf,
            strip_buf,
            strip_buf,
            strip_buf,
            pltpu.VMEM((8, 8, SIDE), f32),
            pltpu.VMEM((8, 8, SIDE), f32),
            face_buf,
            face_buf,
            face_buf,
            face_buf,
            pltpu.SemaphoreType.DMA((4,)),
            pltpu.SemaphoreType.DMA((5,)),
            pltpu.SemaphoreType.DMA,
            pltpu.SemaphoreType.DMA((4, 4)),
            pltpu.SemaphoreType.DMA((4, 4)),
            pltpu.SemaphoreType.DMA((3,)),
            pltpu.SemaphoreType.DMA((3,)),
            pltpu.SemaphoreType.DMA((3,)),
        ],
        compiler_params=pltpu.CompilerParams(
            collective_id=0, has_side_effects=True, vmem_limit_bytes=62 * 1024 * 1024
        ),
        name="regrid_step",
    )(parents, new_counts, neighbours.T, class_diffusivity, class_growth, coarse, land_cover)
    return pl.pallas_call(
        merge_kernel,
        out_shape=jax.ShapeDtypeStruct((3, 3, SIDE, SIDE), f32),
        in_specs=[hbm] * 3,
        out_specs=hbm,
        scratch_shapes=[
            pltpu.SMEM((owners,), jnp.int32),
            pltpu.VMEM(results.shape, f32),
            pltpu.VMEM(rings.shape, f32),
            pltpu.VMEM((3, SIDE, SIDE), f32),
            pltpu.SemaphoreType.DMA,
            pltpu.SemaphoreType.DMA,
            pltpu.SemaphoreType.DMA((3, 3)),
            pltpu.SemaphoreType.DMA((3, 3, 2)),
            pltpu.SemaphoreType.DMA((2,)),
        ],
        compiler_params=pltpu.CompilerParams(vmem_limit_bytes=62 * 1024 * 1024),
        name="merge_slots",
    )(new_counts, whole, outer)


def solution(mesh):
    return jax.shard_map(
        body,
        mesh=mesh,
        in_specs=(
            P("owner", None, None, None),
            P("owner"),
            P(),
            P(),
            P("owner", None, None),
            P(),
            P(),
        ),
        out_specs=P("owner", None, None, None),
        check_vma=False,
    )
```

```python
import functools

import jax
import jax.numpy as jnp
from jax import lax
from jax.experimental import pallas as pl
from jax.experimental.pallas import tpu as pltpu
from jax.sharding import PartitionSpec as P

SIDE = 256
HALF = 128
CLASSES = 11
PAD = 8
REACH = 6
WEIGHTS = (0.5, 0.5, 1.0, 1.0 / 6.0)
MESH = pl.DeviceIdType.MESH


def iota(shape, dim):
    return lax.broadcasted_iota(jnp.int32, shape, dim)


def phased(index):
    return 2 * (index & (HALF - 1)) + (index >> 7)


def prolong_weights(fine, coarse):
    near = fine >> 1
    second = jnp.clip(near + jnp.where((fine & 1) == 0, -1, 1), 0, HALF - 1)
    heavy = jnp.where(coarse == near, 0.75, 0.0)
    light = jnp.where(coarse == second, 0.25, 0.0)
    return (heavy + light).astype(jnp.bfloat16)


def split(block, axis):
    high = block.astype(jnp.bfloat16)
    low = (block - high.astype(jnp.float32)).astype(jnp.bfloat16)
    return jnp.concatenate([high, low], axis=axis)


def dot(a, b):
    return jnp.dot(a, b, preferred_element_type=jnp.float32)


def dot_t(a, b):
    return lax.dot_general(a, b, (((1,), (1,)), ((), ())), preferred_element_type=jnp.float32)


def table_of(ref):
    lane = iota((8, HALF), 1)
    table = jnp.zeros((8, HALF), jnp.float32)
    for number in range(CLASSES):
        table = jnp.where(lane == number, ref[number], table)
    return table


def pick_lanes(table, index):
    return jnp.take_along_axis(table, index, axis=1)


def look_up(classes, tables):
    index = classes.astype(jnp.int32)
    rows, columns = classes.shape
    found = []
    for table in tables:
        bands = []
        for r in range(0, rows, 8):
            blocks = [
                pick_lanes(table, index[r : r + 8, k : k + HALF]) for k in range(0, columns, HALF)
            ]
            bands.append(jnp.concatenate(blocks, axis=1))
        found.append(jnp.concatenate(bands, axis=0))
    return found


def scaled_rates(weight, x0, x1, x2, lap0, lap1, lap2, diffus, growth):
    dw = diffus * weight
    gw = growth * weight
    xw = x0 * weight
    r0 = dw * lap0 + (gw * x0) * (x1 - x0 - x2)
    r1 = (0.5 * dw) * lap1 + (0.4 * weight - x1 * (0.4 * weight + xw))
    r2 = dw * lap2 + (xw - (0.3 * weight) * x2)
    return r0, r1, r2


def combine(x, s2, s3, s4, rate):
    return (s2 + 2.0 * s3 + s4 - x) * (1.0 / 3.0) + rate


def kernel(
    owners,
    parents_hbm,
    counts_hbm,
    nb_hbm,
    diff_hbm,
    grow_hbm,
    coarse_ref,
    land_ref,
    result_out,
    ring_out,
    parents_ref,
    counts_ref,
    nb_ref,
    diff_ref,
    grow_ref,
    quads,
    land,
    x_buf,
    s2_buf,
    s3_buf,
    s4_buf,
    diffus_buf,
    growth_buf,
    result,
    ring,
    t0,
    t1,
    t2,
    t3,
    strip_diffus,
    strip_growth,
    face_data,
    corner_data,
    h0,
    h1,
    h2,
    h3,
    outer_diffus,
    outer_growth,
    l0,
    l1,
    far_diffus,
    far_growth,
    k0,
    load_sem,
    small_sem,
    land_sem,
    face_send,
    face_recv,
    corner_send,
    corner_recv,
    pair_send,
    pair_recv,
    own_sem,
):
    me = lax.axis_index("owner")
    parity = me % 2
    partner = me + 1 - 2 * parity
    moving = 1 - parity
    steps = [by for far in range(1, REACH + 1) for by in (far, -far)]
    reach = [(me + by) % owners for by in steps]
    exists = [(me + by < owners) & (me + by >= 0) for by in steps]
    stages = (x_buf, s2_buf, s3_buf, s4_buf)
    strips = (t0, t1, t2, t3)
    outer = (h0, h1, h2, h3)

    loads = []
    for q in range(4):
        block = coarse_ref.at[0, :, pl.ds((q // 2) * HALF, HALF), pl.ds((q % 2) * HALF, HALF)]
        loads.append(pltpu.make_async_copy(block, quads.at[q], load_sem.at[q]))
    for load in loads:
        load.start()
    small = []
    pairs = (
        (parents_hbm, parents_ref),
        (counts_hbm, counts_ref),
        (nb_hbm, nb_ref),
        (diff_hbm, diff_ref),
        (grow_hbm, grow_ref),
    )
    for n, (src, dst) in enumerate(pairs):
        small.append(pltpu.make_async_copy(src, dst, small_sem.at[n]))
        small[n].start()
    land_load = pltpu.make_async_copy(land_ref, land.at[pl.ds(0, 3)], land_sem)
    land_load.start()
    barrier = pltpu.get_barrier_semaphore()
    for n in range(len(steps)):

        @pl.when(exists[n])
        def _(n=n):
            pl.semaphore_signal(barrier, inc=1, device_id=(reach[n],), device_id_type=MESH)


    shape = (SIDE, SIDE)
    columns_up = prolong_weights(iota(shape, 1), iota(shape, 0) & (HALF - 1))
    phases_across = prolong_weights(phased(iota(shape, 1)), iota(shape, 0) & (HALF - 1))
    phases_along = prolong_weights(phased(iota(shape, 0)), iota(shape, 1) & (HALF - 1))
    weave = jnp.where(phased(iota(shape, 0)) == iota(shape, 1), 1.0, 0.0).astype(jnp.bfloat16)
    unweave = jnp.where(phased(iota(shape, 1)) == iota(shape, 0), 1.0, 0.0).astype(jnp.bfloat16)
    edge = iota((16, SIDE), 0)
    edge = jnp.where(edge < 8, edge, SIDE + 7 - edge)
    edge_up = prolong_weights(edge, iota((16, SIDE), 1) & (HALF - 1))
    rim = iota((16, SIDE), 0)
    rim = jnp.where(rim < 8, rim, HALF + 7 - rim)
    rim_pick = jnp.where((iota((16, SIDE), 1) & (HALF - 1)) == rim, 1.0, 0.0).astype(jnp.bfloat16)
    edge_and_rim = jnp.concatenate([edge_up, rim_pick], axis=0)
    edge_pick = jnp.where(iota((16, SIDE), 1) == edge, 1.0, 0.0).astype(jnp.bfloat16)
    for buf in stages:
        for i in range(2):
            for c in range(3):
                for y in range(2):
                    for x in range(2):
                        buf[i, c, y, x, 0:PAD] = jnp.zeros((PAD, HALF), jnp.float32)
                        buf[i, c, y, x, PAD + HALF :] = jnp.zeros((PAD, HALF), jnp.float32)

    def face_copies():
        ends = [
            (face_data.at[pl.ds(3, 2)], face_data.at[pl.ds(1, 2)]),
            (face_data.at[pl.ds(3, 2)], face_data.at[pl.ds(5, 2)]),
            (face_data.at[4], face_data.at[0]),
            (face_data.at[3], face_data.at[7]),
        ]
        made = []
        for n, (src, dst) in enumerate(ends):
            made.append(
                pltpu.make_async_remote_copy(
                    src_ref=src,
                    dst_ref=dst,
                    send_sem=face_send.at[n],
                    recv_sem=face_recv.at[n],
                    device_id=(reach[n],),
                    device_id_type=MESH,
                )
            )
        return made

    def corner_copies():
        made = []
        for n, by in enumerate(steps):
            made.append(
                pltpu.make_async_remote_copy(
                    src_ref=corner_data.at[REACH, pl.ds(0, 4)],
                    dst_ref=corner_data.at[REACH - by, pl.ds(0, 4)],
                    send_sem=corner_send.at[n],
                    recv_sem=corner_recv.at[n],
                    device_id=(reach[n],),
                    device_id_type=MESH,
                )
            )
        return made

    for load in loads + small:
        load.wait()
    parent = [parents_ref[i] % 4 for i in range(2)]
    edges = []
    for i in range(2):
        for c in range(3):
            block = quads[parent[i], c]
            across = dot_t(edge_and_rim, split(block, 1))
            along = dot(edge_and_rim, split(block, 0))
            edges += [across[0:16], along[0:16]]
            for f in range(4):
                rows = (across, along)[f // 2][16 + 8 * (f % 2) : 19 + 8 * (f % 2)]
                face_data[3 + i, f, 3 * c : 3 * c + 3, :] = rows
    edges = dot(split(jnp.concatenate(edges, axis=0), 1), columns_up).reshape(2, 3, 4, 8, SIDE)
    for c in range(3):
        t0[c] = jnp.concatenate([edges[0, c], edges[1, c]], axis=0)

    pl.semaphore_wait(barrier, sum(jnp.where(there, 1, 0) for there in exists))
    land_copy = pltpu.make_async_remote_copy(
        src_ref=land_ref.at[2 * (1 - parity)],
        dst_ref=land.at[3],
        send_sem=pair_send.at[0],
        recv_sem=pair_recv.at[0],
        device_id=(partner,),
        device_id_type=MESH,
    )
    land_copy.start()

    for i in range(2):
        for c in range(3):
            half_done = dot(split(quads[parent[i], c], 1), phases_across)
            fine = dot(phases_along, split(half_done, 0))
            for y in range(2):
                for x in range(2):
                    x_buf[i, c, y, x, PAD : PAD + HALF] = fine[
                        y * HALF : (y + 1) * HALF, x * HALF : (x + 1) * HALF
                    ]

    land_load.wait()
    land_copy.wait_recv()
    count = counts_ref[me]
    slots = []
    for i in range(2):
        even_slot = jnp.where(i >= count, 3, i)
        odd_slot = jnp.where(i - 2 + count < 0, 3, i - 2 + count)
        slots.append(jnp.where(parity == 0, even_slot, odd_slot))
    tables = (table_of(diff_ref), table_of(grow_ref))
    classes_of = []
    for i in range(2):
        classes = land[slots[i]].astype(jnp.float32).astype(jnp.bfloat16)
        classes_of.append(classes)
        rims = jnp.concatenate([dot_t(edge_pick, classes), dot(edge_pick, classes)], axis=0)
        d, g = look_up(rims, tables)
        for f in range(4):
            rows = slice(8 * f, 8 * f + 8)
            strip_diffus[4 * i + f] = d[rows]
            strip_growth[4 * i + f] = g[rows]
            for a in range(3):
                for j in range(2):
                    at = 9 + 2 * a + j
                    row = 8 * f + a
                    face_data[3 + i, f, at : at + 1, :] = rims[
                        row : row + 1, j * HALF : (j + 1) * HALF
                    ]

    lane8, sub8 = iota((8, HALF), 1), iota((8, HALF), 0)
    for i in range(2):
        for x in range(2):
            row = jnp.zeros((8, HALF), jnp.float32)
            for q in range(5):
                pf = 4 * i + x
                strip_of = t0[q, pf] if q < 3 else (strip_diffus, strip_growth)[q - 3][pf]
                for y in range(2):
                    cell = lane8 - (64 * y + 9 * q + 3 * sub8)
                    inside = (cell >= 0) & (cell < 3) & (sub8 < 3)
                    cell = jnp.clip(cell, 0, 2)
                    cell = HALF - 1 - cell if y else cell
                    part = pick_lanes(strip_of[:, y * HALF : (y + 1) * HALF], cell)
                    row = row + jnp.where(inside, part, 0.0)
            at = 2 * i + x
            corner_data[REACH, at : at + 1, :] = jnp.sum(row, axis=0, keepdims=True)

    for n, copy in enumerate(face_copies()):
        pl.when(exists[n])(copy.start)
    for n, copy in enumerate(corner_copies()):
        pl.when(exists[n])(copy.start)

    for i in range(2):
        classes = dot(classes_of[i], unweave).astype(jnp.bfloat16)
        for n in range(8):
            rows = slice(32 * n, 32 * n + 32)
            d, g = look_up(dot(weave[rows], classes), tables)
            y, m = n // 4, 32 * (n % 4)
            for x in range(2):
                diffus_buf[i, y, x, m : m + 32] = d[:, x * HALF : (x + 1) * HALF]
                growth_buf[i, y, x, m : m + 32] = g[:, x * HALF : (x + 1) * HALF]

    def cross(patch, face):
        value = nb_ref[face, patch]
        has = value >= 0
        return jnp.where(has, value, patch), jnp.where(has, face ^ 1, face)

    strip = (8, 8, SIDE)
    sub = iota(strip, 1)
    lane = iota(strip, 2)
    sub_half = iota((8, 8, HALF), 1)
    lane_half = iota((8, 8, HALF), 2)

    def gather_outer():
        first = [
            jnp.where(sub8 == 0, 1.0, jnp.where(sub8 == 1, 0.75, jnp.where(sub8 == 2, 0.25, 0.0))),
            jnp.where(sub8 == 0, 0.0, jnp.where(sub8 == 1, 0.25, 0.75)),
            jnp.where(sub8 >= 3, 0.25, 0.0),
        ]
        index = {}
        for kind in range(2):
            for e in range(2):
                b = jnp.minimum(lane8 if e else HALF - 1 - lane8, 2)
                a = jnp.minimum(sub8, 2)
                index[kind, e] = 3 * a + b if kind == 0 else 3 * b + a
        walls, classes = [], []
        for i in range(2):
            for f in range(4):
                patch, face = cross(2 * me + i, f)
                where = jnp.clip(patch - (2 * me - 3), 0, 7)
                for c in range(3):
                    parts = []
                    for a in range(3):
                        at = 3 * c + a
                        row = face_data[where, face, at : at + 1, :]
                        parts.append(first[a] * jnp.broadcast_to(row, (8, HALF)))
                    walls.append(parts[0] + parts[1] + parts[2])
                for j in range(2):
                    rows = []
                    for a in range(3):
                        at = 9 + 2 * a + j
                        rows.append(
                            jnp.broadcast_to(face_data[where, face, at : at + 1, :], (8, HALF))
                        )
                    classes.append(jnp.where(sub8 == 0, rows[0], jnp.where(sub8 == 1, rows[1], rows[2])))
        walls = dot(split(jnp.concatenate(walls, axis=0), 1), columns_up).reshape(8, 3, 8, SIDE)
        d, g = look_up(jnp.concatenate(classes, axis=0), tables)
        d, g = d.reshape(8, 2, 8, HALF), g.reshape(8, 2, 8, HALF)
        for c in range(3):
            h0[c, :, :, HALF : HALF + SIDE] = walls[:, c]
        for j in range(2):
            at = slice(HALF + j * HALF, 2 * HALF + j * HALF)
            outer_diffus[:, :, at] = d[:, j]
            outer_growth[:, :, at] = g[:, j]

        for i in range(2):
            for f in range(4):
                pf = 4 * i + f
                kind = f // 2
                for e in range(2):
                    patch, wall = cross(2 * me + i, f)
                    side = 2 * (1 - kind) + e
                    for step in range(3):
                        if step % 2 == 0:
                            patch, side = cross(patch, side)
                        else:
                            patch, wall = cross(patch, wall)
                        x = wall if kind == 0 else side
                        y = (side if kind == 0 else wall) - 2
                        window = jnp.clip((patch >> 1) - me + REACH, 0, 2 * REACH)
                        row = corner_data[window, pl.ds(2 * (patch & 1) + x, 1), :]
                        row = jnp.broadcast_to(row, (8, HALF))
                        row = jnp.where(y == 1, pltpu.roll(row, 64, 1), row)
                        for q in range(5 if step < 2 else 3):
                            if step < 2:
                                tile = pick_lanes(row, index[kind, e] + 9 * q)
                            else:
                                tile = pick_lanes(row, jnp.full((8, HALF), 9 * q, jnp.int32))
                            near = slice(3 * HALF * e, 3 * HALF * e + HALF)
                            far = slice(HALF * e, HALF * e + HALF)
                            if step == 0 and q < 3:
                                h0[q, pf, :, near] = tile
                            elif step == 0:
                                (outer_diffus, outer_growth)[q - 3][pf, :, near] = tile
                            elif step == 1 and q < 3:
                                l0[q, pf, :, far] = tile
                            elif step == 1:
                                (far_diffus, far_growth)[q - 3][pf, :, far] = tile
                            else:
                                k0[q, pf, :, far] = tile

    def rates_of(s, now, laps, diffus, growth):
        return scaled_rates(WEIGHTS[s], *now, *laps, diffus, growth)

    def strip_laplacian(now, beyond):
        ghost = jnp.broadcast_to(beyond[:, 0:1, :], strip)
        low = jnp.sum(
            jnp.where(lane_half == sub_half, ghost[:, :, :HALF], 0.0), axis=2, keepdims=True
        )
        high = jnp.sum(
            jnp.where(lane_half == HALF - 1 - sub_half, ghost[:, :, HALF:], 0.0),
            axis=2,
            keepdims=True,
        )
        ends = []
        for e in range(2):
            columns = []
            for i in range(2):
                for f in range(4):
                    face = 4 * i + (2 if f < 2 else 0) + e
                    columns.append((low, high)[f % 2][face])
            ends.append(jnp.stack(columns, axis=0))
        above = jnp.where(sub == 0, ghost, pltpu.roll(now, 1, 1))
        below = pltpu.roll(now, 7, 1)
        left = jnp.where(lane == 0, ends[0], pltpu.roll(now, 1, 2))
        right = jnp.where(lane == SIDE - 1, ends[1], pltpu.roll(now, SIDE - 1, 2))
        return (left + right) + (below + above) - 4.0 * now

    wide = (8, 8, 2 * SIDE)

    def wide_laplacian(now, facing):
        above = jnp.where(iota(wide, 1) == 0, facing, pltpu.roll(now, 1, 1))
        below = pltpu.roll(now, 7, 1)
        sides = pltpu.roll(now, 1, 2) + pltpu.roll(now, 2 * SIDE - 1, 2)
        return sides + (below + above) - 4.0 * now

    def two_ends(block):
        return jnp.concatenate([block[:, :, :HALF], block[:, :, HALF + SIDE :]], axis=2)

    def between(ends, middle):
        return jnp.concatenate([ends[:, :, :HALF], middle, ends[:, :, HALF:]], axis=2)

    middle = slice(HALF, HALF + SIDE)

    def strip_stage(s):
        inner = [strips[s][c] for c in range(3)]
        beyond = [outer[s][c, :, :, middle] for c in range(3)]
        laps = [strip_laplacian(inner[c], beyond[c]) for c in range(3)]
        rates = rates_of(s, inner, laps, strip_diffus[...], strip_growth[...])
        if s == 3:
            for c in range(3):
                block = combine(t0[c], t1[c], t2[c], t3[c], rates[c])
                for i in range(2):
                    ring[i, c] = block[4 * i : 4 * i + 4]
                    for f in (1, 3):
                        for r in range(4):
                            ring[i, c, f, 7 - r : 8 - r, :] = block[4 * i + f, r : r + 1, :]
            return
        for c in range(3):
            strips[s + 1][c] = t0[c] + rates[c]
        if s == 2:
            now = beyond
            laps = []
            for c in range(3):
                whole = outer[s][c]
                above = jnp.where(sub == 0, inner[c], pltpu.roll(now[c], 1, 1))
                sides = pltpu.roll(whole, 1, 2) + pltpu.roll(whole, 2 * SIDE - 1, 2)
                laps.append(
                    sides[:, :, middle] + (pltpu.roll(now[c], 7, 1) + above) - 4.0 * now[c]
                )
            rates = rates_of(
                s, now, laps, outer_diffus[:, :, middle], outer_growth[:, :, middle]
            )
            for c in range(3):
                outer[3][c, :, :, middle] = h0[c, :, :, middle] + rates[c]
            return
        far = [(l0, l1)[s][c] for c in range(3)]
        now = [outer[s][c] for c in range(3)]
        laps = [wide_laplacian(now[c], between(far[c], inner[c])) for c in range(3)]
        rates = rates_of(s, now, laps, outer_diffus[...], outer_growth[...])
        for c in range(3):
            outer[s + 1][c] = h0[c] + rates[c]
        if s == 0:
            laps = []
            for c in range(3):
                lap = wide_laplacian(between(far[c], k0[c]), now[c])
                laps.append(two_ends(lap))
            rates = rates_of(s, far, laps, far_diffus[...], far_growth[...])
            for c in range(3):
                l1[c] = far[c] + rates[c]

    def bulk_stage(i, s):
        src = stages[s]
        dst = stages[(s + 1) % 4] if s < 3 else s2_buf

        def step_rows(step, carry):
            r = pl.multiple_of(step * 8, 8)
            at = PAD + r
            here = pl.ds(at, 8)
            now = [[src[i, c, n // 2, n % 2, here, :] for n in range(4)] for c in range(3)]
            lap = [[None] * 4 for _ in range(3)]
            for c in range(3):
                for n in range(4):
                    y, x = n // 2, n % 2
                    beside = now[c][2 * y + 1 - x]
                    beyond = pltpu.roll(beside, HALF - 1 if x else 1, 1)
                    upright = now[c][2 * (1 - y) + x]
                    further = src[i, c, 1 - y, x, pl.ds(at + 2 * y - 1, 8), :]
                    lap[c][n] = (beside + beyond) + (upright + further) - 4.0 * now[c][n]
            for n in range(4):
                y, x = n // 2, n % 2
                rates = scaled_rates(
                    WEIGHTS[s],
                    *[now[c][n] for c in range(3)],
                    *[lap[c][n] for c in range(3)],
                    diffus_buf[i, y, x, pl.ds(r, 8), :],
                    growth_buf[i, y, x, pl.ds(r, 8), :],
                )
                for c in range(3):
                    base = now[c][n] if s == 0 else x_buf[i, c, y, x, here, :]
                    if s < 3:
                        value = base + rates[c]
                    else:
                        value = combine(
                            base,
                            s2_buf[i, c, y, x, here, :],
                            s3_buf[i, c, y, x, here, :],
                            now[c][n],
                            rates[c],
                        )
                    dst[i, c, y, x, here, :] = value
            return carry

        lax.fori_loop(0, HALF // 8, step_rows, 0, unroll=4)

    def bulk_weave(i):
        for c in range(3):
            for y in range(2):
                both = jnp.concatenate(
                    [s2_buf[i, c, y, x, PAD : PAD + HALF, :] for x in range(2)], axis=1
                )
                high = both.astype(jnp.bfloat16)
                low = (both - high.astype(jnp.float32)).astype(jnp.bfloat16)
                woven = dot(high, weave) + dot(low, weave)
                for j in range(2):
                    result[i, c, j, pl.ds(y, HALF, stride=2), :] = woven[:, j * HALF : (j + 1) * HALF]

    def to_partner(n, src, dst):
        return pltpu.make_async_remote_copy(
            src_ref=src.at[moving],
            dst_ref=dst.at[2],
            send_sem=pair_send.at[n],
            recv_sem=pair_recv.at[n],
            device_id=(partner,),
            device_id_type=MESH,
        )

    result_copy = to_partner(1, result, result_out)
    ring_copy = to_partner(2, ring, ring_out)
    own_copies = []
    for i in range(2):
        own_copies.append(pltpu.make_async_copy(result.at[i], result_out.at[i], own_sem.at[i]))
    own_copies.append(pltpu.make_async_copy(ring, ring_out.at[pl.ds(0, 2)], own_sem.at[2]))
    for i in (moving, parity):
        for s in range(4):
            bulk_stage(i, s)
        bulk_weave(i)
        if i is moving:
            result_copy.start()
    for n, copy in enumerate(face_copies()):
        pl.when(exists[n ^ 1])(copy.wait_recv)
    for n, copy in enumerate(corner_copies()):
        pl.when(exists[n ^ 1])(copy.wait_recv)
    gather_outer()
    for s in range(4):
        strip_stage(s)
    ring_copy.start()
    for copy in own_copies:
        copy.start()
    for n, copy in enumerate(face_copies()):
        pl.when(exists[n])(copy.wait_send)
    for n, copy in enumerate(corner_copies()):
        pl.when(exists[n])(copy.wait_send)
    land_copy.wait_send()
    for copy in own_copies:
        copy.wait()
    result_copy.wait()
    ring_copy.wait()


def merge_kernel(
    counts_hbm,
    result_hbm,
    ring_hbm,
    out_hbm,
    counts_ref,
    result,
    ring,
    zeros,
    count_sem,
    ring_sem,
    result_sem,
    out_sem,
    zero_sem,
):
    me = lax.axis_index("owner")
    even = me % 2 == 0
    count_copy = pltpu.make_async_copy(counts_hbm, counts_ref, count_sem)
    ring_copy = pltpu.make_async_copy(ring_hbm, ring, ring_sem)
    count_copy.start()
    ring_copy.start()

    def load(e, c):
        return pltpu.make_async_copy(result_hbm.at[e, c], result.at[e, c], result_sem.at[e, c])

    for e in range(3):
        for c in range(3):
            load(e, c).start()
    zeros[...] = jnp.zeros_like(zeros)
    count_copy.wait()
    count = counts_ref[me]
    empties = []
    for s in (1, 2):
        empties.append(pltpu.make_async_copy(zeros, out_hbm.at[s], zero_sem.at[s - 1]))
        pl.when(s >= count)(empties[-1].start)

    slots = []
    for e in range(3):
        slot = jnp.where(even, e, (e + 1) % 3 + count - 3)
        slots.append((slot, (slot >= 0) & (slot < count)))
    low_lanes = iota((8, HALF), 1) < 4
    high_lanes = iota((8, HALF), 1) >= HALF - 4
    sub_rows = iota((8, HALF), 0)
    ring_copy.wait()

    def stores(e, c):
        made = []
        for j in range(2):
            made.append(
                pltpu.make_async_copy(
                    result.at[e, c, j],
                    out_hbm.at[jnp.maximum(slots[e][0], 0), c, :, pl.ds(j * HALF, HALF)],
                    out_sem.at[e, c, j],
                )
            )
        return made

    for e in range(3):
        for c in range(3):
            gap = jnp.zeros((HALF - 16, SIDE), jnp.float32)
            block = jnp.concatenate([ring[e, c, 0], gap, ring[e, c, 1]], axis=0)
            sides = (block[:, :HALF].T, block[:, HALF:].T)
            load(e, c).wait()
            for j in range(2):
                lanes = high_lanes if j else low_lanes
                for t in range(SIDE // 8):
                    rows = slice(8 * t, 8 * t + 8)
                    within = slice(8 * t % HALF, 8 * t % HALF + 8)
                    value = jnp.where(lanes, sides[t // 16][within], result[e, c, j, rows, :])
                    if t == 0:
                        value = jnp.where(
                            sub_rows < 4, ring[e, c, 2, :, j * HALF : (j + 1) * HALF], value
                        )
                    if t == SIDE // 8 - 1:
                        value = jnp.where(
                            sub_rows >= 4, ring[e, c, 3, :, j * HALF : (j + 1) * HALF], value
                        )
                    result[e, c, j, rows, :] = value

            @pl.when(slots[e][1])
            def _(e=e, c=c):
                for copy in stores(e, c):
                    copy.start()

    for e in range(3):

        @pl.when(slots[e][1])
        def _(e=e):
            for c in range(3):
                for copy in stores(e, c):
                    copy.wait()

    for s in (1, 2):
        pl.when(s >= count)(empties[s - 1].wait)


def body(coarse, parents, new_counts, neighbours, land_cover, class_diffusivity, class_growth):
    owners = lax.axis_size("owner")
    f32 = jnp.float32
    hbm = pl.BlockSpec(memory_space=pltpu.HBM)
    stage_buf = pltpu.VMEM((2, 3, 2, 2, HALF + 2 * PAD, HALF), f32)
    strip_buf = pltpu.VMEM((3, 8, 8, SIDE), f32)
    outer_buf = pltpu.VMEM((3, 8, 8, 2 * SIDE), f32)
    results = jax.ShapeDtypeStruct((3, 3, 2, SIDE, HALF), f32)
    rings = jax.ShapeDtypeStruct((3, 3, 4, 8, SIDE), f32)
    whole, outer = pl.pallas_call(
        functools.partial(kernel, owners),
        out_shape=(results, rings),
        in_specs=[hbm] * 7,
        out_specs=(hbm, hbm),
        scratch_shapes=[
            pltpu.SMEM((2,), jnp.int32),
            pltpu.SMEM((owners,), jnp.int32),
            pltpu.SMEM((4, 2 * owners), jnp.int32),
            pltpu.SMEM((CLASSES,), f32),
            pltpu.SMEM((CLASSES,), f32),
            pltpu.VMEM((4, 3, HALF, HALF), f32),
            pltpu.VMEM((4, SIDE, SIDE), jnp.int32),
            stage_buf,
            stage_buf,
            stage_buf,
            stage_buf,
            pltpu.VMEM((2, 2, 2, HALF, HALF), f32),
            pltpu.VMEM((2, 2, 2, HALF, HALF), f32),
            pltpu.VMEM((2, 3, 2, SIDE, HALF), f32),
            pltpu.VMEM((2, 3, 4, 8, SIDE), f32),
            strip_buf,
            strip_buf,
            strip_buf,
            strip_buf,
            pltpu.VMEM((8, 8, SIDE), f32),
            pltpu.VMEM((8, 8, SIDE), f32),
            pltpu.VMEM((8, 4, 16, HALF), f32),
            pltpu.VMEM((2 * REACH + 1, 8, HALF), f32),
            outer_buf,
            outer_buf,
            outer_buf,
            outer_buf,
            pltpu.VMEM((8, 8, 2 * SIDE), f32),
            pltpu.VMEM((8, 8, 2 * SIDE), f32),
            strip_buf,
            strip_buf,
            pltpu.VMEM((8, 8, SIDE), f32),
            pltpu.VMEM((8, 8, SIDE), f32),
            strip_buf,
            pltpu.SemaphoreType.DMA((4,)),
            pltpu.SemaphoreType.DMA((5,)),
            pltpu.SemaphoreType.DMA,
            pltpu.SemaphoreType.DMA((4,)),
            pltpu.SemaphoreType.DMA((4,)),
            pltpu.SemaphoreType.DMA((2 * REACH,)),
            pltpu.SemaphoreType.DMA((2 * REACH,)),
            pltpu.SemaphoreType.DMA((3,)),
            pltpu.SemaphoreType.DMA((3,)),
            pltpu.SemaphoreType.DMA((3,)),
        ],
        compiler_params=pltpu.CompilerParams(
            collective_id=0, has_side_effects=True, vmem_limit_bytes=62 * 1024 * 1024
        ),
        name="regrid_step",
    )(parents, new_counts, neighbours.T, class_diffusivity, class_growth, coarse, land_cover)
    return pl.pallas_call(
        merge_kernel,
        out_shape=jax.ShapeDtypeStruct((3, 3, SIDE, SIDE), f32),
        in_specs=[hbm] * 3,
        out_specs=hbm,
        scratch_shapes=[
            pltpu.SMEM((owners,), jnp.int32),
            pltpu.VMEM(results.shape, f32),
            pltpu.VMEM(rings.shape, f32),
            pltpu.VMEM((3, SIDE, SIDE), f32),
            pltpu.SemaphoreType.DMA,
            pltpu.SemaphoreType.DMA,
            pltpu.SemaphoreType.DMA((3, 3)),
            pltpu.SemaphoreType.DMA((3, 3, 2)),
            pltpu.SemaphoreType.DMA((2,)),
        ],
        compiler_params=pltpu.CompilerParams(vmem_limit_bytes=62 * 1024 * 1024),
        name="merge_slots",
    )(new_counts, whole, outer)


def solution(mesh):
    return jax.shard_map(
        body,
        mesh=mesh,
        in_specs=(
            P("owner", None, None, None),
            P("owner"),
            P(),
            P(),
            P("owner", None, None),
            P(),
            P(),
        ),
        out_specs=P("owner", None, None, None),
        check_vma=False,
    )
```

```python
import functools

import jax
import jax.numpy as jnp
from jax import lax
from jax.experimental import pallas as pl
from jax.experimental.pallas import tpu as pltpu
from jax.sharding import PartitionSpec as P

SIDE = 256
HALF = 128
CLASSES = 11
PAD = 8
REACH = 6
VMEM_LIMIT = 62 * 1024 * 1024
WEIGHTS = (0.5, 0.5, 1.0, 1.0 / 6.0)
MESH = pl.DeviceIdType.MESH


def iota(shape, dim):
    return lax.broadcasted_iota(jnp.int32, shape, dim)


def phased(index):
    return 2 * (index & (HALF - 1)) + (index >> 7)


def prolong_weights(fine, coarse):
    near = fine >> 1
    second = jnp.clip(near + jnp.where((fine & 1) == 0, -1, 1), 0, HALF - 1)
    heavy = jnp.where(coarse == near, 0.75, 0.0)
    light = jnp.where(coarse == second, 0.25, 0.0)
    return (heavy + light).astype(jnp.bfloat16)


def split(block, axis):
    high = block.astype(jnp.bfloat16)
    low = (block - high.astype(jnp.float32)).astype(jnp.bfloat16)
    return jnp.concatenate([high, low], axis=axis)


def dot(a, b):
    return jnp.dot(a, b, preferred_element_type=jnp.float32)


def dot_t(a, b):
    return lax.dot_general(a, b, (((1,), (1,)), ((), ())), preferred_element_type=jnp.float32)


def table_of(ref):
    lane = iota((8, HALF), 1)
    table = jnp.zeros((8, HALF), jnp.float32)
    for number in range(CLASSES):
        table = jnp.where(lane == number, ref[number], table)
    return table


def pick_lanes(table, index):
    return jnp.take_along_axis(table, index, axis=1)


def look_up(classes, tables):
    index = classes.astype(jnp.int32)
    rows, columns = classes.shape
    found = []
    for table in tables:
        bands = []
        for r in range(0, rows, 8):
            blocks = [
                pick_lanes(table, index[r : r + 8, k : k + HALF]) for k in range(0, columns, HALF)
            ]
            bands.append(jnp.concatenate(blocks, axis=1))
        found.append(jnp.concatenate(bands, axis=0))
    return found


def scaled_rates(weight, x0, x1, x2, lap0, lap1, lap2, diffus, growth):
    dw = diffus * weight
    gw = growth * weight
    xw = x0 * weight
    r0 = dw * lap0 + (gw * x0) * (x1 - x0 - x2)
    r1 = (0.5 * dw) * lap1 + (0.4 * weight - x1 * (0.4 * weight + xw))
    r2 = dw * lap2 + (xw - (0.3 * weight) * x2)
    return r0, r1, r2


def combine(x, s2, s3, s4, rate):
    return (s2 + 2.0 * s3 + s4 - x) * (1.0 / 3.0) + rate


def kernel(
    owners,
    parents_hbm,
    counts_hbm,
    nb_hbm,
    diff_hbm,
    grow_hbm,
    coarse_ref,
    land_ref,
    result_out,
    ring_out,
    parents_ref,
    counts_ref,
    nb_ref,
    diff_ref,
    grow_ref,
    quads,
    land,
    x_buf,
    s2_buf,
    s3_buf,
    s4_buf,
    diffus_buf,
    growth_buf,
    result,
    ring,
    t0,
    t1,
    t2,
    t3,
    strip_diffus,
    strip_growth,
    face_data,
    corner_data,
    h0,
    h1,
    h2,
    h3,
    outer_diffus,
    outer_growth,
    l0,
    l1,
    far_diffus,
    far_growth,
    k0,
    load_sem,
    small_sem,
    land_sem,
    face_send,
    face_recv,
    corner_send,
    corner_recv,
    pair_send,
    pair_recv,
    own_sem,
):
    me = lax.axis_index("owner")
    parity = me % 2
    partner = me + 1 - 2 * parity
    moving = 1 - parity
    steps = [by for far in range(1, REACH + 1) for by in (far, -far)]
    reach = [(me + by) % owners for by in steps]
    exists = [(me + by < owners) & (me + by >= 0) for by in steps]
    stages = (x_buf, s2_buf, s3_buf, s4_buf)
    strips = (t0, t1, t2, t3)
    outer = (h0, h1, h2, h3)

    loads = []
    for q in range(4):
        block = coarse_ref.at[0, :, pl.ds((q // 2) * HALF, HALF), pl.ds((q % 2) * HALF, HALF)]
        loads.append(pltpu.make_async_copy(block, quads.at[q], load_sem.at[q]))
    for load in loads:
        load.start()
    small = []
    pairs = (
        (parents_hbm, parents_ref),
        (counts_hbm, counts_ref),
        (nb_hbm, nb_ref),
        (diff_hbm, diff_ref),
        (grow_hbm, grow_ref),
    )
    for n, (src, dst) in enumerate(pairs):
        small.append(pltpu.make_async_copy(src, dst, small_sem.at[n]))
        small[n].start()
    land_load = pltpu.make_async_copy(land_ref, land.at[pl.ds(0, 3)], land_sem)
    land_load.start()
    barrier = pltpu.get_barrier_semaphore()
    for n in range(len(steps)):

        @pl.when(exists[n])
        def _(n=n):
            pl.semaphore_signal(barrier, inc=1, device_id=(reach[n],), device_id_type=MESH)


    shape = (SIDE, SIDE)
    columns_up = prolong_weights(iota(shape, 1), iota(shape, 0) & (HALF - 1))
    phases_across = prolong_weights(phased(iota(shape, 1)), iota(shape, 0) & (HALF - 1))
    phases_along = prolong_weights(phased(iota(shape, 0)), iota(shape, 1) & (HALF - 1))
    weave = jnp.where(phased(iota(shape, 0)) == iota(shape, 1), 1.0, 0.0).astype(jnp.bfloat16)
    unweave = jnp.where(phased(iota(shape, 1)) == iota(shape, 0), 1.0, 0.0).astype(jnp.bfloat16)
    edge = iota((16, SIDE), 0)
    edge = jnp.where(edge < 8, edge, SIDE + 7 - edge)
    edge_up = prolong_weights(edge, iota((16, SIDE), 1) & (HALF - 1))
    rim = iota((16, SIDE), 0)
    rim = jnp.where(rim < 8, rim, HALF + 7 - rim)
    rim_pick = jnp.where((iota((16, SIDE), 1) & (HALF - 1)) == rim, 1.0, 0.0).astype(jnp.bfloat16)
    edge_and_rim = jnp.concatenate([edge_up, rim_pick], axis=0)
    edge_pick = jnp.where(iota((16, SIDE), 1) == edge, 1.0, 0.0).astype(jnp.bfloat16)
    for buf in stages:
        for i in range(2):
            for c in range(3):
                for y in range(2):
                    for x in range(2):
                        buf[i, c, y, x, 0:PAD] = jnp.zeros((PAD, HALF), jnp.float32)
                        buf[i, c, y, x, PAD + HALF :] = jnp.zeros((PAD, HALF), jnp.float32)

    def face_copies():
        ends = [
            (face_data.at[pl.ds(3, 2)], face_data.at[pl.ds(1, 2)]),
            (face_data.at[pl.ds(3, 2)], face_data.at[pl.ds(5, 2)]),
            (face_data.at[4], face_data.at[0]),
            (face_data.at[3], face_data.at[7]),
        ]
        made = []
        for n, (src, dst) in enumerate(ends):
            made.append(
                pltpu.make_async_remote_copy(
                    src_ref=src,
                    dst_ref=dst,
                    send_sem=face_send.at[n],
                    recv_sem=face_recv.at[n],
                    device_id=(reach[n],),
                    device_id_type=MESH,
                )
            )
        return made

    def corner_copies():
        made = []
        for n, by in enumerate(steps):
            made.append(
                pltpu.make_async_remote_copy(
                    src_ref=corner_data.at[REACH, pl.ds(0, 4)],
                    dst_ref=corner_data.at[REACH - by, pl.ds(0, 4)],
                    send_sem=corner_send.at[n],
                    recv_sem=corner_recv.at[n],
                    device_id=(reach[n],),
                    device_id_type=MESH,
                )
            )
        return made

    pl.semaphore_wait(barrier, sum(jnp.where(there, 1, 0) for there in exists))
    land_copy = pltpu.make_async_remote_copy(
        src_ref=land_ref.at[2 * (1 - parity)],
        dst_ref=land.at[3],
        send_sem=pair_send.at[0],
        recv_sem=pair_recv.at[0],
        device_id=(partner,),
        device_id_type=MESH,
    )
    land_copy.start()

    for load in loads + small:
        load.wait()
    parent = [parents_ref[i] % 4 for i in range(2)]
    edges = []
    for i in range(2):
        for c in range(3):
            block = quads[parent[i], c]
            across = dot_t(edge_and_rim, split(block, 1))
            along = dot(edge_and_rim, split(block, 0))
            edges += [across[0:16], along[0:16]]
            for f in range(4):
                rows = (across, along)[f // 2][16 + 8 * (f % 2) : 19 + 8 * (f % 2)]
                face_data[3 + i, f, 3 * c : 3 * c + 3, :] = rows
    edges = dot(split(jnp.concatenate(edges, axis=0), 1), columns_up).reshape(2, 3, 4, 8, SIDE)
    for c in range(3):
        t0[c] = jnp.concatenate([edges[0, c], edges[1, c]], axis=0)

    for i in range(2):
        for c in range(3):
            half_done = dot(split(quads[parent[i], c], 1), phases_across)
            fine = dot(phases_along, split(half_done, 0))
            for y in range(2):
                for x in range(2):
                    x_buf[i, c, y, x, PAD : PAD + HALF] = fine[
                        y * HALF : (y + 1) * HALF, x * HALF : (x + 1) * HALF
                    ]

    land_load.wait()
    land_copy.wait_recv()
    count = counts_ref[me]
    slots = []
    for i in range(2):
        even_slot = jnp.where(i >= count, 3, i)
        odd_slot = jnp.where(i - 2 + count < 0, 3, i - 2 + count)
        slots.append(jnp.where(parity == 0, even_slot, odd_slot))
    tables = (table_of(diff_ref), table_of(grow_ref))
    classes_of = []
    for i in range(2):
        classes = land[slots[i]].astype(jnp.float32).astype(jnp.bfloat16)
        classes_of.append(classes)
        rims = jnp.concatenate([dot_t(edge_pick, classes), dot(edge_pick, classes)], axis=0)
        d, g = look_up(rims, tables)
        for f in range(4):
            rows = slice(8 * f, 8 * f + 8)
            strip_diffus[4 * i + f] = d[rows]
            strip_growth[4 * i + f] = g[rows]
            for a in range(3):
                for j in range(2):
                    at = 9 + 2 * a + j
                    row = 8 * f + a
                    face_data[3 + i, f, at : at + 1, :] = rims[
                        row : row + 1, j * HALF : (j + 1) * HALF
                    ]

    lane8, sub8 = iota((8, HALF), 1), iota((8, HALF), 0)
    for i in range(2):
        for x in range(2):
            row = jnp.zeros((8, HALF), jnp.float32)
            for q in range(5):
                pf = 4 * i + x
                strip_of = t0[q, pf] if q < 3 else (strip_diffus, strip_growth)[q - 3][pf]
                for y in range(2):
                    cell = lane8 - (64 * y + 9 * q + 3 * sub8)
                    inside = (cell >= 0) & (cell < 3) & (sub8 < 3)
                    cell = jnp.clip(cell, 0, 2)
                    cell = HALF - 1 - cell if y else cell
                    part = pick_lanes(strip_of[:, y * HALF : (y + 1) * HALF], cell)
                    row = row + jnp.where(inside, part, 0.0)
            at = 2 * i + x
            corner_data[REACH, at : at + 1, :] = jnp.sum(row, axis=0, keepdims=True)

    for n, copy in enumerate(face_copies()):
        pl.when(exists[n])(copy.start)
    for n, copy in enumerate(corner_copies()):
        pl.when(exists[n])(copy.start)

    for i in range(2):
        classes = dot(classes_of[i], unweave).astype(jnp.bfloat16)
        for n in range(8):
            rows = slice(32 * n, 32 * n + 32)
            d, g = look_up(dot(weave[rows], classes), tables)
            y, m = n // 4, 32 * (n % 4)
            for x in range(2):
                diffus_buf[i, y, x, m : m + 32] = d[:, x * HALF : (x + 1) * HALF]
                growth_buf[i, y, x, m : m + 32] = g[:, x * HALF : (x + 1) * HALF]

    def cross(patch, face):
        value = nb_ref[face, patch]
        has = value >= 0
        return jnp.where(has, value, patch), jnp.where(has, face ^ 1, face)

    strip = (8, 8, SIDE)
    sub = iota(strip, 1)
    lane_half = iota((8, 8, HALF), 2)

    def gather_outer():
        first = [
            jnp.where(sub8 == 0, 1.0, jnp.where(sub8 == 1, 0.75, jnp.where(sub8 == 2, 0.25, 0.0))),
            jnp.where(sub8 == 0, 0.0, jnp.where(sub8 == 1, 0.25, 0.75)),
            jnp.where(sub8 >= 3, 0.25, 0.0),
        ]
        index = {}
        for kind in range(2):
            for e in range(2):
                b = jnp.minimum(lane8 if e else HALF - 1 - lane8, 2)
                a = jnp.minimum(sub8, 2)
                index[kind, e] = 3 * a + b if kind == 0 else 3 * b + a
        walls, classes = [], []
        for i in range(2):
            for f in range(4):
                patch, face = cross(2 * me + i, f)
                where = jnp.clip(patch - (2 * me - 3), 0, 7)
                for c in range(3):
                    parts = []
                    for a in range(3):
                        at = 3 * c + a
                        row = face_data[where, face, at : at + 1, :]
                        parts.append(first[a] * jnp.broadcast_to(row, (8, HALF)))
                    walls.append(parts[0] + parts[1] + parts[2])
                for j in range(2):
                    rows = []
                    for a in range(3):
                        at = 9 + 2 * a + j
                        rows.append(
                            jnp.broadcast_to(face_data[where, face, at : at + 1, :], (8, HALF))
                        )
                    classes.append(jnp.where(sub8 == 0, rows[0], jnp.where(sub8 == 1, rows[1], rows[2])))
        walls = dot(split(jnp.concatenate(walls, axis=0), 1), columns_up).reshape(8, 3, 8, SIDE)
        d, g = look_up(jnp.concatenate(classes, axis=0), tables)
        d, g = d.reshape(8, 2, 8, HALF), g.reshape(8, 2, 8, HALF)
        for c in range(3):
            h0[c, :, :, 0:SIDE] = walls[:, c]
        for j in range(2):
            at = slice(j * HALF, HALF + j * HALF)
            outer_diffus[:, :, at] = d[:, j]
            outer_growth[:, :, at] = g[:, j]

        low_half = lane8 < HALF // 2
        for i in range(2):
            for f in range(4):
                pf = 4 * i + f
                kind = f // 2
                start = cross(2 * me + i, f)
                chains = []
                for e in range(2):
                    patch, wall = start
                    side = 2 * (1 - kind) + e
                    chain = []
                    for step in range(3):
                        if step % 2 == 0:
                            patch, side = cross(patch, side)
                        else:
                            patch, wall = cross(patch, wall)
                        x = wall if kind == 0 else side
                        y = (side if kind == 0 else wall) - 2
                        window = jnp.clip((patch >> 1) - me + REACH, 0, 2 * REACH)
                        row = corner_data[window, pl.ds(2 * (patch & 1) + x, 1), :]
                        row = jnp.broadcast_to(row, (8, HALF))
                        chain.append(jnp.where(y == 1, pltpu.roll(row, 64, 1), row))
                    chains.append(chain)
                for step in range(3):
                    for q in range(5 if step < 2 else 3):
                        tiles = []
                        for e in range(2):
                            if step < 2:
                                at = index[kind, e] + 9 * q
                            else:
                                at = jnp.full((8, HALF), 9 * q, jnp.int32)
                            tiles.append(pick_lanes(chains[e][step], at))
                        if step < 2:
                            tile = jnp.where(low_half, tiles[1], tiles[0])
                        else:
                            tile = jnp.where(low_half, tiles[0], tiles[1])
                        if step == 0 and q < 3:
                            h0[q, pf, :, SIDE:] = tile
                        elif step == 0:
                            (outer_diffus, outer_growth)[q - 3][pf, :, SIDE:] = tile
                        elif step == 1 and q < 3:
                            l0[q, pf] = tile
                        elif step == 1:
                            (far_diffus, far_growth)[q - 3][pf] = tile
                        else:
                            k0[q, pf] = tile

    def rates_of(s, now, laps, diffus, growth):
        return scaled_rates(WEIGHTS[s], *now, *laps, diffus, growth)

    rising = iota((8, HALF), 0)
    falling = HALF - 1 - rising

    def strip_laplacian(now, beyond):
        ghost = jnp.broadcast_to(beyond[:, 0:1, :], strip)
        ends = []
        for e in range(2):
            columns = []
            for i in range(2):
                for f in range(4):
                    face = ghost[4 * i + (2 if f < 2 else 0) + e]
                    if f % 2:
                        columns.append(pick_lanes(face[:, HALF:], falling))
                    else:
                        columns.append(pick_lanes(face[:, :HALF], rising))
            ends.append(jnp.stack(columns, axis=0))
        above = jnp.where(sub == 0, ghost, pltpu.roll(now, 1, 1))
        below = pltpu.roll(now, 7, 1)
        rolled = pltpu.roll(now, 1, 2)
        left = jnp.where(lane_half == 0, ends[0], rolled[:, :, :HALF])
        left = jnp.concatenate([left, rolled[:, :, HALF:]], axis=2)
        rolled = pltpu.roll(now, SIDE - 1, 2)
        right = jnp.where(lane_half == HALF - 1, ends[1], rolled[:, :, HALF:])
        right = jnp.concatenate([rolled[:, :, :HALF], right], axis=2)
        return (left + right) + (below + above) - 4.0 * now

    def round_laplacian(now, facing):
        lanes = now.shape[2]
        above = jnp.where(iota(now.shape, 1) == 0, facing, pltpu.roll(now, 1, 1))
        below = pltpu.roll(now, 7, 1)
        sides = pltpu.roll(now, 1, 2) + pltpu.roll(now, lanes - 1, 2)
        return sides + (below + above) - 4.0 * now

    def strip_stage(s):
        inner = [strips[s][c] for c in range(3)]
        beyond = [outer[s][c, :, :, 0:SIDE] for c in range(3)]
        laps = [strip_laplacian(inner[c], beyond[c]) for c in range(3)]
        rates = rates_of(s, inner, laps, strip_diffus[...], strip_growth[...])
        if s == 3:
            for c in range(3):
                block = combine(t0[c], t1[c], t2[c], t3[c], rates[c])
                for i in range(2):
                    ring[i, c] = block[4 * i : 4 * i + 4]
                    for f in (1, 3):
                        for r in range(4):
                            ring[i, c, f, 7 - r : 8 - r, :] = block[4 * i + f, r : r + 1, :]
            return
        for c in range(3):
            strips[s + 1][c] = t0[c] + rates[c]
        if s == 2:
            laps = []
            for c in range(3):
                whole = outer[s][c]
                now = beyond[c]
                above = jnp.where(sub == 0, inner[c], pltpu.roll(now, 1, 1))
                sides = pltpu.roll(whole, 1, 2) + pltpu.roll(whole, SIDE + HALF - 1, 2)
                laps.append(sides[:, :, 0:SIDE] + (pltpu.roll(now, 7, 1) + above) - 4.0 * now)
            rates = rates_of(
                s, beyond, laps, outer_diffus[:, :, 0:SIDE], outer_growth[:, :, 0:SIDE]
            )
            for c in range(3):
                outer[3][c, :, :, 0:SIDE] = h0[c, :, :, 0:SIDE] + rates[c]
            return
        far = [(l0, l1)[s][c] for c in range(3)]
        now = [outer[s][c] for c in range(3)]
        laps = [
            round_laplacian(now[c], jnp.concatenate([inner[c], far[c]], axis=2)) for c in range(3)
        ]
        rates = rates_of(s, now, laps, outer_diffus[...], outer_growth[...])
        for c in range(3):
            outer[s + 1][c] = h0[c] + rates[c]
        if s == 0:
            laps = []
            for c in range(3):
                both = jnp.concatenate([far[c], k0[c]], axis=2)
                facing = jnp.concatenate([now[c][:, :, SIDE:], k0[c]], axis=2)
                laps.append(round_laplacian(both, facing)[:, :, :HALF])
            rates = rates_of(s, far, laps, far_diffus[...], far_growth[...])
            for c in range(3):
                l1[c] = far[c] + rates[c]

    def bulk_stage(i, s):
        src = stages[s]
        dst = stages[(s + 1) % 4] if s < 3 else s2_buf

        def step_rows(step, carry):
            r = pl.multiple_of(step * 8, 8)
            at = PAD + r
            here = pl.ds(at, 8)
            now = [[src[i, c, n // 2, n % 2, here, :] for n in range(4)] for c in range(3)]
            lap = [[None] * 4 for _ in range(3)]
            for c in range(3):
                for n in range(4):
                    y, x = n // 2, n % 2
                    beside = now[c][2 * y + 1 - x]
                    beyond = pltpu.roll(beside, HALF - 1 if x else 1, 1)
                    upright = now[c][2 * (1 - y) + x]
                    further = src[i, c, 1 - y, x, pl.ds(at + 2 * y - 1, 8), :]
                    lap[c][n] = (beside + beyond) + (upright + further) - 4.0 * now[c][n]
            for n in range(4):
                y, x = n // 2, n % 2
                rates = scaled_rates(
                    WEIGHTS[s],
                    *[now[c][n] for c in range(3)],
                    *[lap[c][n] for c in range(3)],
                    diffus_buf[i, y, x, pl.ds(r, 8), :],
                    growth_buf[i, y, x, pl.ds(r, 8), :],
                )
                for c in range(3):
                    base = now[c][n] if s == 0 else x_buf[i, c, y, x, here, :]
                    if s < 3:
                        value = base + rates[c]
                    else:
                        value = combine(
                            base,
                            s2_buf[i, c, y, x, here, :],
                            s3_buf[i, c, y, x, here, :],
                            now[c][n],
                            rates[c],
                        )
                    dst[i, c, y, x, here, :] = value
            return carry

        lax.fori_loop(0, HALF // 8, step_rows, 0, unroll=4)

    def bulk_weave(i):
        for c in range(3):
            for y in range(2):
                both = jnp.concatenate(
                    [s2_buf[i, c, y, x, PAD : PAD + HALF, :] for x in range(2)], axis=1
                )
                high = both.astype(jnp.bfloat16)
                low = (both - high.astype(jnp.float32)).astype(jnp.bfloat16)
                woven = dot(high, weave) + dot(low, weave)
                for j in range(2):
                    result[i, c, j, pl.ds(y, HALF, stride=2), :] = woven[:, j * HALF : (j + 1) * HALF]

    def to_partner(n, src, dst):
        return pltpu.make_async_remote_copy(
            src_ref=src.at[moving],
            dst_ref=dst.at[2],
            send_sem=pair_send.at[n],
            recv_sem=pair_recv.at[n],
            device_id=(partner,),
            device_id_type=MESH,
        )

    result_copy = to_partner(1, result, result_out)
    ring_copy = to_partner(2, ring, ring_out)
    own_copies = [
        pltpu.make_async_copy(result.at[moving], result_out.at[moving], own_sem.at[0]),
        pltpu.make_async_copy(ring, ring_out.at[pl.ds(0, 2)], own_sem.at[1]),
        pltpu.make_async_copy(result.at[parity], result_out.at[parity], own_sem.at[2]),
    ]
    for s in range(4):
        bulk_stage(moving, s)
    bulk_weave(moving)
    result_copy.start()
    own_copies[0].start()
    for s in range(2):
        bulk_stage(parity, s)
    for n, copy in enumerate(face_copies()):
        pl.when(exists[n ^ 1])(copy.wait_recv)
    for n, copy in enumerate(corner_copies()):
        pl.when(exists[n ^ 1])(copy.wait_recv)
    gather_outer()
    for s in range(4):
        strip_stage(s)
    ring_copy.start()
    own_copies[1].start()
    for s in range(2, 4):
        bulk_stage(parity, s)
    bulk_weave(parity)
    own_copies[2].start()
    for n, copy in enumerate(face_copies()):
        pl.when(exists[n])(copy.wait_send)
    for n, copy in enumerate(corner_copies()):
        pl.when(exists[n])(copy.wait_send)
    land_copy.wait_send()
    for copy in own_copies:
        copy.wait()
    result_copy.wait()
    ring_copy.wait()


def merge_kernel(
    counts_hbm,
    result_hbm,
    ring_hbm,
    out_hbm,
    counts_ref,
    result,
    ring,
    zeros,
    count_sem,
    ring_sem,
    result_sem,
    out_sem,
    zero_sem,
):
    me = lax.axis_index("owner")
    even = me % 2 == 0
    count_copy = pltpu.make_async_copy(counts_hbm, counts_ref, count_sem)
    ring_copy = pltpu.make_async_copy(ring_hbm, ring, ring_sem)
    count_copy.start()
    ring_copy.start()

    def load(e, c):
        return pltpu.make_async_copy(result_hbm.at[e, c], result.at[e, c], result_sem.at[e, c])

    for e in range(3):
        for c in range(3):
            load(e, c).start()
    zeros[...] = jnp.zeros_like(zeros)
    count_copy.wait()
    count = counts_ref[me]
    empties = []
    for s in (1, 2):
        empties.append(pltpu.make_async_copy(zeros, out_hbm.at[s], zero_sem.at[s - 1]))
        pl.when(s >= count)(empties[-1].start)

    slots = []
    for e in range(3):
        slot = jnp.where(even, e, (e + 1) % 3 + count - 3)
        slots.append((slot, (slot >= 0) & (slot < count)))
    low_lanes = iota((8, HALF), 1) < 4
    high_lanes = iota((8, HALF), 1) >= HALF - 4
    sub_rows = iota((8, HALF), 0)
    ring_copy.wait()

    def stores(e, c):
        made = []
        for j in range(2):
            made.append(
                pltpu.make_async_copy(
                    result.at[e, c, j],
                    out_hbm.at[jnp.maximum(slots[e][0], 0), c, :, pl.ds(j * HALF, HALF)],
                    out_sem.at[e, c, j],
                )
            )
        return made

    for e in range(3):
        for c in range(3):
            gap = jnp.zeros((HALF - 16, SIDE), jnp.float32)
            block = jnp.concatenate([ring[e, c, 0], gap, ring[e, c, 1]], axis=0)
            sides = (block[:, :HALF].T, block[:, HALF:].T)
            load(e, c).wait()
            for j in range(2):
                lanes = high_lanes if j else low_lanes
                for t in range(SIDE // 8):
                    rows = slice(8 * t, 8 * t + 8)
                    within = slice(8 * t % HALF, 8 * t % HALF + 8)
                    value = jnp.where(lanes, sides[t // 16][within], result[e, c, j, rows, :])
                    if t == 0:
                        value = jnp.where(
                            sub_rows < 4, ring[e, c, 2, :, j * HALF : (j + 1) * HALF], value
                        )
                    if t == SIDE // 8 - 1:
                        value = jnp.where(
                            sub_rows >= 4, ring[e, c, 3, :, j * HALF : (j + 1) * HALF], value
                        )
                    result[e, c, j, rows, :] = value

            @pl.when(slots[e][1])
            def _(e=e, c=c):
                for copy in stores(e, c):
                    copy.start()

    for e in range(3):

        @pl.when(slots[e][1])
        def _(e=e):
            for c in range(3):
                for copy in stores(e, c):
                    copy.wait()

    for s in (1, 2):
        pl.when(s >= count)(empties[s - 1].wait)


def body(coarse, parents, new_counts, neighbours, land_cover, class_diffusivity, class_growth):
    owners = lax.axis_size("owner")
    f32 = jnp.float32
    hbm = pl.BlockSpec(memory_space=pltpu.HBM)
    stage_buf = pltpu.VMEM((2, 3, 2, 2, HALF + 2 * PAD, HALF), f32)
    strip_buf = pltpu.VMEM((3, 8, 8, SIDE), f32)
    outer_buf = pltpu.VMEM((3, 8, 8, SIDE + HALF), f32)
    far_buf = pltpu.VMEM((3, 8, 8, HALF), f32)
    results = jax.ShapeDtypeStruct((3, 3, 2, SIDE, HALF), f32)
    rings = jax.ShapeDtypeStruct((3, 3, 4, 8, SIDE), f32)
    whole, outer = pl.pallas_call(
        functools.partial(kernel, owners),
        out_shape=(results, rings),
        in_specs=[hbm] * 7,
        out_specs=(hbm, hbm),
        scratch_shapes=[
            pltpu.SMEM((2,), jnp.int32),
            pltpu.SMEM((owners,), jnp.int32),
            pltpu.SMEM((4, 2 * owners), jnp.int32),
            pltpu.SMEM((CLASSES,), f32),
            pltpu.SMEM((CLASSES,), f32),
            pltpu.VMEM((4, 3, HALF, HALF), f32),
            pltpu.VMEM((4, SIDE, SIDE), jnp.int32),
            stage_buf,
            stage_buf,
            stage_buf,
            stage_buf,
            pltpu.VMEM((2, 2, 2, HALF, HALF), f32),
            pltpu.VMEM((2, 2, 2, HALF, HALF), f32),
            pltpu.VMEM((2, 3, 2, SIDE, HALF), f32),
            pltpu.VMEM((2, 3, 4, 8, SIDE), f32),
            strip_buf,
            strip_buf,
            strip_buf,
            strip_buf,
            pltpu.VMEM((8, 8, SIDE), f32),
            pltpu.VMEM((8, 8, SIDE), f32),
            pltpu.VMEM((8, 4, 16, HALF), f32),
            pltpu.VMEM((2 * REACH + 1, 8, HALF), f32),
            outer_buf,
            outer_buf,
            outer_buf,
            outer_buf,
            pltpu.VMEM((8, 8, SIDE + HALF), f32),
            pltpu.VMEM((8, 8, SIDE + HALF), f32),
            far_buf,
            far_buf,
            pltpu.VMEM((8, 8, HALF), f32),
            pltpu.VMEM((8, 8, HALF), f32),
            far_buf,
            pltpu.SemaphoreType.DMA((4,)),
            pltpu.SemaphoreType.DMA((5,)),
            pltpu.SemaphoreType.DMA,
            pltpu.SemaphoreType.DMA((4,)),
            pltpu.SemaphoreType.DMA((4,)),
            pltpu.SemaphoreType.DMA((2 * REACH,)),
            pltpu.SemaphoreType.DMA((2 * REACH,)),
            pltpu.SemaphoreType.DMA((3,)),
            pltpu.SemaphoreType.DMA((3,)),
            pltpu.SemaphoreType.DMA((3,)),
        ],
        compiler_params=pltpu.CompilerParams(
            collective_id=0, has_side_effects=True, vmem_limit_bytes=VMEM_LIMIT
        ),
        name="regrid_step",
    )(parents, new_counts, neighbours.T, class_diffusivity, class_growth, coarse, land_cover)
    return pl.pallas_call(
        merge_kernel,
        out_shape=jax.ShapeDtypeStruct((3, 3, SIDE, SIDE), f32),
        in_specs=[hbm] * 3,
        out_specs=hbm,
        scratch_shapes=[
            pltpu.SMEM((owners,), jnp.int32),
            pltpu.VMEM(results.shape, f32),
            pltpu.VMEM(rings.shape, f32),
            pltpu.VMEM((3, SIDE, SIDE), f32),
            pltpu.SemaphoreType.DMA,
            pltpu.SemaphoreType.DMA,
            pltpu.SemaphoreType.DMA((3, 3)),
            pltpu.SemaphoreType.DMA((3, 3, 2)),
            pltpu.SemaphoreType.DMA((2,)),
        ],
        compiler_params=pltpu.CompilerParams(vmem_limit_bytes=VMEM_LIMIT),
        name="merge_slots",
    )(new_counts, whole, outer)


def solution(mesh):
    return jax.shard_map(
        body,
        mesh=mesh,
        in_specs=(
            P("owner", None, None, None),
            P("owner"),
            P(),
            P(),
            P("owner", None, None),
            P(),
            P(),
        ),
        out_specs=P("owner", None, None, None),
        check_vma=False,
    )
```

```python
import functools

import jax
import jax.numpy as jnp
from jax import lax
from jax.experimental import pallas as pl
from jax.experimental.pallas import tpu as pltpu
from jax.sharding import PartitionSpec as P

SIDE = 256
HALF = 128
CLASSES = 11
PAD = 8
REACH = 6
VMEM_LIMIT = 62 * 1024 * 1024
WEIGHTS = (0.5, 0.5, 1.0, 1.0 / 6.0)
MESH = pl.DeviceIdType.MESH


def iota(shape, dim):
    return lax.broadcasted_iota(jnp.int32, shape, dim)


def phased(index):
    return 2 * (index & (HALF - 1)) + (index >> 7)


def prolong_weights(fine, coarse):
    near = fine >> 1
    second = jnp.clip(near + jnp.where((fine & 1) == 0, -1, 1), 0, HALF - 1)
    heavy = jnp.where(coarse == near, 0.75, 0.0)
    light = jnp.where(coarse == second, 0.25, 0.0)
    return (heavy + light).astype(jnp.bfloat16)


def split(block, axis):
    high = block.astype(jnp.bfloat16)
    low = (block - high.astype(jnp.float32)).astype(jnp.bfloat16)
    return jnp.concatenate([high, low], axis=axis)


def dot(a, b):
    return jnp.dot(a, b, preferred_element_type=jnp.float32)


def dot_t(a, b):
    return lax.dot_general(a, b, (((1,), (1,)), ((), ())), preferred_element_type=jnp.float32)


def table_of(ref):
    lane = iota((8, HALF), 1)
    table = jnp.zeros((8, HALF), jnp.float32)
    for number in range(CLASSES):
        table = jnp.where(lane == number, ref[number], table)
    return table


def pick_lanes(table, index):
    return jnp.take_along_axis(table, index, axis=1)


def look_up(classes, tables):
    index = classes.astype(jnp.int32)
    rows, columns = classes.shape
    found = []
    for table in tables:
        bands = []
        for r in range(0, rows, 8):
            blocks = [
                pick_lanes(table, index[r : r + 8, k : k + HALF]) for k in range(0, columns, HALF)
            ]
            bands.append(jnp.concatenate(blocks, axis=1))
        found.append(jnp.concatenate(bands, axis=0))
    return found


def scaled_rates(weight, x0, x1, x2, lap0, lap1, lap2, diffus, growth):
    dw = diffus * weight
    gw = growth * weight
    xw = x0 * weight
    r0 = dw * lap0 + (gw * x0) * (x1 - x0 - x2)
    r1 = (0.5 * dw) * lap1 + (0.4 * weight - x1 * (0.4 * weight + xw))
    r2 = dw * lap2 + (xw - (0.3 * weight) * x2)
    return r0, r1, r2


def combine(x, s2, s3, s4, rate):
    return (s2 + 2.0 * s3 + s4 - x) * (1.0 / 3.0) + rate


def kernel(
    owners,
    parents_hbm,
    counts_hbm,
    nb_hbm,
    diff_hbm,
    grow_hbm,
    coarse_ref,
    land_ref,
    result_out,
    ring_out,
    parents_ref,
    counts_ref,
    nb_ref,
    diff_ref,
    grow_ref,
    quads,
    land,
    land_far,
    x_buf,
    s2_buf,
    s3_buf,
    s4_buf,
    diffus_buf,
    growth_buf,
    result,
    ring,
    t0,
    t1,
    t2,
    t3,
    strip_diffus,
    strip_growth,
    face_data,
    corner_data,
    h0,
    h1,
    h2,
    h3,
    outer_diffus,
    outer_growth,
    l0,
    l1,
    far_diffus,
    far_growth,
    k0,
    load_sem,
    small_sem,
    land_sem,
    face_send,
    face_recv,
    corner_send,
    corner_recv,
    pair_send,
    pair_recv,
    own_sem,
):
    me = lax.axis_index("owner")
    parity = me % 2
    partner = me + 1 - 2 * parity
    moving = 1 - parity
    steps = [by for far in range(1, REACH + 1) for by in (far, -far)]
    reach = [(me + by) % owners for by in steps]
    exists = [(me + by < owners) & (me + by >= 0) for by in steps]
    stages = (x_buf, s2_buf, s3_buf, s4_buf)
    strips = (t0, t1, t2, t3)
    outer = (h0, h1, h2, h3)

    loads = []
    for q in range(4):
        block = coarse_ref.at[0, :, pl.ds((q // 2) * HALF, HALF), pl.ds((q % 2) * HALF, HALF)]
        loads.append(pltpu.make_async_copy(block, quads.at[q], load_sem.at[q]))
    for load in loads:
        load.start()
    small = []
    pairs = (
        (parents_hbm, parents_ref),
        (counts_hbm, counts_ref),
        (nb_hbm, nb_ref),
        (diff_hbm, diff_ref),
        (grow_hbm, grow_ref),
    )
    for n, (src, dst) in enumerate(pairs):
        small.append(pltpu.make_async_copy(src, dst, small_sem.at[n]))
        small[n].start()
    land_load = pltpu.make_async_copy(land_ref, land, land_sem)
    land_load.start()
    barrier = pltpu.get_barrier_semaphore()
    for n in range(len(steps)):

        @pl.when(exists[n])
        def _(n=n):
            pl.semaphore_signal(barrier, inc=1, device_id=(reach[n],), device_id_type=MESH)


    shape = (SIDE, SIDE)
    columns_up = prolong_weights(iota(shape, 1), iota(shape, 0) & (HALF - 1))
    phases_across = prolong_weights(phased(iota(shape, 1)), iota(shape, 0) & (HALF - 1))
    phases_along = prolong_weights(phased(iota(shape, 0)), iota(shape, 1) & (HALF - 1))
    weave = jnp.where(phased(iota(shape, 0)) == iota(shape, 1), 1.0, 0.0).astype(jnp.bfloat16)
    unweave = jnp.where(phased(iota(shape, 1)) == iota(shape, 0), 1.0, 0.0).astype(jnp.bfloat16)
    edge = iota((16, SIDE), 0)
    edge = jnp.where(edge < 8, edge, SIDE + 7 - edge)
    edge_up = prolong_weights(edge, iota((16, SIDE), 1) & (HALF - 1))
    rim = iota((16, SIDE), 0)
    rim = jnp.where(rim < 8, rim, HALF + 7 - rim)
    rim_pick = jnp.where((iota((16, SIDE), 1) & (HALF - 1)) == rim, 1.0, 0.0).astype(jnp.bfloat16)
    edge_and_rim = jnp.concatenate([edge_up, rim_pick], axis=0)
    edge_pick = jnp.where(iota((16, SIDE), 1) == edge, 1.0, 0.0).astype(jnp.bfloat16)
    for buf in stages:
        for i in range(2):
            for c in range(3):
                for y in range(2):
                    for x in range(2):
                        buf[i, c, y, x, 0:PAD] = jnp.zeros((PAD, HALF), jnp.float32)
                        buf[i, c, y, x, PAD + HALF :] = jnp.zeros((PAD, HALF), jnp.float32)

    def face_copies():
        ends = [
            (face_data.at[pl.ds(3, 2)], face_data.at[pl.ds(1, 2)]),
            (face_data.at[pl.ds(3, 2)], face_data.at[pl.ds(5, 2)]),
            (face_data.at[4], face_data.at[0]),
            (face_data.at[3], face_data.at[7]),
        ]
        made = []
        for n, (src, dst) in enumerate(ends):
            made.append(
                pltpu.make_async_remote_copy(
                    src_ref=src,
                    dst_ref=dst,
                    send_sem=face_send.at[n],
                    recv_sem=face_recv.at[n],
                    device_id=(reach[n],),
                    device_id_type=MESH,
                )
            )
        return made

    def corner_copies():
        made = []
        for n, by in enumerate(steps):
            made.append(
                pltpu.make_async_remote_copy(
                    src_ref=corner_data.at[REACH, pl.ds(0, 4)],
                    dst_ref=corner_data.at[REACH - by, pl.ds(0, 4)],
                    send_sem=corner_send.at[n],
                    recv_sem=corner_recv.at[n],
                    device_id=(reach[n],),
                    device_id_type=MESH,
                )
            )
        return made

    def bulk_stage(i, s):
        src = stages[s]
        dst = stages[(s + 1) % 4] if s < 3 else s2_buf

        def step_rows(step, carry):
            r = pl.multiple_of(step * 8, 8)
            at = PAD + r
            here = pl.ds(at, 8)
            now = [[src[i, c, n // 2, n % 2, here, :] for n in range(4)] for c in range(3)]
            lap = [[None] * 4 for _ in range(3)]
            for c in range(3):
                for n in range(4):
                    y, x = n // 2, n % 2
                    beside = now[c][2 * y + 1 - x]
                    beyond = pltpu.roll(beside, HALF - 1 if x else 1, 1)
                    upright = now[c][2 * (1 - y) + x]
                    further = src[i, c, 1 - y, x, pl.ds(at + 2 * y - 1, 8), :]
                    lap[c][n] = (beside + beyond) + (upright + further) - 4.0 * now[c][n]
            for n in range(4):
                y, x = n // 2, n % 2
                rates = scaled_rates(
                    WEIGHTS[s],
                    *[now[c][n] for c in range(3)],
                    *[lap[c][n] for c in range(3)],
                    diffus_buf[i, y, x, pl.ds(r, 8), :],
                    growth_buf[i, y, x, pl.ds(r, 8), :],
                )
                for c in range(3):
                    base = now[c][n] if s == 0 else x_buf[i, c, y, x, here, :]
                    if s < 3:
                        value = base + rates[c]
                    else:
                        value = combine(
                            base,
                            s2_buf[i, c, y, x, here, :],
                            s3_buf[i, c, y, x, here, :],
                            now[c][n],
                            rates[c],
                        )
                    dst[i, c, y, x, here, :] = value
            return carry

        lax.fori_loop(0, HALF // 8, step_rows, 0, unroll=4)

    for load in loads + small:
        load.wait()
    parent = [parents_ref[i] % 4 for i in range(2)]
    edges = []
    for i in range(2):
        for c in range(3):
            block = quads[parent[i], c]
            across = dot_t(edge_and_rim, split(block, 1))
            along = dot(edge_and_rim, split(block, 0))
            edges += [across[0:16], along[0:16]]
            for f in range(4):
                rows = (across, along)[f // 2][16 + 8 * (f % 2) : 19 + 8 * (f % 2)]
                face_data[3 + i, f, 3 * c : 3 * c + 3, :] = rows
    edges = dot(split(jnp.concatenate(edges, axis=0), 1), columns_up).reshape(2, 3, 4, 8, SIDE)
    for c in range(3):
        t0[c] = jnp.concatenate([edges[0, c], edges[1, c]], axis=0)

    for i in range(2):
        for c in range(3):
            half_done = dot(split(quads[parent[i], c], 1), phases_across)
            fine = dot(phases_along, split(half_done, 0))
            for y in range(2):
                for x in range(2):
                    x_buf[i, c, y, x, PAD : PAD + HALF] = fine[
                        y * HALF : (y + 1) * HALF, x * HALF : (x + 1) * HALF
                    ]

    pl.semaphore_wait(barrier, sum(jnp.where(there, 1, 0) for there in exists))
    land_copy = pltpu.make_async_remote_copy(
        src_ref=land_ref.at[2 * (1 - parity)],
        dst_ref=land_far,
        send_sem=pair_send.at[0],
        recv_sem=pair_recv.at[0],
        device_id=(partner,),
        device_id_type=MESH,
    )
    land_copy.start()

    count = counts_ref[me]
    tables = (table_of(diff_ref), table_of(grow_ref))

    def rim_rates(i, classes):
        rims = jnp.concatenate([dot_t(edge_pick, classes), dot(edge_pick, classes)], axis=0)
        d, g = look_up(rims, tables)
        for f in range(4):
            rows = slice(8 * f, 8 * f + 8)
            strip_diffus[4 * i + f] = d[rows]
            strip_growth[4 * i + f] = g[rows]
            for a in range(3):
                for j in range(2):
                    at = 9 + 2 * a + j
                    row = 8 * f + a
                    face_data[3 + i, f, at : at + 1, :] = rims[
                        row : row + 1, j * HALF : (j + 1) * HALF
                    ]

    def bulk_rates(i, classes):
        classes = dot(classes, unweave).astype(jnp.bfloat16)
        for n in range(8):
            rows = slice(32 * n, 32 * n + 32)
            d, g = look_up(dot(weave[rows], classes), tables)
            y, m = n // 4, 32 * (n % 4)
            for x in range(2):
                diffus_buf[i, y, x, m : m + 32] = d[:, x * HALF : (x + 1) * HALF]
                growth_buf[i, y, x, m : m + 32] = g[:, x * HALF : (x + 1) * HALF]

    land_load.wait()
    classes = land[jnp.where(parity == 0, 0, jnp.clip(count - 1, 0, 2))]
    classes = classes.astype(jnp.float32).astype(jnp.bfloat16)
    rim_rates(parity, classes)
    bulk_rates(parity, classes)
    bulk_stage(parity, 0)

    land_copy.wait_recv()
    classes = jnp.where(
        count < 2, land_far[...], land[jnp.where(parity == 0, 1, jnp.clip(count - 2, 0, 2))]
    )
    classes = classes.astype(jnp.float32).astype(jnp.bfloat16)
    rim_rates(moving, classes)

    lane8, sub8 = iota((8, HALF), 1), iota((8, HALF), 0)
    for i in range(2):
        for x in range(2):
            row = jnp.zeros((8, HALF), jnp.float32)
            for q in range(5):
                pf = 4 * i + x
                strip_of = t0[q, pf] if q < 3 else (strip_diffus, strip_growth)[q - 3][pf]
                for y in range(2):
                    cell = lane8 - (64 * y + 9 * q + 3 * sub8)
                    inside = (cell >= 0) & (cell < 3) & (sub8 < 3)
                    cell = jnp.clip(cell, 0, 2)
                    cell = HALF - 1 - cell if y else cell
                    part = pick_lanes(strip_of[:, y * HALF : (y + 1) * HALF], cell)
                    row = row + jnp.where(inside, part, 0.0)
            at = 2 * i + x
            corner_data[REACH, at : at + 1, :] = jnp.sum(row, axis=0, keepdims=True)

    for n, copy in enumerate(face_copies()):
        pl.when(exists[n])(copy.start)
    for n, copy in enumerate(corner_copies()):
        pl.when(exists[n])(copy.start)

    bulk_rates(moving, classes)

    def cross(patch, face):
        value = nb_ref[face, patch]
        has = value >= 0
        return jnp.where(has, value, patch), jnp.where(has, face ^ 1, face)

    strip = (8, 8, SIDE)
    sub = iota(strip, 1)
    lane_half = iota((8, 8, HALF), 2)

    def gather_outer():
        first = [
            jnp.where(sub8 == 0, 1.0, jnp.where(sub8 == 1, 0.75, jnp.where(sub8 == 2, 0.25, 0.0))),
            jnp.where(sub8 == 0, 0.0, jnp.where(sub8 == 1, 0.25, 0.75)),
            jnp.where(sub8 >= 3, 0.25, 0.0),
        ]
        index = {}
        for kind in range(2):
            for e in range(2):
                b = jnp.minimum(lane8 if e else HALF - 1 - lane8, 2)
                a = jnp.minimum(sub8, 2)
                index[kind, e] = 3 * a + b if kind == 0 else 3 * b + a
        walls, classes = [], []
        for i in range(2):
            for f in range(4):
                patch, face = cross(2 * me + i, f)
                where = jnp.clip(patch - (2 * me - 3), 0, 7)
                for c in range(3):
                    parts = []
                    for a in range(3):
                        at = 3 * c + a
                        row = face_data[where, face, at : at + 1, :]
                        parts.append(first[a] * jnp.broadcast_to(row, (8, HALF)))
                    walls.append(parts[0] + parts[1] + parts[2])
                for j in range(2):
                    rows = []
                    for a in range(3):
                        at = 9 + 2 * a + j
                        rows.append(
                            jnp.broadcast_to(face_data[where, face, at : at + 1, :], (8, HALF))
                        )
                    classes.append(jnp.where(sub8 == 0, rows[0], jnp.where(sub8 == 1, rows[1], rows[2])))
        walls = dot(split(jnp.concatenate(walls, axis=0), 1), columns_up).reshape(8, 3, 8, SIDE)
        d, g = look_up(jnp.concatenate(classes, axis=0), tables)
        d, g = d.reshape(8, 2, 8, HALF), g.reshape(8, 2, 8, HALF)
        for c in range(3):
            h0[c, :, :, 0:SIDE] = walls[:, c]
        for j in range(2):
            at = slice(j * HALF, HALF + j * HALF)
            outer_diffus[:, :, at] = d[:, j]
            outer_growth[:, :, at] = g[:, j]

        low_half = lane8 < HALF // 2
        for i in range(2):
            for f in range(4):
                pf = 4 * i + f
                kind = f // 2
                start = cross(2 * me + i, f)
                chains = []
                for e in range(2):
                    patch, wall = start
                    side = 2 * (1 - kind) + e
                    chain = []
                    for step in range(3):
                        if step % 2 == 0:
                            patch, side = cross(patch, side)
                        else:
                            patch, wall = cross(patch, wall)
                        x = wall if kind == 0 else side
                        y = (side if kind == 0 else wall) - 2
                        window = jnp.clip((patch >> 1) - me + REACH, 0, 2 * REACH)
                        row = corner_data[window, pl.ds(2 * (patch & 1) + x, 1), :]
                        row = jnp.broadcast_to(row, (8, HALF))
                        chain.append(jnp.where(y == 1, pltpu.roll(row, 64, 1), row))
                    chains.append(chain)
                for step in range(3):
                    for q in range(5 if step < 2 else 3):
                        tiles = []
                        for e in range(2):
                            if step < 2:
                                at = index[kind, e] + 9 * q
                            else:
                                at = jnp.full((8, HALF), 9 * q, jnp.int32)
                            tiles.append(pick_lanes(chains[e][step], at))
                        if step < 2:
                            tile = jnp.where(low_half, tiles[1], tiles[0])
                        else:
                            tile = jnp.where(low_half, tiles[0], tiles[1])
                        if step == 0 and q < 3:
                            h0[q, pf, :, SIDE:] = tile
                        elif step == 0:
                            (outer_diffus, outer_growth)[q - 3][pf, :, SIDE:] = tile
                        elif step == 1 and q < 3:
                            l0[q, pf] = tile
                        elif step == 1:
                            (far_diffus, far_growth)[q - 3][pf] = tile
                        else:
                            k0[q, pf] = tile

    def rates_of(s, now, laps, diffus, growth):
        return scaled_rates(WEIGHTS[s], *now, *laps, diffus, growth)

    rising = iota((8, HALF), 0)
    falling = HALF - 1 - rising

    def strip_laplacian(now, beyond):
        ghost = jnp.broadcast_to(beyond[:, 0:1, :], strip)
        ends = []
        for e in range(2):
            columns = []
            for i in range(2):
                for f in range(4):
                    face = ghost[4 * i + (2 if f < 2 else 0) + e]
                    if f % 2:
                        columns.append(pick_lanes(face[:, HALF:], falling))
                    else:
                        columns.append(pick_lanes(face[:, :HALF], rising))
            ends.append(jnp.stack(columns, axis=0))
        above = jnp.where(sub == 0, ghost, pltpu.roll(now, 1, 1))
        below = pltpu.roll(now, 7, 1)
        rolled = pltpu.roll(now, 1, 2)
        left = jnp.where(lane_half == 0, ends[0], rolled[:, :, :HALF])
        left = jnp.concatenate([left, rolled[:, :, HALF:]], axis=2)
        rolled = pltpu.roll(now, SIDE - 1, 2)
        right = jnp.where(lane_half == HALF - 1, ends[1], rolled[:, :, HALF:])
        right = jnp.concatenate([rolled[:, :, :HALF], right], axis=2)
        return (left + right) + (below + above) - 4.0 * now

    def round_laplacian(now, facing):
        lanes = now.shape[2]
        above = jnp.where(iota(now.shape, 1) == 0, facing, pltpu.roll(now, 1, 1))
        below = pltpu.roll(now, 7, 1)
        sides = pltpu.roll(now, 1, 2) + pltpu.roll(now, lanes - 1, 2)
        return sides + (below + above) - 4.0 * now

    def strip_stage(s):
        inner = [strips[s][c] for c in range(3)]
        beyond = [outer[s][c, :, :, 0:SIDE] for c in range(3)]
        laps = [strip_laplacian(inner[c], beyond[c]) for c in range(3)]
        rates = rates_of(s, inner, laps, strip_diffus[...], strip_growth[...])
        if s == 3:
            for c in range(3):
                block = combine(t0[c], t1[c], t2[c], t3[c], rates[c])
                for i in range(2):
                    ring[i, c] = block[4 * i : 4 * i + 4]
                    for f in (1, 3):
                        for r in range(4):
                            ring[i, c, f, 7 - r : 8 - r, :] = block[4 * i + f, r : r + 1, :]
            return
        for c in range(3):
            strips[s + 1][c] = t0[c] + rates[c]
        if s == 2:
            laps = []
            for c in range(3):
                whole = outer[s][c]
                now = beyond[c]
                above = jnp.where(sub == 0, inner[c], pltpu.roll(now, 1, 1))
                sides = pltpu.roll(whole, 1, 2) + pltpu.roll(whole, SIDE + HALF - 1, 2)
                laps.append(sides[:, :, 0:SIDE] + (pltpu.roll(now, 7, 1) + above) - 4.0 * now)
            rates = rates_of(
                s, beyond, laps, outer_diffus[:, :, 0:SIDE], outer_growth[:, :, 0:SIDE]
            )
            for c in range(3):
                outer[3][c, :, :, 0:SIDE] = h0[c, :, :, 0:SIDE] + rates[c]
            return
        far = [(l0, l1)[s][c] for c in range(3)]
        now = [outer[s][c] for c in range(3)]
        laps = [
            round_laplacian(now[c], jnp.concatenate([inner[c], far[c]], axis=2)) for c in range(3)
        ]
        rates = rates_of(s, now, laps, outer_diffus[...], outer_growth[...])
        for c in range(3):
            outer[s + 1][c] = h0[c] + rates[c]
        if s == 0:
            laps = []
            for c in range(3):
                both = jnp.concatenate([far[c], k0[c]], axis=2)
                facing = jnp.concatenate([now[c][:, :, SIDE:], k0[c]], axis=2)
                laps.append(round_laplacian(both, facing)[:, :, :HALF])
            rates = rates_of(s, far, laps, far_diffus[...], far_growth[...])
            for c in range(3):
                l1[c] = far[c] + rates[c]

    def bulk_weave(i):
        for c in range(3):
            for y in range(2):
                both = jnp.concatenate(
                    [s2_buf[i, c, y, x, PAD : PAD + HALF, :] for x in range(2)], axis=1
                )
                high = both.astype(jnp.bfloat16)
                low = (both - high.astype(jnp.float32)).astype(jnp.bfloat16)
                woven = dot(high, weave) + dot(low, weave)
                for j in range(2):
                    result[i, c, j, pl.ds(y, HALF, stride=2), :] = woven[:, j * HALF : (j + 1) * HALF]

    def to_partner(n, src, dst):
        return pltpu.make_async_remote_copy(
            src_ref=src.at[moving],
            dst_ref=dst.at[2],
            send_sem=pair_send.at[n],
            recv_sem=pair_recv.at[n],
            device_id=(partner,),
            device_id_type=MESH,
        )

    result_copy = to_partner(1, result, result_out)
    ring_copy = to_partner(2, ring, ring_out)
    own_copies = [
        pltpu.make_async_copy(result.at[moving], result_out.at[moving], own_sem.at[0]),
        pltpu.make_async_copy(ring, ring_out.at[pl.ds(0, 2)], own_sem.at[1]),
        pltpu.make_async_copy(result.at[parity], result_out.at[parity], own_sem.at[2]),
    ]
    for s in range(4):
        bulk_stage(moving, s)
    bulk_weave(moving)
    result_copy.start()
    own_copies[0].start()
    bulk_stage(parity, 1)
    for n, copy in enumerate(face_copies()):
        pl.when(exists[n ^ 1])(copy.wait_recv)
    for n, copy in enumerate(corner_copies()):
        pl.when(exists[n ^ 1])(copy.wait_recv)
    gather_outer()
    for s in range(4):
        strip_stage(s)
    ring_copy.start()
    own_copies[1].start()
    for s in range(2, 4):
        bulk_stage(parity, s)
    bulk_weave(parity)
    own_copies[2].start()
    for n, copy in enumerate(face_copies()):
        pl.when(exists[n])(copy.wait_send)
    for n, copy in enumerate(corner_copies()):
        pl.when(exists[n])(copy.wait_send)
    land_copy.wait_send()
    for copy in own_copies:
        copy.wait()
    result_copy.wait()
    ring_copy.wait()


def merge_kernel(
    counts_hbm,
    result_hbm,
    ring_hbm,
    out_hbm,
    counts_ref,
    result,
    ring,
    zeros,
    count_sem,
    ring_sem,
    result_sem,
    out_sem,
    zero_sem,
):
    me = lax.axis_index("owner")
    even = me % 2 == 0
    count_copy = pltpu.make_async_copy(counts_hbm, counts_ref, count_sem)
    ring_copy = pltpu.make_async_copy(ring_hbm, ring, ring_sem)
    count_copy.start()
    ring_copy.start()

    def load(e, c):
        return pltpu.make_async_copy(result_hbm.at[e, c], result.at[e, c], result_sem.at[e, c])

    for e in range(3):
        for c in range(3):
            load(e, c).start()
    zeros[...] = jnp.zeros_like(zeros)
    count_copy.wait()
    count = counts_ref[me]
    empties = []
    for s in (1, 2):
        empties.append(pltpu.make_async_copy(zeros, out_hbm.at[s], zero_sem.at[s - 1]))
        pl.when(s >= count)(empties[-1].start)

    slots = []
    for e in range(3):
        slot = jnp.where(even, e, (e + 1) % 3 + count - 3)
        slots.append((slot, (slot >= 0) & (slot < count)))
    low_lanes = iota((8, HALF), 1) < 4
    high_lanes = iota((8, HALF), 1) >= HALF - 4
    sub_rows = iota((8, HALF), 0)
    ring_copy.wait()

    def stores(e, c):
        made = []
        for j in range(2):
            made.append(
                pltpu.make_async_copy(
                    result.at[e, c, j],
                    out_hbm.at[jnp.maximum(slots[e][0], 0), c, :, pl.ds(j * HALF, HALF)],
                    out_sem.at[e, c, j],
                )
            )
        return made

    for e in range(3):
        for c in range(3):
            gap = jnp.zeros((HALF - 16, SIDE), jnp.float32)
            block = jnp.concatenate([ring[e, c, 0], gap, ring[e, c, 1]], axis=0)
            sides = (block[:, :HALF].T, block[:, HALF:].T)
            load(e, c).wait()
            for j in range(2):
                lanes = high_lanes if j else low_lanes
                for t in range(SIDE // 8):
                    rows = slice(8 * t, 8 * t + 8)
                    within = slice(8 * t % HALF, 8 * t % HALF + 8)
                    value = jnp.where(lanes, sides[t // 16][within], result[e, c, j, rows, :])
                    if t == 0:
                        value = jnp.where(
                            sub_rows < 4, ring[e, c, 2, :, j * HALF : (j + 1) * HALF], value
                        )
                    if t == SIDE // 8 - 1:
                        value = jnp.where(
                            sub_rows >= 4, ring[e, c, 3, :, j * HALF : (j + 1) * HALF], value
                        )
                    result[e, c, j, rows, :] = value

            @pl.when(slots[e][1])
            def _(e=e, c=c):
                for copy in stores(e, c):
                    copy.start()

    for e in range(3):

        @pl.when(slots[e][1])
        def _(e=e):
            for c in range(3):
                for copy in stores(e, c):
                    copy.wait()

    for s in (1, 2):
        pl.when(s >= count)(empties[s - 1].wait)


def body(coarse, parents, new_counts, neighbours, land_cover, class_diffusivity, class_growth):
    owners = lax.axis_size("owner")
    f32 = jnp.float32
    hbm = pl.BlockSpec(memory_space=pltpu.HBM)
    stage_buf = pltpu.VMEM((2, 3, 2, 2, HALF + 2 * PAD, HALF), f32)
    strip_buf = pltpu.VMEM((3, 8, 8, SIDE), f32)
    outer_buf = pltpu.VMEM((3, 8, 8, SIDE + HALF), f32)
    far_buf = pltpu.VMEM((3, 8, 8, HALF), f32)
    results = jax.ShapeDtypeStruct((3, 3, 2, SIDE, HALF), f32)
    rings = jax.ShapeDtypeStruct((3, 3, 4, 8, SIDE), f32)
    whole, outer = pl.pallas_call(
        functools.partial(kernel, owners),
        out_shape=(results, rings),
        in_specs=[hbm] * 7,
        out_specs=(hbm, hbm),
        scratch_shapes=[
            pltpu.SMEM((2,), jnp.int32),
            pltpu.SMEM((owners,), jnp.int32),
            pltpu.SMEM((4, 2 * owners), jnp.int32),
            pltpu.SMEM((CLASSES,), f32),
            pltpu.SMEM((CLASSES,), f32),
            pltpu.VMEM((4, 3, HALF, HALF), f32),
            pltpu.VMEM((3, SIDE, SIDE), jnp.int32),
            pltpu.VMEM((SIDE, SIDE), jnp.int32),
            stage_buf,
            stage_buf,
            stage_buf,
            stage_buf,
            pltpu.VMEM((2, 2, 2, HALF, HALF), f32),
            pltpu.VMEM((2, 2, 2, HALF, HALF), f32),
            pltpu.VMEM((2, 3, 2, SIDE, HALF), f32),
            pltpu.VMEM((2, 3, 4, 8, SIDE), f32),
            strip_buf,
            strip_buf,
            strip_buf,
            strip_buf,
            pltpu.VMEM((8, 8, SIDE), f32),
            pltpu.VMEM((8, 8, SIDE), f32),
            pltpu.VMEM((8, 4, 16, HALF), f32),
            pltpu.VMEM((2 * REACH + 1, 8, HALF), f32),
            outer_buf,
            outer_buf,
            outer_buf,
            outer_buf,
            pltpu.VMEM((8, 8, SIDE + HALF), f32),
            pltpu.VMEM((8, 8, SIDE + HALF), f32),
            far_buf,
            far_buf,
            pltpu.VMEM((8, 8, HALF), f32),
            pltpu.VMEM((8, 8, HALF), f32),
            far_buf,
            pltpu.SemaphoreType.DMA((4,)),
            pltpu.SemaphoreType.DMA((5,)),
            pltpu.SemaphoreType.DMA,
            pltpu.SemaphoreType.DMA((4,)),
            pltpu.SemaphoreType.DMA((4,)),
            pltpu.SemaphoreType.DMA((2 * REACH,)),
            pltpu.SemaphoreType.DMA((2 * REACH,)),
            pltpu.SemaphoreType.DMA((3,)),
            pltpu.SemaphoreType.DMA((3,)),
            pltpu.SemaphoreType.DMA((3,)),
        ],
        compiler_params=pltpu.CompilerParams(
            collective_id=0, has_side_effects=True, vmem_limit_bytes=VMEM_LIMIT
        ),
        name="regrid_step",
    )(parents, new_counts, neighbours.T, class_diffusivity, class_growth, coarse, land_cover)
    return pl.pallas_call(
        merge_kernel,
        out_shape=jax.ShapeDtypeStruct((3, 3, SIDE, SIDE), f32),
        in_specs=[hbm] * 3,
        out_specs=hbm,
        scratch_shapes=[
            pltpu.SMEM((owners,), jnp.int32),
            pltpu.VMEM(results.shape, f32),
            pltpu.VMEM(rings.shape, f32),
            pltpu.VMEM((3, SIDE, SIDE), f32),
            pltpu.SemaphoreType.DMA,
            pltpu.SemaphoreType.DMA,
            pltpu.SemaphoreType.DMA((3, 3)),
            pltpu.SemaphoreType.DMA((3, 3, 2)),
            pltpu.SemaphoreType.DMA((2,)),
        ],
        compiler_params=pltpu.CompilerParams(vmem_limit_bytes=VMEM_LIMIT),
        name="merge_slots",
    )(new_counts, whole, outer)


def solution(mesh):
    return jax.shard_map(
        body,
        mesh=mesh,
        in_specs=(
            P("owner", None, None, None),
            P("owner"),
            P(),
            P(),
            P("owner", None, None),
            P(),
            P(),
        ),
        out_specs=P("owner", None, None, None),
        check_vma=False,
    )
```

```python
import functools

import jax
import jax.numpy as jnp
from jax import lax
from jax.experimental import pallas as pl
from jax.experimental.pallas import tpu as pltpu
from jax.sharding import PartitionSpec as P

SIDE = 256
HALF = 128
CLASSES = 11
PAD = 8
REACH = 6
VMEM_LIMIT = 62 * 1024 * 1024
WEIGHTS = (0.5, 0.5, 1.0, 1.0 / 6.0)
MESH = pl.DeviceIdType.MESH


def iota(shape, dim):
    return lax.broadcasted_iota(jnp.int32, shape, dim)


def phased(index):
    return 2 * (index & (HALF - 1)) + (index >> 7)


def prolong_weights(fine, coarse):
    near = fine >> 1
    second = jnp.clip(near + jnp.where((fine & 1) == 0, -1, 1), 0, HALF - 1)
    heavy = jnp.where(coarse == near, 0.75, 0.0)
    light = jnp.where(coarse == second, 0.25, 0.0)
    return (heavy + light).astype(jnp.bfloat16)


def split(block, axis):
    high = block.astype(jnp.bfloat16)
    low = (block - high.astype(jnp.float32)).astype(jnp.bfloat16)
    return jnp.concatenate([high, low], axis=axis)


def dot(a, b):
    return jnp.dot(a, b, preferred_element_type=jnp.float32)


def dot_t(a, b):
    return lax.dot_general(a, b, (((1,), (1,)), ((), ())), preferred_element_type=jnp.float32)


def table_of(ref):
    lane = iota((8, HALF), 1)
    table = jnp.zeros((8, HALF), jnp.float32)
    for number in range(CLASSES):
        table = jnp.where(lane == number, ref[number], table)
    return table


def pick_lanes(table, index):
    return jnp.take_along_axis(table, index, axis=1)


def look_up(classes, tables):
    index = classes.astype(jnp.int32)
    rows, columns = classes.shape
    found = []
    for table in tables:
        bands = []
        for r in range(0, rows, 8):
            blocks = [
                pick_lanes(table, index[r : r + 8, k : k + HALF]) for k in range(0, columns, HALF)
            ]
            bands.append(jnp.concatenate(blocks, axis=1))
        found.append(jnp.concatenate(bands, axis=0))
    return found


def scaled_rates(weight, x0, x1, x2, lap0, lap1, lap2, diffus, growth):
    dw = diffus * weight
    gw = growth * weight
    xw = x0 * weight
    r0 = dw * lap0 + (gw * x0) * (x1 - x0 - x2)
    r1 = (0.5 * dw) * lap1 + (0.4 * weight - x1 * (0.4 * weight + xw))
    r2 = dw * lap2 + (xw - (0.3 * weight) * x2)
    return r0, r1, r2


def combine(x, s2, s3, s4, rate):
    return (s2 + 2.0 * s3 + s4 - x) * (1.0 / 3.0) + rate


def kernel(
    owners,
    parents_hbm,
    counts_hbm,
    nb_hbm,
    diff_hbm,
    grow_hbm,
    coarse_ref,
    land_ref,
    result_out,
    ring_out,
    parents_ref,
    counts_ref,
    nb_ref,
    diff_ref,
    grow_ref,
    quads,
    land,
    x_buf,
    s2_buf,
    s3_buf,
    s4_buf,
    diffus_buf,
    growth_buf,
    result,
    ring,
    t0,
    t1,
    t2,
    t3,
    strip_diffus,
    strip_growth,
    face_data,
    corner_data,
    h0,
    h1,
    h2,
    h3,
    outer_diffus,
    outer_growth,
    l0,
    l1,
    far_diffus,
    far_growth,
    k0,
    load_sem,
    small_sem,
    land_sem,
    face_send,
    face_recv,
    corner_send,
    corner_recv,
    pair_send,
    pair_recv,
    own_sem,
):
    me = lax.axis_index("owner")
    parity = me % 2
    partner = me + 1 - 2 * parity
    moving = 1 - parity
    steps = [by for far in range(1, REACH + 1) for by in (far, -far)]
    reach = [(me + by) % owners for by in steps]
    exists = [(me + by < owners) & (me + by >= 0) for by in steps]
    stages = (x_buf, s2_buf, s3_buf, s4_buf)
    strips = (t0, t1, t2, t3)
    outer = (h0, h1, h2, h3)

    loads = []
    for q in range(4):
        block = coarse_ref.at[0, :, pl.ds((q // 2) * HALF, HALF), pl.ds((q % 2) * HALF, HALF)]
        loads.append(pltpu.make_async_copy(block, quads.at[q], load_sem.at[q]))
    for load in loads:
        load.start()
    small = []
    pairs = (
        (parents_hbm, parents_ref),
        (counts_hbm, counts_ref),
        (nb_hbm, nb_ref),
        (diff_hbm, diff_ref),
        (grow_hbm, grow_ref),
    )
    for n, (src, dst) in enumerate(pairs):
        small.append(pltpu.make_async_copy(src, dst, small_sem.at[n]))
        small[n].start()
    land_load = pltpu.make_async_copy(land_ref, land.at[pl.ds(0, 3)], land_sem)
    land_load.start()
    barrier = pltpu.get_barrier_semaphore()
    for n in range(len(steps)):

        @pl.when(exists[n])
        def _(n=n):
            pl.semaphore_signal(barrier, inc=1, device_id=(reach[n],), device_id_type=MESH)


    shape = (SIDE, SIDE)
    columns_up = prolong_weights(iota(shape, 1), iota(shape, 0) & (HALF - 1))
    phases_across = prolong_weights(phased(iota(shape, 1)), iota(shape, 0) & (HALF - 1))
    phases_along = prolong_weights(phased(iota(shape, 0)), iota(shape, 1) & (HALF - 1))
    weave = jnp.where(phased(iota(shape, 0)) == iota(shape, 1), 1.0, 0.0).astype(jnp.bfloat16)
    unweave = jnp.where(phased(iota(shape, 1)) == iota(shape, 0), 1.0, 0.0).astype(jnp.bfloat16)
    edge = iota((16, SIDE), 0)
    edge = jnp.where(edge < 8, edge, SIDE + 7 - edge)
    edge_up = prolong_weights(edge, iota((16, SIDE), 1) & (HALF - 1))
    rim = iota((16, SIDE), 0)
    rim = jnp.where(rim < 8, rim, HALF + 7 - rim)
    rim_pick = jnp.where((iota((16, SIDE), 1) & (HALF - 1)) == rim, 1.0, 0.0).astype(jnp.bfloat16)
    edge_and_rim = jnp.concatenate([edge_up, rim_pick], axis=0)
    edge_pick = jnp.where(iota((16, SIDE), 1) == edge, 1.0, 0.0).astype(jnp.bfloat16)
    for buf in stages:
        for i in range(2):
            for c in range(3):
                for y in range(2):
                    for x in range(2):
                        buf[i, c, y, x, 0:PAD] = jnp.zeros((PAD, HALF), jnp.float32)
                        buf[i, c, y, x, PAD + HALF :] = jnp.zeros((PAD, HALF), jnp.float32)

    def face_copies():
        ends = [
            (face_data.at[pl.ds(3, 2)], face_data.at[pl.ds(1, 2)]),
            (face_data.at[pl.ds(3, 2)], face_data.at[pl.ds(5, 2)]),
            (face_data.at[4], face_data.at[0]),
            (face_data.at[3], face_data.at[7]),
        ]
        made = []
        for n, (src, dst) in enumerate(ends):
            made.append(
                pltpu.make_async_remote_copy(
                    src_ref=src,
                    dst_ref=dst,
                    send_sem=face_send.at[n],
                    recv_sem=face_recv.at[n],
                    device_id=(reach[n],),
                    device_id_type=MESH,
                )
            )
        return made

    def corner_copies():
        made = []
        for n, by in enumerate(steps):
            made.append(
                pltpu.make_async_remote_copy(
                    src_ref=corner_data.at[REACH, pl.ds(0, 4)],
                    dst_ref=corner_data.at[REACH - by, pl.ds(0, 4)],
                    send_sem=corner_send.at[n],
                    recv_sem=corner_recv.at[n],
                    device_id=(reach[n],),
                    device_id_type=MESH,
                )
            )
        return made

    pl.semaphore_wait(barrier, sum(jnp.where(there, 1, 0) for there in exists))
    land_copy = pltpu.make_async_remote_copy(
        src_ref=land_ref.at[2 * (1 - parity)],
        dst_ref=land.at[3],
        send_sem=pair_send.at[0],
        recv_sem=pair_recv.at[0],
        device_id=(partner,),
        device_id_type=MESH,
    )
    land_copy.start()

    for load in loads + small:
        load.wait()
    parent = [parents_ref[i] % 4 for i in range(2)]
    edges = []
    for i in range(2):
        for c in range(3):
            block = quads[parent[i], c]
            across = dot_t(edge_and_rim, split(block, 1))
            along = dot(edge_and_rim, split(block, 0))
            edges += [across[0:16], along[0:16]]
            for f in range(4):
                rows = (across, along)[f // 2][16 + 8 * (f % 2) : 19 + 8 * (f % 2)]
                face_data[3 + i, f, 3 * c : 3 * c + 3, :] = rows
    edges = dot(split(jnp.concatenate(edges, axis=0), 1), columns_up).reshape(2, 3, 4, 8, SIDE)
    for c in range(3):
        t0[c] = jnp.concatenate([edges[0, c], edges[1, c]], axis=0)

    for i in range(2):
        for c in range(3):
            half_done = dot(split(quads[parent[i], c], 1), phases_across)
            fine = dot(phases_along, split(half_done, 0))
            for y in range(2):
                for x in range(2):
                    x_buf[i, c, y, x, PAD : PAD + HALF] = fine[
                        y * HALF : (y + 1) * HALF, x * HALF : (x + 1) * HALF
                    ]

    land_load.wait()
    land_copy.wait_recv()
    count = counts_ref[me]
    slots = []
    for i in range(2):
        even_slot = jnp.where(i >= count, 3, i)
        odd_slot = jnp.where(i - 2 + count < 0, 3, i - 2 + count)
        slots.append(jnp.where(parity == 0, even_slot, odd_slot))
    tables = (table_of(diff_ref), table_of(grow_ref))
    classes_of = []
    for i in range(2):
        classes = land[slots[i]].astype(jnp.float32).astype(jnp.bfloat16)
        classes_of.append(classes)
        rims = jnp.concatenate([dot_t(edge_pick, classes), dot(edge_pick, classes)], axis=0)
        d, g = look_up(rims, tables)
        for f in range(4):
            rows = slice(8 * f, 8 * f + 8)
            strip_diffus[4 * i + f] = d[rows]
            strip_growth[4 * i + f] = g[rows]
            for a in range(3):
                for j in range(2):
                    at = 9 + 2 * a + j
                    row = 8 * f + a
                    face_data[3 + i, f, at : at + 1, :] = rims[
                        row : row + 1, j * HALF : (j + 1) * HALF
                    ]

    lane8, sub8 = iota((8, HALF), 1), iota((8, HALF), 0)
    for i in range(2):
        for x in range(2):
            row = jnp.zeros((8, HALF), jnp.float32)
            for q in range(5):
                pf = 4 * i + x
                strip_of = t0[q, pf] if q < 3 else (strip_diffus, strip_growth)[q - 3][pf]
                for y in range(2):
                    cell = lane8 - (64 * y + 9 * q + 3 * sub8)
                    inside = (cell >= 0) & (cell < 3) & (sub8 < 3)
                    cell = jnp.clip(cell, 0, 2)
                    cell = HALF - 1 - cell if y else cell
                    part = pick_lanes(strip_of[:, y * HALF : (y + 1) * HALF], cell)
                    row = row + jnp.where(inside, part, 0.0)
            at = 2 * i + x
            corner_data[REACH, at : at + 1, :] = jnp.sum(row, axis=0, keepdims=True)

    for n, copy in enumerate(face_copies()):
        pl.when(exists[n])(copy.start)
    for n, copy in enumerate(corner_copies()):
        pl.when(exists[n])(copy.start)

    for i in range(2):
        classes = dot(classes_of[i], unweave).astype(jnp.bfloat16)
        for n in range(8):
            rows = slice(32 * n, 32 * n + 32)
            d, g = look_up(dot(weave[rows], classes), tables)
            y, m = n // 4, 32 * (n % 4)
            for x in range(2):
                diffus_buf[i, y, x, m : m + 32] = d[:, x * HALF : (x + 1) * HALF]
                growth_buf[i, y, x, m : m + 32] = g[:, x * HALF : (x + 1) * HALF]

    def cross(patch, face):
        value = nb_ref[face, patch]
        has = value >= 0
        return jnp.where(has, value, patch), jnp.where(has, face ^ 1, face)

    strip = (8, 8, SIDE)
    sub = iota(strip, 1)
    lane_half = iota((8, 8, HALF), 2)

    def gather_outer():
        first = [
            jnp.where(sub8 == 0, 1.0, jnp.where(sub8 == 1, 0.75, jnp.where(sub8 == 2, 0.25, 0.0))),
            jnp.where(sub8 == 0, 0.0, jnp.where(sub8 == 1, 0.25, 0.75)),
            jnp.where(sub8 >= 3, 0.25, 0.0),
        ]
        index = {}
        for kind in range(2):
            for e in range(2):
                b = jnp.minimum(lane8 if e else HALF - 1 - lane8, 2)
                a = jnp.minimum(sub8, 2)
                index[kind, e] = 3 * a + b if kind == 0 else 3 * b + a
        walls, classes = [], []
        for i in range(2):
            for f in range(4):
                patch, face = cross(2 * me + i, f)
                where = jnp.clip(patch - (2 * me - 3), 0, 7)
                for c in range(3):
                    parts = []
                    for a in range(3):
                        at = 3 * c + a
                        row = face_data[where, face, at : at + 1, :]
                        parts.append(first[a] * jnp.broadcast_to(row, (8, HALF)))
                    walls.append(parts[0] + parts[1] + parts[2])
                for j in range(2):
                    rows = []
                    for a in range(3):
                        at = 9 + 2 * a + j
                        rows.append(
                            jnp.broadcast_to(face_data[where, face, at : at + 1, :], (8, HALF))
                        )
                    classes.append(jnp.where(sub8 == 0, rows[0], jnp.where(sub8 == 1, rows[1], rows[2])))
        walls = dot(split(jnp.concatenate(walls, axis=0), 1), columns_up).reshape(8, 3, 8, SIDE)
        d, g = look_up(jnp.concatenate(classes, axis=0), tables)
        d, g = d.reshape(8, 2, 8, HALF), g.reshape(8, 2, 8, HALF)
        for c in range(3):
            h0[c, :, :, 0:SIDE] = walls[:, c]
        for j in range(2):
            at = slice(j * HALF, HALF + j * HALF)
            outer_diffus[:, :, at] = d[:, j]
            outer_growth[:, :, at] = g[:, j]

        low_half = lane8 < HALF // 2
        for i in range(2):
            for f in range(4):
                pf = 4 * i + f
                kind = f // 2
                start = cross(2 * me + i, f)
                chains = []
                for e in range(2):
                    patch, wall = start
                    side = 2 * (1 - kind) + e
                    chain = []
                    for step in range(3):
                        if step % 2 == 0:
                            patch, side = cross(patch, side)
                        else:
                            patch, wall = cross(patch, wall)
                        x = wall if kind == 0 else side
                        y = (side if kind == 0 else wall) - 2
                        window = jnp.clip((patch >> 1) - me + REACH, 0, 2 * REACH)
                        row = corner_data[window, pl.ds(2 * (patch & 1) + x, 1), :]
                        row = jnp.broadcast_to(row, (8, HALF))
                        chain.append(jnp.where(y == 1, pltpu.roll(row, 64, 1), row))
                    chains.append(chain)
                for step in range(3):
                    for q in range(5 if step < 2 else 3):
                        tiles = []
                        for e in range(2):
                            if step < 2:
                                at = index[kind, e] + 9 * q
                            else:
                                at = jnp.full((8, HALF), 9 * q, jnp.int32)
                            tiles.append(pick_lanes(chains[e][step], at))
                        if step < 2:
                            tile = jnp.where(low_half, tiles[1], tiles[0])
                        else:
                            tile = jnp.where(low_half, tiles[0], tiles[1])
                        if step == 0 and q < 3:
                            h0[q, pf, :, SIDE:] = tile
                        elif step == 0:
                            (outer_diffus, outer_growth)[q - 3][pf, :, SIDE:] = tile
                        elif step == 1 and q < 3:
                            l0[q, pf] = tile
                        elif step == 1:
                            (far_diffus, far_growth)[q - 3][pf] = tile
                        else:
                            k0[q, pf] = tile

    def rates_of(s, now, laps, diffus, growth):
        return scaled_rates(WEIGHTS[s], *now, *laps, diffus, growth)

    rising = iota((8, HALF), 0)
    falling = HALF - 1 - rising

    def strip_laplacian(now, beyond):
        ghost = jnp.broadcast_to(beyond[:, 0:1, :], strip)
        ends = []
        for e in range(2):
            columns = []
            for i in range(2):
                for f in range(4):
                    face = ghost[4 * i + (2 if f < 2 else 0) + e]
                    if f % 2:
                        columns.append(pick_lanes(face[:, HALF:], falling))
                    else:
                        columns.append(pick_lanes(face[:, :HALF], rising))
            ends.append(jnp.stack(columns, axis=0))
        above = jnp.where(sub == 0, ghost, pltpu.roll(now, 1, 1))
        below = pltpu.roll(now, 7, 1)
        rolled = pltpu.roll(now, 1, 2)
        left = jnp.where(lane_half == 0, ends[0], rolled[:, :, :HALF])
        left = jnp.concatenate([left, rolled[:, :, HALF:]], axis=2)
        rolled = pltpu.roll(now, SIDE - 1, 2)
        right = jnp.where(lane_half == HALF - 1, ends[1], rolled[:, :, HALF:])
        right = jnp.concatenate([rolled[:, :, :HALF], right], axis=2)
        return (left + right) + (below + above) - 4.0 * now

    def round_laplacian(now, facing):
        lanes = now.shape[2]
        above = jnp.where(iota(now.shape, 1) == 0, facing, pltpu.roll(now, 1, 1))
        below = pltpu.roll(now, 7, 1)
        sides = pltpu.roll(now, 1, 2) + pltpu.roll(now, lanes - 1, 2)
        return sides + (below + above) - 4.0 * now

    def strip_stage(s):
        inner = [strips[s][c] for c in range(3)]
        beyond = [outer[s][c, :, :, 0:SIDE] for c in range(3)]
        laps = [strip_laplacian(inner[c], beyond[c]) for c in range(3)]
        rates = rates_of(s, inner, laps, strip_diffus[...], strip_growth[...])
        if s == 3:
            for c in range(3):
                block = combine(t0[c], t1[c], t2[c], t3[c], rates[c])
                for i in range(2):
                    ring[i, c] = block[4 * i : 4 * i + 4]
                    for f in (1, 3):
                        for r in range(4):
                            ring[i, c, f, 7 - r : 8 - r, :] = block[4 * i + f, r : r + 1, :]
            return
        for c in range(3):
            strips[s + 1][c] = t0[c] + rates[c]
        if s == 2:
            laps = []
            for c in range(3):
                whole = outer[s][c]
                now = beyond[c]
                above = jnp.where(sub == 0, inner[c], pltpu.roll(now, 1, 1))
                sides = pltpu.roll(whole, 1, 2) + pltpu.roll(whole, SIDE + HALF - 1, 2)
                laps.append(sides[:, :, 0:SIDE] + (pltpu.roll(now, 7, 1) + above) - 4.0 * now)
            rates = rates_of(
                s, beyond, laps, outer_diffus[:, :, 0:SIDE], outer_growth[:, :, 0:SIDE]
            )
            for c in range(3):
                outer[3][c, :, :, 0:SIDE] = h0[c, :, :, 0:SIDE] + rates[c]
            return
        far = [(l0, l1)[s][c] for c in range(3)]
        now = [outer[s][c] for c in range(3)]
        laps = [
            round_laplacian(now[c], jnp.concatenate([inner[c], far[c]], axis=2)) for c in range(3)
        ]
        rates = rates_of(s, now, laps, outer_diffus[...], outer_growth[...])
        for c in range(3):
            outer[s + 1][c] = h0[c] + rates[c]
        if s == 0:
            laps = []
            for c in range(3):
                both = jnp.concatenate([far[c], k0[c]], axis=2)
                facing = jnp.concatenate([now[c][:, :, SIDE:], k0[c]], axis=2)
                laps.append(round_laplacian(both, facing)[:, :, :HALF])
            rates = rates_of(s, far, laps, far_diffus[...], far_growth[...])
            for c in range(3):
                l1[c] = far[c] + rates[c]

    def bulk_stage(i, s):
        src = stages[s]
        dst = stages[(s + 1) % 4] if s < 3 else s2_buf

        def step_rows(step, carry):
            r = pl.multiple_of(step * 8, 8)
            at = PAD + r
            here = pl.ds(at, 8)
            now = [[src[i, c, n // 2, n % 2, here, :] for n in range(4)] for c in range(3)]
            lap = [[None] * 4 for _ in range(3)]
            for c in range(3):
                for n in range(4):
                    y, x = n // 2, n % 2
                    beside = now[c][2 * y + 1 - x]
                    beyond = pltpu.roll(beside, HALF - 1 if x else 1, 1)
                    upright = now[c][2 * (1 - y) + x]
                    further = src[i, c, 1 - y, x, pl.ds(at + 2 * y - 1, 8), :]
                    lap[c][n] = (beside + beyond) + (upright + further) - 4.0 * now[c][n]
            for n in range(4):
                y, x = n // 2, n % 2
                rates = scaled_rates(
                    WEIGHTS[s],
                    *[now[c][n] for c in range(3)],
                    *[lap[c][n] for c in range(3)],
                    diffus_buf[i, y, x, pl.ds(r, 8), :],
                    growth_buf[i, y, x, pl.ds(r, 8), :],
                )
                for c in range(3):
                    base = now[c][n] if s == 0 else x_buf[i, c, y, x, here, :]
                    if s < 3:
                        value = base + rates[c]
                    else:
                        value = combine(
                            base,
                            s2_buf[i, c, y, x, here, :],
                            s3_buf[i, c, y, x, here, :],
                            now[c][n],
                            rates[c],
                        )
                    dst[i, c, y, x, here, :] = value
            return carry

        lax.fori_loop(0, HALF // 8, step_rows, 0, unroll=8)

    def bulk_weave(i):
        for c in range(3):
            for y in range(2):
                both = jnp.concatenate(
                    [s2_buf[i, c, y, x, PAD : PAD + HALF, :] for x in range(2)], axis=1
                )
                high = both.astype(jnp.bfloat16)
                low = (both - high.astype(jnp.float32)).astype(jnp.bfloat16)
                woven = dot(high, weave) + dot(low, weave)
                for j in range(2):
                    result[i, c, j, pl.ds(y, HALF, stride=2), :] = woven[:, j * HALF : (j + 1) * HALF]

    def to_partner(n, src, dst):
        return pltpu.make_async_remote_copy(
            src_ref=src.at[moving],
            dst_ref=dst.at[2],
            send_sem=pair_send.at[n],
            recv_sem=pair_recv.at[n],
            device_id=(partner,),
            device_id_type=MESH,
        )

    result_copy = to_partner(1, result, result_out)
    ring_copy = to_partner(2, ring, ring_out)
    own_copies = [
        pltpu.make_async_copy(result.at[moving], result_out.at[moving], own_sem.at[0]),
        pltpu.make_async_copy(ring, ring_out.at[pl.ds(0, 2)], own_sem.at[1]),
        pltpu.make_async_copy(result.at[parity], result_out.at[parity], own_sem.at[2]),
    ]
    for s in range(4):
        bulk_stage(moving, s)
    bulk_weave(moving)
    result_copy.start()
    own_copies[0].start()
    for s in range(4):
        bulk_stage(parity, s)
    for n, copy in enumerate(face_copies()):
        pl.when(exists[n ^ 1])(copy.wait_recv)
    for n, copy in enumerate(corner_copies()):
        pl.when(exists[n ^ 1])(copy.wait_recv)
    gather_outer()
    for s in range(4):
        strip_stage(s)
    ring_copy.start()
    own_copies[1].start()
    bulk_weave(parity)
    own_copies[2].start()
    for n, copy in enumerate(face_copies()):
        pl.when(exists[n])(copy.wait_send)
    for n, copy in enumerate(corner_copies()):
        pl.when(exists[n])(copy.wait_send)
    land_copy.wait_send()
    for copy in own_copies:
        copy.wait()
    result_copy.wait()
    ring_copy.wait()


def merge_kernel(
    counts_hbm,
    result_hbm,
    ring_hbm,
    out_hbm,
    counts_ref,
    result,
    ring,
    zeros,
    count_sem,
    ring_sem,
    result_sem,
    out_sem,
    zero_sem,
):
    me = lax.axis_index("owner")
    even = me % 2 == 0
    count_copy = pltpu.make_async_copy(counts_hbm, counts_ref, count_sem)
    ring_copy = pltpu.make_async_copy(ring_hbm, ring, ring_sem)
    count_copy.start()
    ring_copy.start()

    def load(e, c):
        return pltpu.make_async_copy(result_hbm.at[e, c], result.at[e, c], result_sem.at[e, c])

    for e in range(3):
        for c in range(3):
            load(e, c).start()
    zeros[...] = jnp.zeros_like(zeros)
    count_copy.wait()
    count = counts_ref[me]
    empties = []
    for s in (1, 2):
        empties.append(pltpu.make_async_copy(zeros, out_hbm.at[s], zero_sem.at[s - 1]))
        pl.when(s >= count)(empties[-1].start)

    slots = []
    for e in range(3):
        slot = jnp.where(even, e, (e + 1) % 3 + count - 3)
        slots.append((slot, (slot >= 0) & (slot < count)))
    low_lanes = iota((8, HALF), 1) < 4
    high_lanes = iota((8, HALF), 1) >= HALF - 4
    sub_rows = iota((8, HALF), 0)
    ring_copy.wait()

    def stores(e, c):
        made = []
        for j in range(2):
            made.append(
                pltpu.make_async_copy(
                    result.at[e, c, j],
                    out_hbm.at[jnp.maximum(slots[e][0], 0), c, :, pl.ds(j * HALF, HALF)],
                    out_sem.at[e, c, j],
                )
            )
        return made

    for e in range(3):
        for c in range(3):
            gap = jnp.zeros((HALF - 16, SIDE), jnp.float32)
            block = jnp.concatenate([ring[e, c, 0], gap, ring[e, c, 1]], axis=0)
            sides = (block[:, :HALF].T, block[:, HALF:].T)
            load(e, c).wait()
            for j in range(2):
                lanes = high_lanes if j else low_lanes
                for t in range(SIDE // 8):
                    rows = slice(8 * t, 8 * t + 8)
                    within = slice(8 * t % HALF, 8 * t % HALF + 8)
                    value = jnp.where(lanes, sides[t // 16][within], result[e, c, j, rows, :])
                    if t == 0:
                        value = jnp.where(
                            sub_rows < 4, ring[e, c, 2, :, j * HALF : (j + 1) * HALF], value
                        )
                    if t == SIDE // 8 - 1:
                        value = jnp.where(
                            sub_rows >= 4, ring[e, c, 3, :, j * HALF : (j + 1) * HALF], value
                        )
                    result[e, c, j, rows, :] = value

            @pl.when(slots[e][1])
            def _(e=e, c=c):
                for copy in stores(e, c):
                    copy.start()

    for e in range(3):

        @pl.when(slots[e][1])
        def _(e=e):
            for c in range(3):
                for copy in stores(e, c):
                    copy.wait()

    for s in (1, 2):
        pl.when(s >= count)(empties[s - 1].wait)


def body(coarse, parents, new_counts, neighbours, land_cover, class_diffusivity, class_growth):
    owners = lax.axis_size("owner")
    f32 = jnp.float32
    hbm = pl.BlockSpec(memory_space=pltpu.HBM)
    stage_buf = pltpu.VMEM((2, 3, 2, 2, HALF + 2 * PAD, HALF), f32)
    strip_buf = pltpu.VMEM((3, 8, 8, SIDE), f32)
    outer_buf = pltpu.VMEM((3, 8, 8, SIDE + HALF), f32)
    far_buf = pltpu.VMEM((3, 8, 8, HALF), f32)
    results = jax.ShapeDtypeStruct((3, 3, 2, SIDE, HALF), f32)
    rings = jax.ShapeDtypeStruct((3, 3, 4, 8, SIDE), f32)
    whole, outer = pl.pallas_call(
        functools.partial(kernel, owners),
        out_shape=(results, rings),
        in_specs=[hbm] * 7,
        out_specs=(hbm, hbm),
        scratch_shapes=[
            pltpu.SMEM((2,), jnp.int32),
            pltpu.SMEM((owners,), jnp.int32),
            pltpu.SMEM((4, 2 * owners), jnp.int32),
            pltpu.SMEM((CLASSES,), f32),
            pltpu.SMEM((CLASSES,), f32),
            pltpu.VMEM((4, 3, HALF, HALF), f32),
            pltpu.VMEM((4, SIDE, SIDE), jnp.int32),
            stage_buf,
            stage_buf,
            stage_buf,
            stage_buf,
            pltpu.VMEM((2, 2, 2, HALF, HALF), f32),
            pltpu.VMEM((2, 2, 2, HALF, HALF), f32),
            pltpu.VMEM((2, 3, 2, SIDE, HALF), f32),
            pltpu.VMEM((2, 3, 4, 8, SIDE), f32),
            strip_buf,
            strip_buf,
            strip_buf,
            strip_buf,
            pltpu.VMEM((8, 8, SIDE), f32),
            pltpu.VMEM((8, 8, SIDE), f32),
            pltpu.VMEM((8, 4, 16, HALF), f32),
            pltpu.VMEM((2 * REACH + 1, 8, HALF), f32),
            outer_buf,
            outer_buf,
            outer_buf,
            outer_buf,
            pltpu.VMEM((8, 8, SIDE + HALF), f32),
            pltpu.VMEM((8, 8, SIDE + HALF), f32),
            far_buf,
            far_buf,
            pltpu.VMEM((8, 8, HALF), f32),
            pltpu.VMEM((8, 8, HALF), f32),
            far_buf,
            pltpu.SemaphoreType.DMA((4,)),
            pltpu.SemaphoreType.DMA((5,)),
            pltpu.SemaphoreType.DMA,
            pltpu.SemaphoreType.DMA((4,)),
            pltpu.SemaphoreType.DMA((4,)),
            pltpu.SemaphoreType.DMA((2 * REACH,)),
            pltpu.SemaphoreType.DMA((2 * REACH,)),
            pltpu.SemaphoreType.DMA((3,)),
            pltpu.SemaphoreType.DMA((3,)),
            pltpu.SemaphoreType.DMA((3,)),
        ],
        compiler_params=pltpu.CompilerParams(
            collective_id=0, has_side_effects=True, vmem_limit_bytes=VMEM_LIMIT
        ),
        name="regrid_step",
    )(parents, new_counts, neighbours.T, class_diffusivity, class_growth, coarse, land_cover)
    return pl.pallas_call(
        merge_kernel,
        out_shape=jax.ShapeDtypeStruct((3, 3, SIDE, SIDE), f32),
        in_specs=[hbm] * 3,
        out_specs=hbm,
        scratch_shapes=[
            pltpu.SMEM((owners,), jnp.int32),
            pltpu.VMEM(results.shape, f32),
            pltpu.VMEM(rings.shape, f32),
            pltpu.VMEM((3, SIDE, SIDE), f32),
            pltpu.SemaphoreType.DMA,
            pltpu.SemaphoreType.DMA,
            pltpu.SemaphoreType.DMA((3, 3)),
            pltpu.SemaphoreType.DMA((3, 3, 2)),
            pltpu.SemaphoreType.DMA((2,)),
        ],
        compiler_params=pltpu.CompilerParams(vmem_limit_bytes=VMEM_LIMIT),
        name="merge_slots",
    )(new_counts, whole, outer)


def solution(mesh):
    return jax.shard_map(
        body,
        mesh=mesh,
        in_specs=(
            P("owner", None, None, None),
            P("owner"),
            P(),
            P(),
            P("owner", None, None),
            P(),
            P(),
        ),
        out_specs=P("owner", None, None, None),
        check_vma=False,
    )
```

```python
import functools

import jax
import jax.numpy as jnp
from jax import lax
from jax.experimental import pallas as pl
from jax.experimental.pallas import tpu as pltpu
from jax.sharding import PartitionSpec as P

SIDE = 256
HALF = 128
CLASSES = 11
PAD = 8
REACH = 6
VMEM_LIMIT = 62 * 1024 * 1024
WEIGHTS = (0.5, 0.5, 1.0, 1.0 / 6.0)
MESH = pl.DeviceIdType.MESH


def iota(shape, dim):
    return lax.broadcasted_iota(jnp.int32, shape, dim)


def phased(index):
    return 2 * (index & (HALF - 1)) + (index >> 7)


def prolong_weights(fine, coarse):
    near = fine >> 1
    second = jnp.clip(near + jnp.where((fine & 1) == 0, -1, 1), 0, HALF - 1)
    heavy = jnp.where(coarse == near, 0.75, 0.0)
    light = jnp.where(coarse == second, 0.25, 0.0)
    return (heavy + light).astype(jnp.bfloat16)


def split(block, axis):
    high = block.astype(jnp.bfloat16)
    low = (block - high.astype(jnp.float32)).astype(jnp.bfloat16)
    return jnp.concatenate([high, low], axis=axis)


def dot(a, b):
    return jnp.dot(a, b, preferred_element_type=jnp.float32)


def dot_t(a, b):
    return lax.dot_general(a, b, (((1,), (1,)), ((), ())), preferred_element_type=jnp.float32)


def table_of(ref):
    lane = iota((8, HALF), 1)
    table = jnp.zeros((8, HALF), jnp.float32)
    for number in range(CLASSES):
        table = jnp.where(lane == number, ref[number], table)
    return table


def pick_lanes(table, index):
    return jnp.take_along_axis(table, index, axis=1)


def look_up(classes, tables):
    index = classes.astype(jnp.int32)
    rows, columns = classes.shape
    found = []
    for table in tables:
        bands = []
        for r in range(0, rows, 8):
            blocks = [
                pick_lanes(table, index[r : r + 8, k : k + HALF]) for k in range(0, columns, HALF)
            ]
            bands.append(jnp.concatenate(blocks, axis=1))
        found.append(jnp.concatenate(bands, axis=0))
    return found


def scaled_rates(weight, x0, x1, x2, lap0, lap1, lap2, diffus, growth):
    dw = diffus * weight
    gw = growth * weight
    xw = x0 * weight
    r0 = dw * lap0 + (gw * x0) * (x1 - x0 - x2)
    r1 = (0.5 * dw) * lap1 + (0.4 * weight - x1 * (0.4 * weight + xw))
    r2 = dw * lap2 + (xw - (0.3 * weight) * x2)
    return r0, r1, r2


def combine(x, s2, s3, s4, rate):
    return (s2 + 2.0 * s3 + s4 - x) * (1.0 / 3.0) + rate


def kernel(
    owners,
    parents_hbm,
    counts_hbm,
    nb_hbm,
    diff_hbm,
    grow_hbm,
    coarse_ref,
    land_ref,
    result_out,
    ring_out,
    parents_ref,
    counts_ref,
    nb_ref,
    diff_ref,
    grow_ref,
    quads,
    land,
    x_buf,
    s2_buf,
    s3_buf,
    s4_buf,
    diffus_buf,
    growth_buf,
    result,
    ring,
    t0,
    t1,
    t2,
    t3,
    strip_diffus,
    strip_growth,
    face_data,
    corner_data,
    h0,
    h1,
    h2,
    h3,
    outer_diffus,
    outer_growth,
    l0,
    l1,
    far_diffus,
    far_growth,
    k0,
    load_sem,
    small_sem,
    land_sem,
    face_send,
    face_recv,
    corner_send,
    corner_recv,
    pair_send,
    pair_recv,
    own_sem,
):
    me = lax.axis_index("owner")
    parity = me % 2
    partner = me + 1 - 2 * parity
    moving = 1 - parity
    steps = [by for far in range(1, REACH + 1) for by in (far, -far)]
    reach = [(me + by) % owners for by in steps]
    exists = [(me + by < owners) & (me + by >= 0) for by in steps]
    stages = (x_buf, s2_buf, s3_buf, s4_buf)
    strips = (t0, t1, t2, t3)
    outer = (h0, h1, h2, h3)

    loads = []
    for q in range(4):
        block = coarse_ref.at[0, :, pl.ds((q // 2) * HALF, HALF), pl.ds((q % 2) * HALF, HALF)]
        loads.append(pltpu.make_async_copy(block, quads.at[q], load_sem.at[q]))
    for load in loads:
        load.start()
    small = []
    pairs = (
        (parents_hbm, parents_ref),
        (counts_hbm, counts_ref),
        (nb_hbm, nb_ref),
        (diff_hbm, diff_ref),
        (grow_hbm, grow_ref),
    )
    for n, (src, dst) in enumerate(pairs):
        small.append(pltpu.make_async_copy(src, dst, small_sem.at[n]))
        small[n].start()
    land_load = pltpu.make_async_copy(land_ref, land.at[pl.ds(0, 3)], land_sem)
    land_load.start()
    barrier = pltpu.get_barrier_semaphore()
    for n in range(len(steps)):

        @pl.when(exists[n])
        def _(n=n):
            pl.semaphore_signal(barrier, inc=1, device_id=(reach[n],), device_id_type=MESH)


    shape = (SIDE, SIDE)
    columns_up = prolong_weights(iota(shape, 1), iota(shape, 0) & (HALF - 1))
    phases_across = prolong_weights(phased(iota(shape, 1)), iota(shape, 0) & (HALF - 1))
    phases_along = prolong_weights(phased(iota(shape, 0)), iota(shape, 1) & (HALF - 1))
    weave = jnp.where(phased(iota(shape, 0)) == iota(shape, 1), 1.0, 0.0).astype(jnp.bfloat16)
    unweave = jnp.where(phased(iota(shape, 1)) == iota(shape, 0), 1.0, 0.0).astype(jnp.bfloat16)
    edge = iota((16, SIDE), 0)
    edge = jnp.where(edge < 8, edge, SIDE + 7 - edge)
    edge_up = prolong_weights(edge, iota((16, SIDE), 1) & (HALF - 1))
    rim = iota((16, SIDE), 0)
    rim = jnp.where(rim < 8, rim, HALF + 7 - rim)
    rim_pick = jnp.where((iota((16, SIDE), 1) & (HALF - 1)) == rim, 1.0, 0.0).astype(jnp.bfloat16)
    edge_and_rim = jnp.concatenate([edge_up, rim_pick], axis=0)
    edge_pick = jnp.where(iota((16, SIDE), 1) == edge, 1.0, 0.0).astype(jnp.bfloat16)
    for buf in stages:
        for i in range(2):
            for c in range(3):
                for y in range(2):
                    for x in range(2):
                        buf[i, c, y, x, 0:PAD] = jnp.zeros((PAD, HALF), jnp.float32)
                        buf[i, c, y, x, PAD + HALF :] = jnp.zeros((PAD, HALF), jnp.float32)

    def face_copies():
        ends = [
            (face_data.at[pl.ds(3, 2)], face_data.at[pl.ds(1, 2)]),
            (face_data.at[pl.ds(3, 2)], face_data.at[pl.ds(5, 2)]),
            (face_data.at[4], face_data.at[0]),
            (face_data.at[3], face_data.at[7]),
        ]
        made = []
        for n, (src, dst) in enumerate(ends):
            made.append(
                pltpu.make_async_remote_copy(
                    src_ref=src,
                    dst_ref=dst,
                    send_sem=face_send.at[n],
                    recv_sem=face_recv.at[n],
                    device_id=(reach[n],),
                    device_id_type=MESH,
                )
            )
        return made

    def corner_copies():
        made = []
        for n, by in enumerate(steps):
            made.append(
                pltpu.make_async_remote_copy(
                    src_ref=corner_data.at[REACH, pl.ds(0, 4)],
                    dst_ref=corner_data.at[REACH - by, pl.ds(0, 4)],
                    send_sem=corner_send.at[n],
                    recv_sem=corner_recv.at[n],
                    device_id=(reach[n],),
                    device_id_type=MESH,
                )
            )
        return made

    pl.semaphore_wait(barrier, sum(jnp.where(there, 1, 0) for there in exists))
    land_copy = pltpu.make_async_remote_copy(
        src_ref=land_ref.at[2 * (1 - parity)],
        dst_ref=land.at[3],
        send_sem=pair_send.at[0],
        recv_sem=pair_recv.at[0],
        device_id=(partner,),
        device_id_type=MESH,
    )
    land_copy.start()

    for load in loads + small:
        load.wait()
    parent = [parents_ref[i] % 4 for i in range(2)]
    edges = []
    for i in range(2):
        for c in range(3):
            block = quads[parent[i], c]
            across = dot_t(edge_and_rim, split(block, 1))
            along = dot(edge_and_rim, split(block, 0))
            edges += [across[0:16], along[0:16]]
            for f in range(4):
                rows = (across, along)[f // 2][16 + 8 * (f % 2) : 19 + 8 * (f % 2)]
                face_data[3 + i, f, 3 * c : 3 * c + 3, :] = rows
    edges = dot(split(jnp.concatenate(edges, axis=0), 1), columns_up).reshape(2, 3, 4, 8, SIDE)
    for c in range(3):
        t0[c] = jnp.concatenate([edges[0, c], edges[1, c]], axis=0)

    for i in range(2):
        for c in range(3):
            half_done = dot(split(quads[parent[i], c], 1), phases_across)
            fine = dot(phases_along, split(half_done, 0))
            for y in range(2):
                for x in range(2):
                    x_buf[i, c, y, x, PAD : PAD + HALF] = fine[
                        y * HALF : (y + 1) * HALF, x * HALF : (x + 1) * HALF
                    ]

    land_load.wait()
    land_copy.wait_recv()
    count = counts_ref[me]
    slots = []
    for i in range(2):
        even_slot = jnp.where(i >= count, 3, i)
        odd_slot = jnp.where(i - 2 + count < 0, 3, i - 2 + count)
        slots.append(jnp.where(parity == 0, even_slot, odd_slot))
    tables = (table_of(diff_ref), table_of(grow_ref))
    classes_of = []
    for i in range(2):
        classes = land[slots[i]].astype(jnp.float32).astype(jnp.bfloat16)
        classes_of.append(classes)
        rims = jnp.concatenate([dot_t(edge_pick, classes), dot(edge_pick, classes)], axis=0)
        d, g = look_up(rims, tables)
        for f in range(4):
            rows = slice(8 * f, 8 * f + 8)
            strip_diffus[4 * i + f] = d[rows]
            strip_growth[4 * i + f] = g[rows]
            for a in range(3):
                for j in range(2):
                    at = 9 + 2 * a + j
                    row = 8 * f + a
                    face_data[3 + i, f, at : at + 1, :] = rims[
                        row : row + 1, j * HALF : (j + 1) * HALF
                    ]

    lane8, sub8 = iota((8, HALF), 1), iota((8, HALF), 0)
    for i in range(2):
        for x in range(2):
            row = jnp.zeros((8, HALF), jnp.float32)
            for q in range(5):
                pf = 4 * i + x
                strip_of = t0[q, pf] if q < 3 else (strip_diffus, strip_growth)[q - 3][pf]
                for y in range(2):
                    cell = lane8 - (64 * y + 9 * q + 3 * sub8)
                    inside = (cell >= 0) & (cell < 3) & (sub8 < 3)
                    cell = jnp.clip(cell, 0, 2)
                    cell = HALF - 1 - cell if y else cell
                    part = pick_lanes(strip_of[:, y * HALF : (y + 1) * HALF], cell)
                    row = row + jnp.where(inside, part, 0.0)
            at = 2 * i + x
            corner_data[REACH, at : at + 1, :] = jnp.sum(row, axis=0, keepdims=True)

    for n, copy in enumerate(face_copies()):
        pl.when(exists[n])(copy.start)
    for n, copy in enumerate(corner_copies()):
        pl.when(exists[n])(copy.start)

    for i in range(2):
        classes = dot(classes_of[i], unweave).astype(jnp.bfloat16)
        for n in range(8):
            rows = slice(32 * n, 32 * n + 32)
            d, g = look_up(dot(weave[rows], classes), tables)
            y, m = n // 4, 32 * (n % 4)
            for x in range(2):
                diffus_buf[i, y, x, m : m + 32] = d[:, x * HALF : (x + 1) * HALF]
                growth_buf[i, y, x, m : m + 32] = g[:, x * HALF : (x + 1) * HALF]

    def cross(patch, face):
        value = nb_ref[face, patch]
        has = value >= 0
        return jnp.where(has, value, patch), jnp.where(has, face ^ 1, face)

    strip = (8, 8, SIDE)
    sub = iota(strip, 1)
    lane_half = iota((8, 8, HALF), 2)

    def gather_outer():
        first = [
            jnp.where(sub8 == 0, 1.0, jnp.where(sub8 == 1, 0.75, jnp.where(sub8 == 2, 0.25, 0.0))),
            jnp.where(sub8 == 0, 0.0, jnp.where(sub8 == 1, 0.25, 0.75)),
            jnp.where(sub8 >= 3, 0.25, 0.0),
        ]
        index = {}
        for kind in range(2):
            for e in range(2):
                b = jnp.minimum(lane8 if e else HALF - 1 - lane8, 2)
                a = jnp.minimum(sub8, 2)
                index[kind, e] = 3 * a + b if kind == 0 else 3 * b + a
        walls, classes = [], []
        for i in range(2):
            for f in range(4):
                patch, face = cross(2 * me + i, f)
                where = jnp.clip(patch - (2 * me - 3), 0, 7)
                for c in range(3):
                    parts = []
                    for a in range(3):
                        at = 3 * c + a
                        row = face_data[where, face, at : at + 1, :]
                        parts.append(first[a] * jnp.broadcast_to(row, (8, HALF)))
                    walls.append(parts[0] + parts[1] + parts[2])
                for j in range(2):
                    rows = []
                    for a in range(3):
                        at = 9 + 2 * a + j
                        rows.append(
                            jnp.broadcast_to(face_data[where, face, at : at + 1, :], (8, HALF))
                        )
                    classes.append(jnp.where(sub8 == 0, rows[0], jnp.where(sub8 == 1, rows[1], rows[2])))
        walls = dot(split(jnp.concatenate(walls, axis=0), 1), columns_up).reshape(8, 3, 8, SIDE)
        d, g = look_up(jnp.concatenate(classes, axis=0), tables)
        d, g = d.reshape(8, 2, 8, HALF), g.reshape(8, 2, 8, HALF)
        for c in range(3):
            h0[c, :, :, 0:SIDE] = walls[:, c]
        for j in range(2):
            at = slice(j * HALF, HALF + j * HALF)
            outer_diffus[:, :, at] = d[:, j]
            outer_growth[:, :, at] = g[:, j]

        low_half = lane8 < HALF // 2
        for i in range(2):
            for f in range(4):
                pf = 4 * i + f
                kind = f // 2
                start = cross(2 * me + i, f)
                chains = []
                for e in range(2):
                    patch, wall = start
                    side = 2 * (1 - kind) + e
                    chain = []
                    for step in range(3):
                        if step % 2 == 0:
                            patch, side = cross(patch, side)
                        else:
                            patch, wall = cross(patch, wall)
                        x = wall if kind == 0 else side
                        y = (side if kind == 0 else wall) - 2
                        window = jnp.clip((patch >> 1) - me + REACH, 0, 2 * REACH)
                        row = corner_data[window, pl.ds(2 * (patch & 1) + x, 1), :]
                        row = jnp.broadcast_to(row, (8, HALF))
                        chain.append(jnp.where(y == 1, pltpu.roll(row, 64, 1), row))
                    chains.append(chain)
                for step in range(3):
                    for q in range(5 if step < 2 else 3):
                        tiles = []
                        for e in range(2):
                            if step < 2:
                                at = index[kind, e] + 9 * q
                            else:
                                at = jnp.full((8, HALF), 9 * q, jnp.int32)
                            tiles.append(pick_lanes(chains[e][step], at))
                        if step < 2:
                            tile = jnp.where(low_half, tiles[1], tiles[0])
                        else:
                            tile = jnp.where(low_half, tiles[0], tiles[1])
                        if step == 0 and q < 3:
                            h0[q, pf, :, SIDE:] = tile
                        elif step == 0:
                            (outer_diffus, outer_growth)[q - 3][pf, :, SIDE:] = tile
                        elif step == 1 and q < 3:
                            l0[q, pf] = tile
                        elif step == 1:
                            (far_diffus, far_growth)[q - 3][pf] = tile
                        else:
                            k0[q, pf] = tile

    def rates_of(s, now, laps, diffus, growth):
        return scaled_rates(WEIGHTS[s], *now, *laps, diffus, growth)

    rising = iota((8, HALF), 0)
    falling = HALF - 1 - rising

    def strip_laplacian(now, beyond):
        ghost = jnp.broadcast_to(beyond[:, 0:1, :], strip)
        ends = []
        for e in range(2):
            columns = []
            for i in range(2):
                for f in range(4):
                    face = ghost[4 * i + (2 if f < 2 else 0) + e]
                    if f % 2:
                        columns.append(pick_lanes(face[:, HALF:], falling))
                    else:
                        columns.append(pick_lanes(face[:, :HALF], rising))
            ends.append(jnp.stack(columns, axis=0))
        above = jnp.where(sub == 0, ghost, pltpu.roll(now, 1, 1))
        below = pltpu.roll(now, 7, 1)
        rolled = pltpu.roll(now, 1, 2)
        left = jnp.where(lane_half == 0, ends[0], rolled[:, :, :HALF])
        left = jnp.concatenate([left, rolled[:, :, HALF:]], axis=2)
        rolled = pltpu.roll(now, SIDE - 1, 2)
        right = jnp.where(lane_half == HALF - 1, ends[1], rolled[:, :, HALF:])
        right = jnp.concatenate([rolled[:, :, :HALF], right], axis=2)
        return (left + right) + (below + above) - 4.0 * now

    def round_laplacian(now, facing):
        lanes = now.shape[2]
        above = jnp.where(iota(now.shape, 1) == 0, facing, pltpu.roll(now, 1, 1))
        below = pltpu.roll(now, 7, 1)
        sides = pltpu.roll(now, 1, 2) + pltpu.roll(now, lanes - 1, 2)
        return sides + (below + above) - 4.0 * now

    def strip_stage(s):
        inner = [strips[s][c] for c in range(3)]
        beyond = [outer[s][c, :, :, 0:SIDE] for c in range(3)]
        laps = [strip_laplacian(inner[c], beyond[c]) for c in range(3)]
        rates = rates_of(s, inner, laps, strip_diffus[...], strip_growth[...])
        if s == 3:
            for c in range(3):
                block = combine(t0[c], t1[c], t2[c], t3[c], rates[c])
                for i in range(2):
                    ring[i, c] = block[4 * i : 4 * i + 4]
                    for f in (1, 3):
                        for r in range(4):
                            ring[i, c, f, 7 - r : 8 - r, :] = block[4 * i + f, r : r + 1, :]
            return
        for c in range(3):
            strips[s + 1][c] = t0[c] + rates[c]
        if s == 2:
            laps = []
            for c in range(3):
                whole = outer[s][c]
                now = beyond[c]
                above = jnp.where(sub == 0, inner[c], pltpu.roll(now, 1, 1))
                sides = pltpu.roll(whole, 1, 2) + pltpu.roll(whole, SIDE + HALF - 1, 2)
                laps.append(sides[:, :, 0:SIDE] + (pltpu.roll(now, 7, 1) + above) - 4.0 * now)
            rates = rates_of(
                s, beyond, laps, outer_diffus[:, :, 0:SIDE], outer_growth[:, :, 0:SIDE]
            )
            for c in range(3):
                outer[3][c, :, :, 0:SIDE] = h0[c, :, :, 0:SIDE] + rates[c]
            return
        far = [(l0, l1)[s][c] for c in range(3)]
        now = [outer[s][c] for c in range(3)]
        laps = [
            round_laplacian(now[c], jnp.concatenate([inner[c], far[c]], axis=2)) for c in range(3)
        ]
        rates = rates_of(s, now, laps, outer_diffus[...], outer_growth[...])
        for c in range(3):
            outer[s + 1][c] = h0[c] + rates[c]
        if s == 0:
            laps = []
            for c in range(3):
                both = jnp.concatenate([far[c], k0[c]], axis=2)
                facing = jnp.concatenate([now[c][:, :, SIDE:], k0[c]], axis=2)
                laps.append(round_laplacian(both, facing)[:, :, :HALF])
            rates = rates_of(s, far, laps, far_diffus[...], far_growth[...])
            for c in range(3):
                l1[c] = far[c] + rates[c]

    def bulk_stage(i, s):
        src = stages[s]
        dst = stages[(s + 1) % 4] if s < 3 else s2_buf

        def step_rows(step, carry):
            r = pl.multiple_of(step * 8, 8)
            at = PAD + r
            here = pl.ds(at, 8)
            now = [[src[i, c, n // 2, n % 2, here, :] for n in range(4)] for c in range(3)]
            lap = [[None] * 4 for _ in range(3)]
            for c in range(3):
                for n in range(4):
                    y, x = n // 2, n % 2
                    beside = now[c][2 * y + 1 - x]
                    beyond = pltpu.roll(beside, HALF - 1 if x else 1, 1)
                    upright = now[c][2 * (1 - y) + x]
                    further = src[i, c, 1 - y, x, pl.ds(at + 2 * y - 1, 8), :]
                    lap[c][n] = (beside + beyond) + (upright + further) - 4.0 * now[c][n]
            for n in range(4):
                y, x = n // 2, n % 2
                rates = scaled_rates(
                    WEIGHTS[s],
                    *[now[c][n] for c in range(3)],
                    *[lap[c][n] for c in range(3)],
                    diffus_buf[i, y, x, pl.ds(r, 8), :],
                    growth_buf[i, y, x, pl.ds(r, 8), :],
                )
                for c in range(3):
                    base = now[c][n] if s == 0 else x_buf[i, c, y, x, here, :]
                    if s < 3:
                        value = base + rates[c]
                    else:
                        value = combine(
                            base,
                            s2_buf[i, c, y, x, here, :],
                            s3_buf[i, c, y, x, here, :],
                            now[c][n],
                            rates[c],
                        )
                    dst[i, c, y, x, here, :] = value
            return carry

        lax.fori_loop(0, HALF // 8, step_rows, 0, unroll=16)

    def bulk_weave(i):
        for c in range(3):
            for y in range(2):
                both = jnp.concatenate(
                    [s2_buf[i, c, y, x, PAD : PAD + HALF, :] for x in range(2)], axis=1
                )
                high = both.astype(jnp.bfloat16)
                low = (both - high.astype(jnp.float32)).astype(jnp.bfloat16)
                woven = dot(high, weave) + dot(low, weave)
                for j in range(2):
                    result[i, c, j, pl.ds(y, HALF, stride=2), :] = woven[:, j * HALF : (j + 1) * HALF]

    def to_partner(n, src, dst):
        return pltpu.make_async_remote_copy(
            src_ref=src.at[moving],
            dst_ref=dst.at[2],
            send_sem=pair_send.at[n],
            recv_sem=pair_recv.at[n],
            device_id=(partner,),
            device_id_type=MESH,
        )

    result_copy = to_partner(1, result, result_out)
    ring_copy = to_partner(2, ring, ring_out)
    own_copies = [
        pltpu.make_async_copy(result.at[moving], result_out.at[moving], own_sem.at[0]),
        pltpu.make_async_copy(ring, ring_out.at[pl.ds(0, 2)], own_sem.at[1]),
        pltpu.make_async_copy(result.at[parity], result_out.at[parity], own_sem.at[2]),
    ]
    for s in range(4):
        bulk_stage(moving, s)
    bulk_weave(moving)
    result_copy.start()
    own_copies[0].start()
    for s in range(4):
        bulk_stage(parity, s)
    for n, copy in enumerate(face_copies()):
        pl.when(exists[n ^ 1])(copy.wait_recv)
    for n, copy in enumerate(corner_copies()):
        pl.when(exists[n ^ 1])(copy.wait_recv)
    gather_outer()
    for s in range(4):
        strip_stage(s)
    ring_copy.start()
    own_copies[1].start()
    bulk_weave(parity)
    own_copies[2].start()
    for n, copy in enumerate(face_copies()):
        pl.when(exists[n])(copy.wait_send)
    for n, copy in enumerate(corner_copies()):
        pl.when(exists[n])(copy.wait_send)
    land_copy.wait_send()
    for copy in own_copies:
        copy.wait()
    result_copy.wait()
    ring_copy.wait()


def merge_kernel(
    counts_hbm,
    result_hbm,
    ring_hbm,
    out_hbm,
    counts_ref,
    result,
    ring,
    zeros,
    count_sem,
    ring_sem,
    result_sem,
    out_sem,
    zero_sem,
):
    me = lax.axis_index("owner")
    even = me % 2 == 0
    count_copy = pltpu.make_async_copy(counts_hbm, counts_ref, count_sem)
    ring_copy = pltpu.make_async_copy(ring_hbm, ring, ring_sem)
    count_copy.start()
    ring_copy.start()

    def load(e, c):
        return pltpu.make_async_copy(result_hbm.at[e, c], result.at[e, c], result_sem.at[e, c])

    for e in range(3):
        for c in range(3):
            load(e, c).start()
    zeros[...] = jnp.zeros_like(zeros)
    count_copy.wait()
    count = counts_ref[me]
    empties = []
    for s in (1, 2):
        empties.append(pltpu.make_async_copy(zeros, out_hbm.at[s], zero_sem.at[s - 1]))
        pl.when(s >= count)(empties[-1].start)

    slots = []
    for e in range(3):
        slot = jnp.where(even, e, (e + 1) % 3 + count - 3)
        slots.append((slot, (slot >= 0) & (slot < count)))
    low_lanes = iota((8, HALF), 1) < 4
    high_lanes = iota((8, HALF), 1) >= HALF - 4
    sub_rows = iota((8, HALF), 0)
    ring_copy.wait()

    def stores(e, c):
        made = []
        for j in range(2):
            made.append(
                pltpu.make_async_copy(
                    result.at[e, c, j],
                    out_hbm.at[jnp.maximum(slots[e][0], 0), c, :, pl.ds(j * HALF, HALF)],
                    out_sem.at[e, c, j],
                )
            )
        return made

    for e in range(3):
        for c in range(3):
            gap = jnp.zeros((HALF - 16, SIDE), jnp.float32)
            block = jnp.concatenate([ring[e, c, 0], gap, ring[e, c, 1]], axis=0)
            sides = (block[:, :HALF].T, block[:, HALF:].T)
            load(e, c).wait()
            for j in range(2):
                lanes = high_lanes if j else low_lanes
                for t in range(SIDE // 8):
                    rows = slice(8 * t, 8 * t + 8)
                    within = slice(8 * t % HALF, 8 * t % HALF + 8)
                    value = jnp.where(lanes, sides[t // 16][within], result[e, c, j, rows, :])
                    if t == 0:
                        value = jnp.where(
                            sub_rows < 4, ring[e, c, 2, :, j * HALF : (j + 1) * HALF], value
                        )
                    if t == SIDE // 8 - 1:
                        value = jnp.where(
                            sub_rows >= 4, ring[e, c, 3, :, j * HALF : (j + 1) * HALF], value
                        )
                    result[e, c, j, rows, :] = value

            @pl.when(slots[e][1])
            def _(e=e, c=c):
                for copy in stores(e, c):
                    copy.start()

    for e in range(3):

        @pl.when(slots[e][1])
        def _(e=e):
            for c in range(3):
                for copy in stores(e, c):
                    copy.wait()

    for s in (1, 2):
        pl.when(s >= count)(empties[s - 1].wait)


def body(coarse, parents, new_counts, neighbours, land_cover, class_diffusivity, class_growth):
    owners = lax.axis_size("owner")
    f32 = jnp.float32
    hbm = pl.BlockSpec(memory_space=pltpu.HBM)
    stage_buf = pltpu.VMEM((2, 3, 2, 2, HALF + 2 * PAD, HALF), f32)
    strip_buf = pltpu.VMEM((3, 8, 8, SIDE), f32)
    outer_buf = pltpu.VMEM((3, 8, 8, SIDE + HALF), f32)
    far_buf = pltpu.VMEM((3, 8, 8, HALF), f32)
    results = jax.ShapeDtypeStruct((3, 3, 2, SIDE, HALF), f32)
    rings = jax.ShapeDtypeStruct((3, 3, 4, 8, SIDE), f32)
    whole, outer = pl.pallas_call(
        functools.partial(kernel, owners),
        out_shape=(results, rings),
        in_specs=[hbm] * 7,
        out_specs=(hbm, hbm),
        scratch_shapes=[
            pltpu.SMEM((2,), jnp.int32),
            pltpu.SMEM((owners,), jnp.int32),
            pltpu.SMEM((4, 2 * owners), jnp.int32),
            pltpu.SMEM((CLASSES,), f32),
            pltpu.SMEM((CLASSES,), f32),
            pltpu.VMEM((4, 3, HALF, HALF), f32),
            pltpu.VMEM((4, SIDE, SIDE), jnp.int32),
            stage_buf,
            stage_buf,
            stage_buf,
            stage_buf,
            pltpu.VMEM((2, 2, 2, HALF, HALF), f32),
            pltpu.VMEM((2, 2, 2, HALF, HALF), f32),
            pltpu.VMEM((2, 3, 2, SIDE, HALF), f32),
            pltpu.VMEM((2, 3, 4, 8, SIDE), f32),
            strip_buf,
            strip_buf,
            strip_buf,
            strip_buf,
            pltpu.VMEM((8, 8, SIDE), f32),
            pltpu.VMEM((8, 8, SIDE), f32),
            pltpu.VMEM((8, 4, 16, HALF), f32),
            pltpu.VMEM((2 * REACH + 1, 8, HALF), f32),
            outer_buf,
            outer_buf,
            outer_buf,
            outer_buf,
            pltpu.VMEM((8, 8, SIDE + HALF), f32),
            pltpu.VMEM((8, 8, SIDE + HALF), f32),
            far_buf,
            far_buf,
            pltpu.VMEM((8, 8, HALF), f32),
            pltpu.VMEM((8, 8, HALF), f32),
            far_buf,
            pltpu.SemaphoreType.DMA((4,)),
            pltpu.SemaphoreType.DMA((5,)),
            pltpu.SemaphoreType.DMA,
            pltpu.SemaphoreType.DMA((4,)),
            pltpu.SemaphoreType.DMA((4,)),
            pltpu.SemaphoreType.DMA((2 * REACH,)),
            pltpu.SemaphoreType.DMA((2 * REACH,)),
            pltpu.SemaphoreType.DMA((3,)),
            pltpu.SemaphoreType.DMA((3,)),
            pltpu.SemaphoreType.DMA((3,)),
        ],
        compiler_params=pltpu.CompilerParams(
            collective_id=0, has_side_effects=True, vmem_limit_bytes=VMEM_LIMIT
        ),
        name="regrid_step",
    )(parents, new_counts, neighbours.T, class_diffusivity, class_growth, coarse, land_cover)
    return pl.pallas_call(
        merge_kernel,
        out_shape=jax.ShapeDtypeStruct((3, 3, SIDE, SIDE), f32),
        in_specs=[hbm] * 3,
        out_specs=hbm,
        scratch_shapes=[
            pltpu.SMEM((owners,), jnp.int32),
            pltpu.VMEM(results.shape, f32),
            pltpu.VMEM(rings.shape, f32),
            pltpu.VMEM((3, SIDE, SIDE), f32),
            pltpu.SemaphoreType.DMA,
            pltpu.SemaphoreType.DMA,
            pltpu.SemaphoreType.DMA((3, 3)),
            pltpu.SemaphoreType.DMA((3, 3, 2)),
            pltpu.SemaphoreType.DMA((2,)),
        ],
        compiler_params=pltpu.CompilerParams(vmem_limit_bytes=VMEM_LIMIT),
        name="merge_slots",
    )(new_counts, whole, outer)


def solution(mesh):
    return jax.shard_map(
        body,
        mesh=mesh,
        in_specs=(
            P("owner", None, None, None),
            P("owner"),
            P(),
            P(),
            P("owner", None, None),
            P(),
            P(),
        ),
        out_specs=P("owner", None, None, None),
        check_vma=False,
    )
```

```python
import functools

import jax
import jax.numpy as jnp
from jax import lax
from jax.experimental import pallas as pl
from jax.experimental.pallas import tpu as pltpu
from jax.sharding import PartitionSpec as P

SIDE = 256
HALF = 128
CLASSES = 11
PAD = 8
REACH = 6
VMEM_LIMIT = 62 * 1024 * 1024
WEIGHTS = (0.5, 0.5, 1.0, 1.0 / 6.0)
MESH = pl.DeviceIdType.MESH


def iota(shape, dim):
    return lax.broadcasted_iota(jnp.int32, shape, dim)


def phased(index):
    return 2 * (index & (HALF - 1)) + (index >> 7)


def prolong_weights(fine, coarse):
    near = fine >> 1
    second = jnp.clip(near + jnp.where((fine & 1) == 0, -1, 1), 0, HALF - 1)
    heavy = jnp.where(coarse == near, 0.75, 0.0)
    light = jnp.where(coarse == second, 0.25, 0.0)
    return (heavy + light).astype(jnp.bfloat16)


def split(block, axis):
    high = block.astype(jnp.bfloat16)
    low = (block - high.astype(jnp.float32)).astype(jnp.bfloat16)
    return jnp.concatenate([high, low], axis=axis)


def dot(a, b):
    return jnp.dot(a, b, preferred_element_type=jnp.float32)


def dot_t(a, b):
    return lax.dot_general(a, b, (((1,), (1,)), ((), ())), preferred_element_type=jnp.float32)


def table_of(ref):
    lane = iota((8, HALF), 1)
    table = jnp.zeros((8, HALF), jnp.float32)
    for number in range(CLASSES):
        table = jnp.where(lane == number, ref[number], table)
    return table


def pick_lanes(table, index):
    return jnp.take_along_axis(table, index, axis=1)


def look_up(classes, tables):
    index = classes.astype(jnp.int32)
    rows, columns = classes.shape
    found = []
    for table in tables:
        bands = []
        for r in range(0, rows, 8):
            blocks = [
                pick_lanes(table, index[r : r + 8, k : k + HALF]) for k in range(0, columns, HALF)
            ]
            bands.append(jnp.concatenate(blocks, axis=1))
        found.append(jnp.concatenate(bands, axis=0))
    return found


def scaled_rates(weight, x0, x1, x2, lap0, lap1, lap2, diffus, growth):
    dw = diffus * weight
    gw = growth * weight
    xw = x0 * weight
    r0 = dw * lap0 + (gw * x0) * (x1 - x0 - x2)
    r1 = (0.5 * dw) * lap1 + (0.4 * weight - x1 * (0.4 * weight + xw))
    r2 = dw * lap2 + (xw - (0.3 * weight) * x2)
    return r0, r1, r2


def combine(x, s2, s3, s4, rate):
    return (s2 + 2.0 * s3 + s4 - x) * (1.0 / 3.0) + rate


def kernel(
    owners,
    parents_hbm,
    counts_hbm,
    nb_hbm,
    diff_hbm,
    grow_hbm,
    coarse_ref,
    land_ref,
    result_out,
    ring_out,
    parents_ref,
    counts_ref,
    nb_ref,
    diff_ref,
    grow_ref,
    quads,
    land,
    land_far,
    x_buf,
    s2_buf,
    s3_buf,
    s4_buf,
    diffus_buf,
    growth_buf,
    result,
    ring,
    t0,
    t1,
    t2,
    t3,
    strip_diffus,
    strip_growth,
    face_data,
    corner_data,
    h0,
    h1,
    h2,
    h3,
    outer_diffus,
    outer_growth,
    l0,
    l1,
    far_diffus,
    far_growth,
    k0,
    load_sem,
    small_sem,
    land_sem,
    face_send,
    face_recv,
    corner_send,
    corner_recv,
    pair_send,
    pair_recv,
    own_sem,
):
    me = lax.axis_index("owner")
    parity = me % 2
    partner = me + 1 - 2 * parity
    moving = 1 - parity
    steps = [by for far in range(1, REACH + 1) for by in (far, -far)]
    reach = [(me + by) % owners for by in steps]
    exists = [(me + by < owners) & (me + by >= 0) for by in steps]
    stages = (x_buf, s2_buf, s3_buf, s4_buf)
    strips = (t0, t1, t2, t3)
    outer = (h0, h1, h2, h3)

    loads = []
    for q in range(4):
        block = coarse_ref.at[0, :, pl.ds((q // 2) * HALF, HALF), pl.ds((q % 2) * HALF, HALF)]
        loads.append(pltpu.make_async_copy(block, quads.at[q], load_sem.at[q]))
    for load in loads:
        load.start()
    small = []
    pairs = (
        (parents_hbm, parents_ref),
        (counts_hbm, counts_ref),
        (nb_hbm, nb_ref),
        (diff_hbm, diff_ref),
        (grow_hbm, grow_ref),
    )
    for n, (src, dst) in enumerate(pairs):
        small.append(pltpu.make_async_copy(src, dst, small_sem.at[n]))
        small[n].start()
    land_load = pltpu.make_async_copy(land_ref, land, land_sem)
    land_load.start()
    barrier = pltpu.get_barrier_semaphore()
    for n in range(len(steps)):

        @pl.when(exists[n])
        def _(n=n):
            pl.semaphore_signal(barrier, inc=1, device_id=(reach[n],), device_id_type=MESH)


    shape = (SIDE, SIDE)
    columns_up = prolong_weights(iota(shape, 1), iota(shape, 0) & (HALF - 1))
    phases_across = prolong_weights(phased(iota(shape, 1)), iota(shape, 0) & (HALF - 1))
    phases_along = prolong_weights(phased(iota(shape, 0)), iota(shape, 1) & (HALF - 1))
    weave = jnp.where(phased(iota(shape, 0)) == iota(shape, 1), 1.0, 0.0).astype(jnp.bfloat16)
    unweave = jnp.where(phased(iota(shape, 1)) == iota(shape, 0), 1.0, 0.0).astype(jnp.bfloat16)
    edge = iota((16, SIDE), 0)
    edge = jnp.where(edge < 8, edge, SIDE + 7 - edge)
    edge_up = prolong_weights(edge, iota((16, SIDE), 1) & (HALF - 1))
    rim = iota((16, SIDE), 0)
    rim = jnp.where(rim < 8, rim, HALF + 7 - rim)
    rim_pick = jnp.where((iota((16, SIDE), 1) & (HALF - 1)) == rim, 1.0, 0.0).astype(jnp.bfloat16)
    edge_and_rim = jnp.concatenate([edge_up, rim_pick], axis=0)
    edge_pick = jnp.where(iota((16, SIDE), 1) == edge, 1.0, 0.0).astype(jnp.bfloat16)
    for buf in stages:
        for i in range(2):
            for c in range(3):
                for y in range(2):
                    for x in range(2):
                        buf[i, c, y, x, 0:PAD] = jnp.zeros((PAD, HALF), jnp.float32)
                        buf[i, c, y, x, PAD + HALF :] = jnp.zeros((PAD, HALF), jnp.float32)

    def face_copies():
        ends = [
            (face_data.at[pl.ds(3, 2)], face_data.at[pl.ds(1, 2)]),
            (face_data.at[pl.ds(3, 2)], face_data.at[pl.ds(5, 2)]),
            (face_data.at[4], face_data.at[0]),
            (face_data.at[3], face_data.at[7]),
        ]
        made = []
        for n, (src, dst) in enumerate(ends):
            made.append(
                pltpu.make_async_remote_copy(
                    src_ref=src,
                    dst_ref=dst,
                    send_sem=face_send.at[n],
                    recv_sem=face_recv.at[n],
                    device_id=(reach[n],),
                    device_id_type=MESH,
                )
            )
        return made

    def corner_copies():
        made = []
        for n, by in enumerate(steps):
            made.append(
                pltpu.make_async_remote_copy(
                    src_ref=corner_data.at[REACH, pl.ds(0, 4)],
                    dst_ref=corner_data.at[REACH - by, pl.ds(0, 4)],
                    send_sem=corner_send.at[n],
                    recv_sem=corner_recv.at[n],
                    device_id=(reach[n],),
                    device_id_type=MESH,
                )
            )
        return made

    def bulk_stage(i, s):
        src = stages[s]
        dst = stages[(s + 1) % 4] if s < 3 else s2_buf

        def step_rows(step, carry):
            r = pl.multiple_of(step * 8, 8)
            at = PAD + r
            here = pl.ds(at, 8)
            now = [[src[i, c, n // 2, n % 2, here, :] for n in range(4)] for c in range(3)]
            lap = [[None] * 4 for _ in range(3)]
            for c in range(3):
                for n in range(4):
                    y, x = n // 2, n % 2
                    beside = now[c][2 * y + 1 - x]
                    beyond = pltpu.roll(beside, HALF - 1 if x else 1, 1)
                    upright = now[c][2 * (1 - y) + x]
                    further = src[i, c, 1 - y, x, pl.ds(at + 2 * y - 1, 8), :]
                    lap[c][n] = (beside + beyond) + (upright + further) - 4.0 * now[c][n]
            for n in range(4):
                y, x = n // 2, n % 2
                rates = scaled_rates(
                    WEIGHTS[s],
                    *[now[c][n] for c in range(3)],
                    *[lap[c][n] for c in range(3)],
                    diffus_buf[i, y, x, pl.ds(r, 8), :],
                    growth_buf[i, y, x, pl.ds(r, 8), :],
                )
                for c in range(3):
                    base = now[c][n] if s == 0 else x_buf[i, c, y, x, here, :]
                    if s < 3:
                        value = base + rates[c]
                    else:
                        value = combine(
                            base,
                            s2_buf[i, c, y, x, here, :],
                            s3_buf[i, c, y, x, here, :],
                            now[c][n],
                            rates[c],
                        )
                    dst[i, c, y, x, here, :] = value
            return carry

        lax.fori_loop(0, HALF // 8, step_rows, 0, unroll=8)

    for load in loads + small:
        load.wait()
    parent = [parents_ref[i] % 4 for i in range(2)]
    edges = []
    for i in range(2):
        for c in range(3):
            block = quads[parent[i], c]
            across = dot_t(edge_and_rim, split(block, 1))
            along = dot(edge_and_rim, split(block, 0))
            edges += [across[0:16], along[0:16]]
            for f in range(4):
                rows = (across, along)[f // 2][16 + 8 * (f % 2) : 19 + 8 * (f % 2)]
                face_data[3 + i, f, 3 * c : 3 * c + 3, :] = rows
    edges = dot(split(jnp.concatenate(edges, axis=0), 1), columns_up).reshape(2, 3, 4, 8, SIDE)
    for c in range(3):
        t0[c] = jnp.concatenate([edges[0, c], edges[1, c]], axis=0)

    for i in range(2):
        for c in range(3):
            half_done = dot(split(quads[parent[i], c], 1), phases_across)
            fine = dot(phases_along, split(half_done, 0))
            for y in range(2):
                for x in range(2):
                    x_buf[i, c, y, x, PAD : PAD + HALF] = fine[
                        y * HALF : (y + 1) * HALF, x * HALF : (x + 1) * HALF
                    ]

    pl.semaphore_wait(barrier, sum(jnp.where(there, 1, 0) for there in exists))
    land_copy = pltpu.make_async_remote_copy(
        src_ref=land_ref.at[2 * (1 - parity)],
        dst_ref=land_far,
        send_sem=pair_send.at[0],
        recv_sem=pair_recv.at[0],
        device_id=(partner,),
        device_id_type=MESH,
    )
    land_copy.start()

    count = counts_ref[me]
    tables = (table_of(diff_ref), table_of(grow_ref))

    def rim_rates(i, classes):
        rims = jnp.concatenate([dot_t(edge_pick, classes), dot(edge_pick, classes)], axis=0)
        d, g = look_up(rims, tables)
        for f in range(4):
            rows = slice(8 * f, 8 * f + 8)
            strip_diffus[4 * i + f] = d[rows]
            strip_growth[4 * i + f] = g[rows]
            for a in range(3):
                for j in range(2):
                    at = 9 + 2 * a + j
                    row = 8 * f + a
                    face_data[3 + i, f, at : at + 1, :] = rims[
                        row : row + 1, j * HALF : (j + 1) * HALF
                    ]

    def bulk_rates(i, classes):
        classes = dot(classes, unweave).astype(jnp.bfloat16)
        for n in range(8):
            rows = slice(32 * n, 32 * n + 32)
            d, g = look_up(dot(weave[rows], classes), tables)
            y, m = n // 4, 32 * (n % 4)
            for x in range(2):
                diffus_buf[i, y, x, m : m + 32] = d[:, x * HALF : (x + 1) * HALF]
                growth_buf[i, y, x, m : m + 32] = g[:, x * HALF : (x + 1) * HALF]

    land_load.wait()
    classes = land[jnp.where(parity == 0, 0, jnp.clip(count - 1, 0, 2))]
    classes = classes.astype(jnp.float32).astype(jnp.bfloat16)
    rim_rates(parity, classes)
    bulk_rates(parity, classes)
    bulk_stage(parity, 0)

    land_copy.wait_recv()
    classes = jnp.where(
        count < 2, land_far[...], land[jnp.where(parity == 0, 1, jnp.clip(count - 2, 0, 2))]
    )
    classes = classes.astype(jnp.float32).astype(jnp.bfloat16)
    rim_rates(moving, classes)

    lane8, sub8 = iota((8, HALF), 1), iota((8, HALF), 0)
    for i in range(2):
        for x in range(2):
            row = jnp.zeros((8, HALF), jnp.float32)
            for q in range(5):
                pf = 4 * i + x
                strip_of = t0[q, pf] if q < 3 else (strip_diffus, strip_growth)[q - 3][pf]
                for y in range(2):
                    cell = lane8 - (64 * y + 9 * q + 3 * sub8)
                    inside = (cell >= 0) & (cell < 3) & (sub8 < 3)
                    cell = jnp.clip(cell, 0, 2)
                    cell = HALF - 1 - cell if y else cell
                    part = pick_lanes(strip_of[:, y * HALF : (y + 1) * HALF], cell)
                    row = row + jnp.where(inside, part, 0.0)
            at = 2 * i + x
            corner_data[REACH, at : at + 1, :] = jnp.sum(row, axis=0, keepdims=True)

    for n, copy in enumerate(face_copies()):
        pl.when(exists[n])(copy.start)
    for n, copy in enumerate(corner_copies()):
        pl.when(exists[n])(copy.start)

    bulk_rates(moving, classes)

    def cross(patch, face):
        value = nb_ref[face, patch]
        has = value >= 0
        return jnp.where(has, value, patch), jnp.where(has, face ^ 1, face)

    strip = (8, 8, SIDE)
    sub = iota(strip, 1)
    lane_half = iota((8, 8, HALF), 2)

    def gather_outer():
        first = [
            jnp.where(sub8 == 0, 1.0, jnp.where(sub8 == 1, 0.75, jnp.where(sub8 == 2, 0.25, 0.0))),
            jnp.where(sub8 == 0, 0.0, jnp.where(sub8 == 1, 0.25, 0.75)),
            jnp.where(sub8 >= 3, 0.25, 0.0),
        ]
        index = {}
        for kind in range(2):
            for e in range(2):
                b = jnp.minimum(lane8 if e else HALF - 1 - lane8, 2)
                a = jnp.minimum(sub8, 2)
                index[kind, e] = 3 * a + b if kind == 0 else 3 * b + a
        walls, classes = [], []
        for i in range(2):
            for f in range(4):
                patch, face = cross(2 * me + i, f)
                where = jnp.clip(patch - (2 * me - 3), 0, 7)
                for c in range(3):
                    parts = []
                    for a in range(3):
                        at = 3 * c + a
                        row = face_data[where, face, at : at + 1, :]
                        parts.append(first[a] * jnp.broadcast_to(row, (8, HALF)))
                    walls.append(parts[0] + parts[1] + parts[2])
                for j in range(2):
                    rows = []
                    for a in range(3):
                        at = 9 + 2 * a + j
                        rows.append(
                            jnp.broadcast_to(face_data[where, face, at : at + 1, :], (8, HALF))
                        )
                    classes.append(jnp.where(sub8 == 0, rows[0], jnp.where(sub8 == 1, rows[1], rows[2])))
        walls = dot(split(jnp.concatenate(walls, axis=0), 1), columns_up).reshape(8, 3, 8, SIDE)
        d, g = look_up(jnp.concatenate(classes, axis=0), tables)
        d, g = d.reshape(8, 2, 8, HALF), g.reshape(8, 2, 8, HALF)
        for c in range(3):
            h0[c, :, :, 0:SIDE] = walls[:, c]
        for j in range(2):
            at = slice(j * HALF, HALF + j * HALF)
            outer_diffus[:, :, at] = d[:, j]
            outer_growth[:, :, at] = g[:, j]

        low_half = lane8 < HALF // 2
        for i in range(2):
            for f in range(4):
                pf = 4 * i + f
                kind = f // 2
                start = cross(2 * me + i, f)
                chains = []
                for e in range(2):
                    patch, wall = start
                    side = 2 * (1 - kind) + e
                    chain = []
                    for step in range(3):
                        if step % 2 == 0:
                            patch, side = cross(patch, side)
                        else:
                            patch, wall = cross(patch, wall)
                        x = wall if kind == 0 else side
                        y = (side if kind == 0 else wall) - 2
                        window = jnp.clip((patch >> 1) - me + REACH, 0, 2 * REACH)
                        row = corner_data[window, pl.ds(2 * (patch & 1) + x, 1), :]
                        row = jnp.broadcast_to(row, (8, HALF))
                        chain.append(jnp.where(y == 1, pltpu.roll(row, 64, 1), row))
                    chains.append(chain)
                for step in range(3):
                    for q in range(5 if step < 2 else 3):
                        tiles = []
                        for e in range(2):
                            if step < 2:
                                at = index[kind, e] + 9 * q
                            else:
                                at = jnp.full((8, HALF), 9 * q, jnp.int32)
                            tiles.append(pick_lanes(chains[e][step], at))
                        if step < 2:
                            tile = jnp.where(low_half, tiles[1], tiles[0])
                        else:
                            tile = jnp.where(low_half, tiles[0], tiles[1])
                        if step == 0 and q < 3:
                            h0[q, pf, :, SIDE:] = tile
                        elif step == 0:
                            (outer_diffus, outer_growth)[q - 3][pf, :, SIDE:] = tile
                        elif step == 1 and q < 3:
                            l0[q, pf] = tile
                        elif step == 1:
                            (far_diffus, far_growth)[q - 3][pf] = tile
                        else:
                            k0[q, pf] = tile

    def rates_of(s, now, laps, diffus, growth):
        return scaled_rates(WEIGHTS[s], *now, *laps, diffus, growth)

    rising = iota((8, HALF), 0)
    falling = HALF - 1 - rising

    def strip_laplacian(now, beyond):
        ghost = jnp.broadcast_to(beyond[:, 0:1, :], strip)
        ends = []
        for e in range(2):
            columns = []
            for i in range(2):
                for f in range(4):
                    face = ghost[4 * i + (2 if f < 2 else 0) + e]
                    if f % 2:
                        columns.append(pick_lanes(face[:, HALF:], falling))
                    else:
                        columns.append(pick_lanes(face[:, :HALF], rising))
            ends.append(jnp.stack(columns, axis=0))
        above = jnp.where(sub == 0, ghost, pltpu.roll(now, 1, 1))
        below = pltpu.roll(now, 7, 1)
        rolled = pltpu.roll(now, 1, 2)
        left = jnp.where(lane_half == 0, ends[0], rolled[:, :, :HALF])
        left = jnp.concatenate([left, rolled[:, :, HALF:]], axis=2)
        rolled = pltpu.roll(now, SIDE - 1, 2)
        right = jnp.where(lane_half == HALF - 1, ends[1], rolled[:, :, HALF:])
        right = jnp.concatenate([rolled[:, :, :HALF], right], axis=2)
        return (left + right) + (below + above) - 4.0 * now

    def round_laplacian(now, facing):
        lanes = now.shape[2]
        above = jnp.where(iota(now.shape, 1) == 0, facing, pltpu.roll(now, 1, 1))
        below = pltpu.roll(now, 7, 1)
        sides = pltpu.roll(now, 1, 2) + pltpu.roll(now, lanes - 1, 2)
        return sides + (below + above) - 4.0 * now

    def strip_stage(s):
        inner = [strips[s][c] for c in range(3)]
        beyond = [outer[s][c, :, :, 0:SIDE] for c in range(3)]
        laps = [strip_laplacian(inner[c], beyond[c]) for c in range(3)]
        rates = rates_of(s, inner, laps, strip_diffus[...], strip_growth[...])
        if s == 3:
            for c in range(3):
                block = combine(t0[c], t1[c], t2[c], t3[c], rates[c])
                for i in range(2):
                    ring[i, c] = block[4 * i : 4 * i + 4]
                    for f in (1, 3):
                        for r in range(4):
                            ring[i, c, f, 7 - r : 8 - r, :] = block[4 * i + f, r : r + 1, :]
            return
        for c in range(3):
            strips[s + 1][c] = t0[c] + rates[c]
        if s == 2:
            laps = []
            for c in range(3):
                whole = outer[s][c]
                now = beyond[c]
                above = jnp.where(sub == 0, inner[c], pltpu.roll(now, 1, 1))
                sides = pltpu.roll(whole, 1, 2) + pltpu.roll(whole, SIDE + HALF - 1, 2)
                laps.append(sides[:, :, 0:SIDE] + (pltpu.roll(now, 7, 1) + above) - 4.0 * now)
            rates = rates_of(
                s, beyond, laps, outer_diffus[:, :, 0:SIDE], outer_growth[:, :, 0:SIDE]
            )
            for c in range(3):
                outer[3][c, :, :, 0:SIDE] = h0[c, :, :, 0:SIDE] + rates[c]
            return
        far = [(l0, l1)[s][c] for c in range(3)]
        now = [outer[s][c] for c in range(3)]
        laps = [
            round_laplacian(now[c], jnp.concatenate([inner[c], far[c]], axis=2)) for c in range(3)
        ]
        rates = rates_of(s, now, laps, outer_diffus[...], outer_growth[...])
        for c in range(3):
            outer[s + 1][c] = h0[c] + rates[c]
        if s == 0:
            laps = []
            for c in range(3):
                both = jnp.concatenate([far[c], k0[c]], axis=2)
                facing = jnp.concatenate([now[c][:, :, SIDE:], k0[c]], axis=2)
                laps.append(round_laplacian(both, facing)[:, :, :HALF])
            rates = rates_of(s, far, laps, far_diffus[...], far_growth[...])
            for c in range(3):
                l1[c] = far[c] + rates[c]

    def bulk_weave(i):
        for c in range(3):
            for y in range(2):
                both = jnp.concatenate(
                    [s2_buf[i, c, y, x, PAD : PAD + HALF, :] for x in range(2)], axis=1
                )
                high = both.astype(jnp.bfloat16)
                low = (both - high.astype(jnp.float32)).astype(jnp.bfloat16)
                woven = dot(high, weave) + dot(low, weave)
                for j in range(2):
                    result[i, c, j, pl.ds(y, HALF, stride=2), :] = woven[:, j * HALF : (j + 1) * HALF]

    def to_partner(n, src, dst):
        return pltpu.make_async_remote_copy(
            src_ref=src.at[moving],
            dst_ref=dst.at[2],
            send_sem=pair_send.at[n],
            recv_sem=pair_recv.at[n],
            device_id=(partner,),
            device_id_type=MESH,
        )

    result_copy = to_partner(1, result, result_out)
    ring_copy = to_partner(2, ring, ring_out)
    own_copies = [
        pltpu.make_async_copy(result.at[moving], result_out.at[moving], own_sem.at[0]),
        pltpu.make_async_copy(ring, ring_out.at[pl.ds(0, 2)], own_sem.at[1]),
        pltpu.make_async_copy(result.at[parity], result_out.at[parity], own_sem.at[2]),
    ]
    for s in range(4):
        bulk_stage(moving, s)
    bulk_weave(moving)
    result_copy.start()
    own_copies[0].start()
    for s in range(1, 4):
        bulk_stage(parity, s)
    for n, copy in enumerate(face_copies()):
        pl.when(exists[n ^ 1])(copy.wait_recv)
    for n, copy in enumerate(corner_copies()):
        pl.when(exists[n ^ 1])(copy.wait_recv)
    gather_outer()
    for s in range(4):
        strip_stage(s)
    ring_copy.start()
    own_copies[1].start()
    bulk_weave(parity)
    own_copies[2].start()
    for n, copy in enumerate(face_copies()):
        pl.when(exists[n])(copy.wait_send)
    for n, copy in enumerate(corner_copies()):
        pl.when(exists[n])(copy.wait_send)
    land_copy.wait_send()
    for copy in own_copies:
        copy.wait()
    result_copy.wait()
    ring_copy.wait()


def merge_kernel(
    counts_hbm,
    result_hbm,
    ring_hbm,
    out_hbm,
    counts_ref,
    result,
    ring,
    zeros,
    count_sem,
    ring_sem,
    result_sem,
    out_sem,
    zero_sem,
):
    me = lax.axis_index("owner")
    even = me % 2 == 0
    count_copy = pltpu.make_async_copy(counts_hbm, counts_ref, count_sem)
    ring_copy = pltpu.make_async_copy(ring_hbm, ring, ring_sem)
    count_copy.start()
    ring_copy.start()

    def load(e, c):
        return pltpu.make_async_copy(result_hbm.at[e, c], result.at[e, c], result_sem.at[e, c])

    for e in range(3):
        for c in range(3):
            load(e, c).start()
    zeros[...] = jnp.zeros_like(zeros)
    count_copy.wait()
    count = counts_ref[me]
    empties = []
    for s in (1, 2):
        empties.append(pltpu.make_async_copy(zeros, out_hbm.at[s], zero_sem.at[s - 1]))
        pl.when(s >= count)(empties[-1].start)

    slots = []
    for e in range(3):
        slot = jnp.where(even, e, (e + 1) % 3 + count - 3)
        slots.append((slot, (slot >= 0) & (slot < count)))
    low_lanes = iota((8, HALF), 1) < 4
    high_lanes = iota((8, HALF), 1) >= HALF - 4
    sub_rows = iota((8, HALF), 0)
    ring_copy.wait()

    def stores(e, c):
        made = []
        for j in range(2):
            made.append(
                pltpu.make_async_copy(
                    result.at[e, c, j],
                    out_hbm.at[jnp.maximum(slots[e][0], 0), c, :, pl.ds(j * HALF, HALF)],
                    out_sem.at[e, c, j],
                )
            )
        return made

    for e in range(3):
        for c in range(3):
            gap = jnp.zeros((HALF - 16, SIDE), jnp.float32)
            block = jnp.concatenate([ring[e, c, 0], gap, ring[e, c, 1]], axis=0)
            sides = (block[:, :HALF].T, block[:, HALF:].T)
            load(e, c).wait()
            for j in range(2):
                lanes = high_lanes if j else low_lanes
                for t in range(SIDE // 8):
                    rows = slice(8 * t, 8 * t + 8)
                    within = slice(8 * t % HALF, 8 * t % HALF + 8)
                    value = jnp.where(lanes, sides[t // 16][within], result[e, c, j, rows, :])
                    if t == 0:
                        value = jnp.where(
                            sub_rows < 4, ring[e, c, 2, :, j * HALF : (j + 1) * HALF], value
                        )
                    if t == SIDE // 8 - 1:
                        value = jnp.where(
                            sub_rows >= 4, ring[e, c, 3, :, j * HALF : (j + 1) * HALF], value
                        )
                    result[e, c, j, rows, :] = value

            @pl.when(slots[e][1])
            def _(e=e, c=c):
                for copy in stores(e, c):
                    copy.start()

    for e in range(3):

        @pl.when(slots[e][1])
        def _(e=e):
            for c in range(3):
                for copy in stores(e, c):
                    copy.wait()

    for s in (1, 2):
        pl.when(s >= count)(empties[s - 1].wait)


def body(coarse, parents, new_counts, neighbours, land_cover, class_diffusivity, class_growth):
    owners = lax.axis_size("owner")
    f32 = jnp.float32
    hbm = pl.BlockSpec(memory_space=pltpu.HBM)
    stage_buf = pltpu.VMEM((2, 3, 2, 2, HALF + 2 * PAD, HALF), f32)
    strip_buf = pltpu.VMEM((3, 8, 8, SIDE), f32)
    outer_buf = pltpu.VMEM((3, 8, 8, SIDE + HALF), f32)
    far_buf = pltpu.VMEM((3, 8, 8, HALF), f32)
    results = jax.ShapeDtypeStruct((3, 3, 2, SIDE, HALF), f32)
    rings = jax.ShapeDtypeStruct((3, 3, 4, 8, SIDE), f32)
    whole, outer = pl.pallas_call(
        functools.partial(kernel, owners),
        out_shape=(results, rings),
        in_specs=[hbm] * 7,
        out_specs=(hbm, hbm),
        scratch_shapes=[
            pltpu.SMEM((2,), jnp.int32),
            pltpu.SMEM((owners,), jnp.int32),
            pltpu.SMEM((4, 2 * owners), jnp.int32),
            pltpu.SMEM((CLASSES,), f32),
            pltpu.SMEM((CLASSES,), f32),
            pltpu.VMEM((4, 3, HALF, HALF), f32),
            pltpu.VMEM((3, SIDE, SIDE), jnp.int32),
            pltpu.VMEM((SIDE, SIDE), jnp.int32),
            stage_buf,
            stage_buf,
            stage_buf,
            stage_buf,
            pltpu.VMEM((2, 2, 2, HALF, HALF), f32),
            pltpu.VMEM((2, 2, 2, HALF, HALF), f32),
            pltpu.VMEM((2, 3, 2, SIDE, HALF), f32),
            pltpu.VMEM((2, 3, 4, 8, SIDE), f32),
            strip_buf,
            strip_buf,
            strip_buf,
            strip_buf,
            pltpu.VMEM((8, 8, SIDE), f32),
            pltpu.VMEM((8, 8, SIDE), f32),
            pltpu.VMEM((8, 4, 16, HALF), f32),
            pltpu.VMEM((2 * REACH + 1, 8, HALF), f32),
            outer_buf,
            outer_buf,
            outer_buf,
            outer_buf,
            pltpu.VMEM((8, 8, SIDE + HALF), f32),
            pltpu.VMEM((8, 8, SIDE + HALF), f32),
            far_buf,
            far_buf,
            pltpu.VMEM((8, 8, HALF), f32),
            pltpu.VMEM((8, 8, HALF), f32),
            far_buf,
            pltpu.SemaphoreType.DMA((4,)),
            pltpu.SemaphoreType.DMA((5,)),
            pltpu.SemaphoreType.DMA,
            pltpu.SemaphoreType.DMA((4,)),
            pltpu.SemaphoreType.DMA((4,)),
            pltpu.SemaphoreType.DMA((2 * REACH,)),
            pltpu.SemaphoreType.DMA((2 * REACH,)),
            pltpu.SemaphoreType.DMA((3,)),
            pltpu.SemaphoreType.DMA((3,)),
            pltpu.SemaphoreType.DMA((3,)),
        ],
        compiler_params=pltpu.CompilerParams(
            collective_id=0, has_side_effects=True, vmem_limit_bytes=VMEM_LIMIT
        ),
        name="regrid_step",
    )(parents, new_counts, neighbours.T, class_diffusivity, class_growth, coarse, land_cover)
    return pl.pallas_call(
        merge_kernel,
        out_shape=jax.ShapeDtypeStruct((3, 3, SIDE, SIDE), f32),
        in_specs=[hbm] * 3,
        out_specs=hbm,
        scratch_shapes=[
            pltpu.SMEM((owners,), jnp.int32),
            pltpu.VMEM(results.shape, f32),
            pltpu.VMEM(rings.shape, f32),
            pltpu.VMEM((3, SIDE, SIDE), f32),
            pltpu.SemaphoreType.DMA,
            pltpu.SemaphoreType.DMA,
            pltpu.SemaphoreType.DMA((3, 3)),
            pltpu.SemaphoreType.DMA((3, 3, 2)),
            pltpu.SemaphoreType.DMA((2,)),
        ],
        compiler_params=pltpu.CompilerParams(vmem_limit_bytes=VMEM_LIMIT),
        name="merge_slots",
    )(new_counts, whole, outer)


def solution(mesh):
    return jax.shard_map(
        body,
        mesh=mesh,
        in_specs=(
            P("owner", None, None, None),
            P("owner"),
            P(),
            P(),
            P("owner", None, None),
            P(),
            P(),
        ),
        out_specs=P("owner", None, None, None),
        check_vma=False,
    )
```

```python
import functools

import jax
import jax.numpy as jnp
from jax import lax
from jax.experimental import pallas as pl
from jax.experimental.pallas import tpu as pltpu
from jax.sharding import PartitionSpec as P

SIDE = 256
HALF = 128
CLASSES = 11
PAD = 8
REACH = 6
VMEM_LIMIT = 62 * 1024 * 1024
WEIGHTS = (0.5, 0.5, 1.0, 1.0 / 6.0)
MESH = pl.DeviceIdType.MESH


def iota(shape, dim):
    return lax.broadcasted_iota(jnp.int32, shape, dim)


def phased(index):
    return 2 * (index & (HALF - 1)) + (index >> 7)


def prolong_weights(fine, coarse):
    near = fine >> 1
    second = jnp.clip(near + jnp.where((fine & 1) == 0, -1, 1), 0, HALF - 1)
    heavy = jnp.where(coarse == near, 0.75, 0.0)
    light = jnp.where(coarse == second, 0.25, 0.0)
    return (heavy + light).astype(jnp.bfloat16)


def split(block, axis):
    high = block.astype(jnp.bfloat16)
    low = (block - high.astype(jnp.float32)).astype(jnp.bfloat16)
    return jnp.concatenate([high, low], axis=axis)


def dot(a, b):
    return jnp.dot(a, b, preferred_element_type=jnp.float32)


def dot_t(a, b):
    return lax.dot_general(a, b, (((1,), (1,)), ((), ())), preferred_element_type=jnp.float32)


def table_of(ref):
    lane = iota((8, HALF), 1)
    table = jnp.zeros((8, HALF), jnp.float32)
    for number in range(CLASSES):
        table = jnp.where(lane == number, ref[number], table)
    return table


def pick_lanes(table, index):
    return jnp.take_along_axis(table, index, axis=1)


def look_up(classes, tables):
    index = classes.astype(jnp.int32)
    rows, columns = classes.shape
    found = []
    for table in tables:
        bands = []
        for r in range(0, rows, 8):
            blocks = [
                pick_lanes(table, index[r : r + 8, k : k + HALF]) for k in range(0, columns, HALF)
            ]
            bands.append(jnp.concatenate(blocks, axis=1))
        found.append(jnp.concatenate(bands, axis=0))
    return found


def scaled_rates(weight, x0, x1, x2, lap0, lap1, lap2, diffus, growth):
    dw = diffus * weight
    gw = growth * weight
    xw = x0 * weight
    r0 = dw * lap0 + (gw * x0) * (x1 - x0 - x2)
    r1 = (0.5 * dw) * lap1 + (0.4 * weight - x1 * (0.4 * weight + xw))
    r2 = dw * lap2 + (xw - (0.3 * weight) * x2)
    return r0, r1, r2


def combine(x, s2, s3, s4, rate):
    return (s2 + 2.0 * s3 + s4 - x) * (1.0 / 3.0) + rate


def kernel(
    owners,
    parents_hbm,
    counts_hbm,
    nb_hbm,
    diff_hbm,
    grow_hbm,
    coarse_ref,
    land_ref,
    result_out,
    ring_out,
    parents_ref,
    counts_ref,
    nb_ref,
    diff_ref,
    grow_ref,
    quads,
    land,
    x_buf,
    s2_buf,
    s3_buf,
    s4_buf,
    diffus_buf,
    growth_buf,
    result,
    ring,
    t0,
    t1,
    t2,
    t3,
    strip_diffus,
    strip_growth,
    face_data,
    corner_data,
    h0,
    h1,
    h2,
    h3,
    outer_diffus,
    outer_growth,
    l0,
    l1,
    far_diffus,
    far_growth,
    k0,
    load_sem,
    small_sem,
    land_sem,
    face_send,
    face_recv,
    corner_send,
    corner_recv,
    pair_send,
    pair_recv,
    own_sem,
):
    me = lax.axis_index("owner")
    parity = me % 2
    partner = me + 1 - 2 * parity
    moving = 1 - parity
    steps = [by for far in range(1, REACH + 1) for by in (far, -far)]
    reach = [(me + by) % owners for by in steps]
    exists = [(me + by < owners) & (me + by >= 0) for by in steps]
    stages = (x_buf, s2_buf, s3_buf, s4_buf)
    strips = (t0, t1, t2, t3)
    outer = (h0, h1, h2, h3)

    loads = []
    for q in range(4):
        block = coarse_ref.at[0, :, pl.ds((q // 2) * HALF, HALF), pl.ds((q % 2) * HALF, HALF)]
        loads.append(pltpu.make_async_copy(block, quads.at[q], load_sem.at[q]))
    for load in loads:
        load.start()
    small = []
    pairs = (
        (parents_hbm, parents_ref),
        (counts_hbm, counts_ref),
        (nb_hbm, nb_ref),
        (diff_hbm, diff_ref),
        (grow_hbm, grow_ref),
    )
    for n, (src, dst) in enumerate(pairs):
        small.append(pltpu.make_async_copy(src, dst, small_sem.at[n]))
        small[n].start()
    land_load = pltpu.make_async_copy(land_ref, land.at[pl.ds(0, 3)], land_sem)
    land_load.start()
    barrier = pltpu.get_barrier_semaphore()
    for n in range(len(steps)):

        @pl.when(exists[n])
        def _(n=n):
            pl.semaphore_signal(barrier, inc=1, device_id=(reach[n],), device_id_type=MESH)


    shape = (SIDE, SIDE)
    columns_up = prolong_weights(iota(shape, 1), iota(shape, 0) & (HALF - 1))
    phases_across = prolong_weights(phased(iota(shape, 1)), iota(shape, 0) & (HALF - 1))
    phases_along = prolong_weights(phased(iota(shape, 0)), iota(shape, 1) & (HALF - 1))
    weave = jnp.where(phased(iota(shape, 0)) == iota(shape, 1), 1.0, 0.0).astype(jnp.bfloat16)
    unweave = jnp.where(phased(iota(shape, 1)) == iota(shape, 0), 1.0, 0.0).astype(jnp.bfloat16)
    edge = iota((16, SIDE), 0)
    edge = jnp.where(edge < 8, edge, SIDE + 7 - edge)
    edge_up = prolong_weights(edge, iota((16, SIDE), 1) & (HALF - 1))
    rim = iota((16, SIDE), 0)
    rim = jnp.where(rim < 8, rim, HALF + 7 - rim)
    rim_pick = jnp.where((iota((16, SIDE), 1) & (HALF - 1)) == rim, 1.0, 0.0).astype(jnp.bfloat16)
    edge_and_rim = jnp.concatenate([edge_up, rim_pick], axis=0)
    edge_pick = jnp.where(iota((16, SIDE), 1) == edge, 1.0, 0.0).astype(jnp.bfloat16)
    for buf in stages:
        for i in range(2):
            for c in range(3):
                for y in range(2):
                    for x in range(2):
                        buf[i, c, y, x, 0:PAD] = jnp.zeros((PAD, HALF), jnp.float32)
                        buf[i, c, y, x, PAD + HALF :] = jnp.zeros((PAD, HALF), jnp.float32)

    def face_copies():
        ends = [
            (face_data.at[pl.ds(3, 2)], face_data.at[pl.ds(1, 2)]),
            (face_data.at[pl.ds(3, 2)], face_data.at[pl.ds(5, 2)]),
            (face_data.at[4], face_data.at[0]),
            (face_data.at[3], face_data.at[7]),
        ]
        made = []
        for n, (src, dst) in enumerate(ends):
            made.append(
                pltpu.make_async_remote_copy(
                    src_ref=src,
                    dst_ref=dst,
                    send_sem=face_send.at[n],
                    recv_sem=face_recv.at[n],
                    device_id=(reach[n],),
                    device_id_type=MESH,
                )
            )
        return made

    def corner_copies():
        made = []
        for n, by in enumerate(steps):
            made.append(
                pltpu.make_async_remote_copy(
                    src_ref=corner_data.at[REACH, pl.ds(0, 4)],
                    dst_ref=corner_data.at[REACH - by, pl.ds(0, 4)],
                    send_sem=corner_send.at[n],
                    recv_sem=corner_recv.at[n],
                    device_id=(reach[n],),
                    device_id_type=MESH,
                )
            )
        return made

    pl.semaphore_wait(barrier, sum(jnp.where(there, 1, 0) for there in exists))
    land_copy = pltpu.make_async_remote_copy(
        src_ref=land_ref.at[2 * (1 - parity)],
        dst_ref=land.at[3],
        send_sem=pair_send.at[0],
        recv_sem=pair_recv.at[0],
        device_id=(partner,),
        device_id_type=MESH,
    )
    land_copy.start()

    for load in loads + small:
        load.wait()
    parent = [parents_ref[i] % 4 for i in range(2)]
    edges = []
    for i in range(2):
        for c in range(3):
            block = quads[parent[i], c]
            across = dot_t(edge_and_rim, split(block, 1))
            along = dot(edge_and_rim, split(block, 0))
            edges += [across[0:16], along[0:16]]
            for f in range(4):
                rows = (across, along)[f // 2][16 + 8 * (f % 2) : 19 + 8 * (f % 2)]
                face_data[3 + i, f, 3 * c : 3 * c + 3, :] = rows
    edges = dot(split(jnp.concatenate(edges, axis=0), 1), columns_up).reshape(2, 3, 4, 8, SIDE)
    for c in range(3):
        t0[c] = jnp.concatenate([edges[0, c], edges[1, c]], axis=0)

    for i in range(2):
        for c in range(3):
            half_done = dot(split(quads[parent[i], c], 1), phases_across)
            fine = dot(phases_along, split(half_done, 0))
            for y in range(2):
                for x in range(2):
                    x_buf[i, c, y, x, PAD : PAD + HALF] = fine[
                        y * HALF : (y + 1) * HALF, x * HALF : (x + 1) * HALF
                    ]

    land_load.wait()
    land_copy.wait_recv()
    count = counts_ref[me]
    slots = []
    for i in range(2):
        even_slot = jnp.where(i >= count, 3, i)
        odd_slot = jnp.where(i - 2 + count < 0, 3, i - 2 + count)
        slots.append(jnp.where(parity == 0, even_slot, odd_slot))
    tables = (table_of(diff_ref), table_of(grow_ref))
    classes_of = []
    for i in range(2):
        classes = land[slots[i]].astype(jnp.float32).astype(jnp.bfloat16)
        classes_of.append(classes)
        rims = jnp.concatenate([dot_t(edge_pick, classes), dot(edge_pick, classes)], axis=0)
        d, g = look_up(rims, tables)
        for f in range(4):
            rows = slice(8 * f, 8 * f + 8)
            strip_diffus[4 * i + f] = d[rows]
            strip_growth[4 * i + f] = g[rows]
            for a in range(3):
                for j in range(2):
                    at = 9 + 2 * a + j
                    row = 8 * f + a
                    face_data[3 + i, f, at : at + 1, :] = rims[
                        row : row + 1, j * HALF : (j + 1) * HALF
                    ]

    lane8, sub8 = iota((8, HALF), 1), iota((8, HALF), 0)
    for i in range(2):
        for x in range(2):
            row = jnp.zeros((8, HALF), jnp.float32)
            for q in range(5):
                pf = 4 * i + x
                strip_of = t0[q, pf] if q < 3 else (strip_diffus, strip_growth)[q - 3][pf]
                for y in range(2):
                    cell = lane8 - (64 * y + 9 * q + 3 * sub8)
                    inside = (cell >= 0) & (cell < 3) & (sub8 < 3)
                    cell = jnp.clip(cell, 0, 2)
                    cell = HALF - 1 - cell if y else cell
                    part = pick_lanes(strip_of[:, y * HALF : (y + 1) * HALF], cell)
                    row = row + jnp.where(inside, part, 0.0)
            at = 2 * i + x
            corner_data[REACH, at : at + 1, :] = jnp.sum(row, axis=0, keepdims=True)

    for n, copy in enumerate(face_copies()):
        pl.when(exists[n])(copy.start)
    for n, copy in enumerate(corner_copies()):
        pl.when(exists[n])(copy.start)

    for i in range(2):
        classes = dot(classes_of[i], unweave).astype(jnp.bfloat16)
        for n in range(8):
            rows = slice(32 * n, 32 * n + 32)
            d, g = look_up(dot(weave[rows], classes), tables)
            y, m = n // 4, 32 * (n % 4)
            for x in range(2):
                diffus_buf[i, y, x, m : m + 32] = d[:, x * HALF : (x + 1) * HALF]
                growth_buf[i, y, x, m : m + 32] = g[:, x * HALF : (x + 1) * HALF]

    def cross(patch, face):
        value = nb_ref[face, patch]
        has = value >= 0
        return jnp.where(has, value, patch), jnp.where(has, face ^ 1, face)

    strip = (8, 8, SIDE)
    sub = iota(strip, 1)
    lane_half = iota((8, 8, HALF), 2)

    def gather_outer():
        first = [
            jnp.where(sub8 == 0, 1.0, jnp.where(sub8 == 1, 0.75, jnp.where(sub8 == 2, 0.25, 0.0))),
            jnp.where(sub8 == 0, 0.0, jnp.where(sub8 == 1, 0.25, 0.75)),
            jnp.where(sub8 >= 3, 0.25, 0.0),
        ]
        index = {}
        for kind in range(2):
            for e in range(2):
                b = jnp.minimum(lane8 if e else HALF - 1 - lane8, 2)
                a = jnp.minimum(sub8, 2)
                index[kind, e] = 3 * a + b if kind == 0 else 3 * b + a
        walls, classes = [], []
        for i in range(2):
            for f in range(4):
                patch, face = cross(2 * me + i, f)
                where = jnp.clip(patch - (2 * me - 3), 0, 7)
                for c in range(3):
                    parts = []
                    for a in range(3):
                        at = 3 * c + a
                        row = face_data[where, face, at : at + 1, :]
                        parts.append(first[a] * jnp.broadcast_to(row, (8, HALF)))
                    walls.append(parts[0] + parts[1] + parts[2])
                for j in range(2):
                    rows = []
                    for a in range(3):
                        at = 9 + 2 * a + j
                        rows.append(
                            jnp.broadcast_to(face_data[where, face, at : at + 1, :], (8, HALF))
                        )
                    classes.append(jnp.where(sub8 == 0, rows[0], jnp.where(sub8 == 1, rows[1], rows[2])))
        walls = dot(split(jnp.concatenate(walls, axis=0), 1), columns_up).reshape(8, 3, 8, SIDE)
        d, g = look_up(jnp.concatenate(classes, axis=0), tables)
        d, g = d.reshape(8, 2, 8, HALF), g.reshape(8, 2, 8, HALF)
        for c in range(3):
            h0[c, :, :, 0:SIDE] = walls[:, c]
        for j in range(2):
            at = slice(j * HALF, HALF + j * HALF)
            outer_diffus[:, :, at] = d[:, j]
            outer_growth[:, :, at] = g[:, j]

        low_half = lane8 < HALF // 2
        for i in range(2):
            for f in range(4):
                pf = 4 * i + f
                kind = f // 2
                start = cross(2 * me + i, f)
                chains = []
                for e in range(2):
                    patch, wall = start
                    side = 2 * (1 - kind) + e
                    chain = []
                    for step in range(3):
                        if step % 2 == 0:
                            patch, side = cross(patch, side)
                        else:
                            patch, wall = cross(patch, wall)
                        x = wall if kind == 0 else side
                        y = (side if kind == 0 else wall) - 2
                        window = jnp.clip((patch >> 1) - me + REACH, 0, 2 * REACH)
                        row = corner_data[window, pl.ds(2 * (patch & 1) + x, 1), :]
                        row = jnp.broadcast_to(row, (8, HALF))
                        chain.append(jnp.where(y == 1, pltpu.roll(row, 64, 1), row))
                    chains.append(chain)
                for step in range(3):
                    for q in range(5 if step < 2 else 3):
                        tiles = []
                        for e in range(2):
                            if step < 2:
                                at = index[kind, e] + 9 * q
                            else:
                                at = jnp.full((8, HALF), 9 * q, jnp.int32)
                            tiles.append(pick_lanes(chains[e][step], at))
                        if step < 2:
                            tile = jnp.where(low_half, tiles[1], tiles[0])
                        else:
                            tile = jnp.where(low_half, tiles[0], tiles[1])
                        if step == 0 and q < 3:
                            h0[q, pf, :, SIDE:] = tile
                        elif step == 0:
                            (outer_diffus, outer_growth)[q - 3][pf, :, SIDE:] = tile
                        elif step == 1 and q < 3:
                            l0[q, pf] = tile
                        elif step == 1:
                            (far_diffus, far_growth)[q - 3][pf] = tile
                        else:
                            k0[q, pf] = tile

    def rates_of(s, now, laps, diffus, growth):
        return scaled_rates(WEIGHTS[s], *now, *laps, diffus, growth)

    rising = iota((8, HALF), 0)
    falling = HALF - 1 - rising

    def strip_laplacian(now, beyond):
        ghost = jnp.broadcast_to(beyond[:, 0:1, :], strip)
        ends = []
        for e in range(2):
            columns = []
            for i in range(2):
                for f in range(4):
                    face = ghost[4 * i + (2 if f < 2 else 0) + e]
                    if f % 2:
                        columns.append(pick_lanes(face[:, HALF:], falling))
                    else:
                        columns.append(pick_lanes(face[:, :HALF], rising))
            ends.append(jnp.stack(columns, axis=0))
        above = jnp.where(sub == 0, ghost, pltpu.roll(now, 1, 1))
        below = pltpu.roll(now, 7, 1)
        rolled = pltpu.roll(now, 1, 2)
        left = jnp.where(lane_half == 0, ends[0], rolled[:, :, :HALF])
        left = jnp.concatenate([left, rolled[:, :, HALF:]], axis=2)
        rolled = pltpu.roll(now, SIDE - 1, 2)
        right = jnp.where(lane_half == HALF - 1, ends[1], rolled[:, :, HALF:])
        right = jnp.concatenate([rolled[:, :, :HALF], right], axis=2)
        return (left + right) + (below + above) - 4.0 * now

    def round_laplacian(now, facing):
        lanes = now.shape[2]
        above = jnp.where(iota(now.shape, 1) == 0, facing, pltpu.roll(now, 1, 1))
        below = pltpu.roll(now, 7, 1)
        sides = pltpu.roll(now, 1, 2) + pltpu.roll(now, lanes - 1, 2)
        return sides + (below + above) - 4.0 * now

    def strip_stage(s):
        inner = [strips[s][c] for c in range(3)]
        beyond = [outer[s][c, :, :, 0:SIDE] for c in range(3)]
        laps = [strip_laplacian(inner[c], beyond[c]) for c in range(3)]
        rates = rates_of(s, inner, laps, strip_diffus[...], strip_growth[...])
        if s == 3:
            for c in range(3):
                block = combine(t0[c], t1[c], t2[c], t3[c], rates[c])
                for i in range(2):
                    ring[i, c] = block[4 * i : 4 * i + 4]
                    for f in (1, 3):
                        for r in range(4):
                            ring[i, c, f, 7 - r : 8 - r, :] = block[4 * i + f, r : r + 1, :]
            return
        for c in range(3):
            strips[s + 1][c] = t0[c] + rates[c]
        if s == 2:
            laps = []
            for c in range(3):
                whole = outer[s][c]
                now = beyond[c]
                above = jnp.where(sub == 0, inner[c], pltpu.roll(now, 1, 1))
                sides = pltpu.roll(whole, 1, 2) + pltpu.roll(whole, SIDE + HALF - 1, 2)
                laps.append(sides[:, :, 0:SIDE] + (pltpu.roll(now, 7, 1) + above) - 4.0 * now)
            rates = rates_of(
                s, beyond, laps, outer_diffus[:, :, 0:SIDE], outer_growth[:, :, 0:SIDE]
            )
            for c in range(3):
                outer[3][c, :, :, 0:SIDE] = h0[c, :, :, 0:SIDE] + rates[c]
            return
        far = [(l0, l1)[s][c] for c in range(3)]
        now = [outer[s][c] for c in range(3)]
        laps = [
            round_laplacian(now[c], jnp.concatenate([inner[c], far[c]], axis=2)) for c in range(3)
        ]
        rates = rates_of(s, now, laps, outer_diffus[...], outer_growth[...])
        for c in range(3):
            outer[s + 1][c] = h0[c] + rates[c]
        if s == 0:
            laps = []
            for c in range(3):
                both = jnp.concatenate([far[c], k0[c]], axis=2)
                facing = jnp.concatenate([now[c][:, :, SIDE:], k0[c]], axis=2)
                laps.append(round_laplacian(both, facing)[:, :, :HALF])
            rates = rates_of(s, far, laps, far_diffus[...], far_growth[...])
            for c in range(3):
                l1[c] = far[c] + rates[c]

    def bulk_stage(i, s):
        src = stages[s]
        dst = stages[(s + 1) % 4] if s < 3 else s2_buf

        def step_rows(step, carry):
            r = pl.multiple_of(step * 8, 8)
            at = PAD + r
            here = pl.ds(at, 8)
            now = [[src[i, c, n // 2, n % 2, here, :] for n in range(4)] for c in range(3)]
            lap = [[None] * 4 for _ in range(3)]
            for c in range(3):
                for n in range(4):
                    y, x = n // 2, n % 2
                    beside = now[c][2 * y + 1 - x]
                    beyond = pltpu.roll(beside, HALF - 1 if x else 1, 1)
                    upright = now[c][2 * (1 - y) + x]
                    further = src[i, c, 1 - y, x, pl.ds(at + 2 * y - 1, 8), :]
                    lap[c][n] = (beside + beyond) + (upright + further) - 4.0 * now[c][n]
            for n in range(4):
                y, x = n // 2, n % 2
                rates = scaled_rates(
                    WEIGHTS[s],
                    *[now[c][n] for c in range(3)],
                    *[lap[c][n] for c in range(3)],
                    diffus_buf[i, y, x, pl.ds(r, 8), :],
                    growth_buf[i, y, x, pl.ds(r, 8), :],
                )
                for c in range(3):
                    base = now[c][n] if s == 0 else x_buf[i, c, y, x, here, :]
                    if s < 3:
                        value = base + rates[c]
                    else:
                        value = combine(
                            base,
                            s2_buf[i, c, y, x, here, :],
                            s3_buf[i, c, y, x, here, :],
                            now[c][n],
                            rates[c],
                        )
                    dst[i, c, y, x, here, :] = value
            return carry

        lax.fori_loop(0, HALF // 8, step_rows, 0, unroll=8)

    def bulk_weave(i):
        for c in range(3):
            for y in range(2):
                both = jnp.concatenate(
                    [s2_buf[i, c, y, x, PAD : PAD + HALF, :] for x in range(2)], axis=1
                )
                high = both.astype(jnp.bfloat16)
                low = (both - high.astype(jnp.float32)).astype(jnp.bfloat16)
                woven = dot(high, weave) + dot(low, weave)
                for j in range(2):
                    result[i, c, j, pl.ds(y, HALF, stride=2), :] = woven[:, j * HALF : (j + 1) * HALF]

    def to_partner(n, src, dst):
        return pltpu.make_async_remote_copy(
            src_ref=src.at[moving],
            dst_ref=dst.at[2],
            send_sem=pair_send.at[n],
            recv_sem=pair_recv.at[n],
            device_id=(partner,),
            device_id_type=MESH,
        )

    result_copy = to_partner(1, result, result_out)
    ring_copy = to_partner(2, ring, ring_out)
    own_copies = [
        pltpu.make_async_copy(result.at[moving], result_out.at[moving], own_sem.at[0]),
        pltpu.make_async_copy(ring, ring_out.at[pl.ds(0, 2)], own_sem.at[1]),
        pltpu.make_async_copy(result.at[parity], result_out.at[parity], own_sem.at[2]),
    ]
    for s in range(4):
        bulk_stage(moving, s)
    bulk_weave(moving)
    result_copy.start()
    own_copies[0].start()
    for s in range(4):
        bulk_stage(parity, s)
    bulk_weave(parity)
    own_copies[2].start()
    for n, copy in enumerate(face_copies()):
        pl.when(exists[n ^ 1])(copy.wait_recv)
    for n, copy in enumerate(corner_copies()):
        pl.when(exists[n ^ 1])(copy.wait_recv)
    gather_outer()
    for s in range(4):
        strip_stage(s)
    ring_copy.start()
    own_copies[1].start()
    for n, copy in enumerate(face_copies()):
        pl.when(exists[n])(copy.wait_send)
    for n, copy in enumerate(corner_copies()):
        pl.when(exists[n])(copy.wait_send)
    land_copy.wait_send()
    for copy in own_copies:
        copy.wait()
    result_copy.wait()
    ring_copy.wait()


def merge_kernel(
    counts_hbm,
    result_hbm,
    ring_hbm,
    out_hbm,
    counts_ref,
    result,
    ring,
    zeros,
    count_sem,
    ring_sem,
    result_sem,
    out_sem,
    zero_sem,
):
    me = lax.axis_index("owner")
    even = me % 2 == 0
    count_copy = pltpu.make_async_copy(counts_hbm, counts_ref, count_sem)
    ring_copy = pltpu.make_async_copy(ring_hbm, ring, ring_sem)
    count_copy.start()
    ring_copy.start()

    def load(e, c):
        return pltpu.make_async_copy(result_hbm.at[e, c], result.at[e, c], result_sem.at[e, c])

    for e in range(3):
        for c in range(3):
            load(e, c).start()
    zeros[...] = jnp.zeros_like(zeros)
    count_copy.wait()
    count = counts_ref[me]
    empties = []
    for s in (1, 2):
        empties.append(pltpu.make_async_copy(zeros, out_hbm.at[s], zero_sem.at[s - 1]))
        pl.when(s >= count)(empties[-1].start)

    slots = []
    for e in range(3):
        slot = jnp.where(even, e, (e + 1) % 3 + count - 3)
        slots.append((slot, (slot >= 0) & (slot < count)))
    low_lanes = iota((8, HALF), 1) < 4
    high_lanes = iota((8, HALF), 1) >= HALF - 4
    sub_rows = iota((8, HALF), 0)
    ring_copy.wait()

    def stores(e, c):
        made = []
        for j in range(2):
            made.append(
                pltpu.make_async_copy(
                    result.at[e, c, j],
                    out_hbm.at[jnp.maximum(slots[e][0], 0), c, :, pl.ds(j * HALF, HALF)],
                    out_sem.at[e, c, j],
                )
            )
        return made

    for e in range(3):
        for c in range(3):
            gap = jnp.zeros((HALF - 16, SIDE), jnp.float32)
            block = jnp.concatenate([ring[e, c, 0], gap, ring[e, c, 1]], axis=0)
            sides = (block[:, :HALF].T, block[:, HALF:].T)
            load(e, c).wait()
            for j in range(2):
                lanes = high_lanes if j else low_lanes
                for t in range(SIDE // 8):
                    rows = slice(8 * t, 8 * t + 8)
                    within = slice(8 * t % HALF, 8 * t % HALF + 8)
                    value = jnp.where(lanes, sides[t // 16][within], result[e, c, j, rows, :])
                    if t == 0:
                        value = jnp.where(
                            sub_rows < 4, ring[e, c, 2, :, j * HALF : (j + 1) * HALF], value
                        )
                    if t == SIDE // 8 - 1:
                        value = jnp.where(
                            sub_rows >= 4, ring[e, c, 3, :, j * HALF : (j + 1) * HALF], value
                        )
                    result[e, c, j, rows, :] = value

            @pl.when(slots[e][1])
            def _(e=e, c=c):
                for copy in stores(e, c):
                    copy.start()

    for e in range(3):

        @pl.when(slots[e][1])
        def _(e=e):
            for c in range(3):
                for copy in stores(e, c):
                    copy.wait()

    for s in (1, 2):
        pl.when(s >= count)(empties[s - 1].wait)


def body(coarse, parents, new_counts, neighbours, land_cover, class_diffusivity, class_growth):
    owners = lax.axis_size("owner")
    f32 = jnp.float32
    hbm = pl.BlockSpec(memory_space=pltpu.HBM)
    stage_buf = pltpu.VMEM((2, 3, 2, 2, HALF + 2 * PAD, HALF), f32)
    strip_buf = pltpu.VMEM((3, 8, 8, SIDE), f32)
    outer_buf = pltpu.VMEM((3, 8, 8, SIDE + HALF), f32)
    far_buf = pltpu.VMEM((3, 8, 8, HALF), f32)
    results = jax.ShapeDtypeStruct((3, 3, 2, SIDE, HALF), f32)
    rings = jax.ShapeDtypeStruct((3, 3, 4, 8, SIDE), f32)
    whole, outer = pl.pallas_call(
        functools.partial(kernel, owners),
        out_shape=(results, rings),
        in_specs=[hbm] * 7,
        out_specs=(hbm, hbm),
        scratch_shapes=[
            pltpu.SMEM((2,), jnp.int32),
            pltpu.SMEM((owners,), jnp.int32),
            pltpu.SMEM((4, 2 * owners), jnp.int32),
            pltpu.SMEM((CLASSES,), f32),
            pltpu.SMEM((CLASSES,), f32),
            pltpu.VMEM((4, 3, HALF, HALF), f32),
            pltpu.VMEM((4, SIDE, SIDE), jnp.int32),
            stage_buf,
            stage_buf,
            stage_buf,
            stage_buf,
            pltpu.VMEM((2, 2, 2, HALF, HALF), f32),
            pltpu.VMEM((2, 2, 2, HALF, HALF), f32),
            pltpu.VMEM((2, 3, 2, SIDE, HALF), f32),
            pltpu.VMEM((2, 3, 4, 8, SIDE), f32),
            strip_buf,
            strip_buf,
            strip_buf,
            strip_buf,
            pltpu.VMEM((8, 8, SIDE), f32),
            pltpu.VMEM((8, 8, SIDE), f32),
            pltpu.VMEM((8, 4, 16, HALF), f32),
            pltpu.VMEM((2 * REACH + 1, 8, HALF), f32),
            outer_buf,
            outer_buf,
            outer_buf,
            outer_buf,
            pltpu.VMEM((8, 8, SIDE + HALF), f32),
            pltpu.VMEM((8, 8, SIDE + HALF), f32),
            far_buf,
            far_buf,
            pltpu.VMEM((8, 8, HALF), f32),
            pltpu.VMEM((8, 8, HALF), f32),
            far_buf,
            pltpu.SemaphoreType.DMA((4,)),
            pltpu.SemaphoreType.DMA((5,)),
            pltpu.SemaphoreType.DMA,
            pltpu.SemaphoreType.DMA((4,)),
            pltpu.SemaphoreType.DMA((4,)),
            pltpu.SemaphoreType.DMA((2 * REACH,)),
            pltpu.SemaphoreType.DMA((2 * REACH,)),
            pltpu.SemaphoreType.DMA((3,)),
            pltpu.SemaphoreType.DMA((3,)),
            pltpu.SemaphoreType.DMA((3,)),
        ],
        compiler_params=pltpu.CompilerParams(
            collective_id=0, has_side_effects=True, vmem_limit_bytes=VMEM_LIMIT
        ),
        name="regrid_step",
    )(parents, new_counts, neighbours.T, class_diffusivity, class_growth, coarse, land_cover)
    return pl.pallas_call(
        merge_kernel,
        out_shape=jax.ShapeDtypeStruct((3, 3, SIDE, SIDE), f32),
        in_specs=[hbm] * 3,
        out_specs=hbm,
        scratch_shapes=[
            pltpu.SMEM((owners,), jnp.int32),
            pltpu.VMEM(results.shape, f32),
            pltpu.VMEM(rings.shape, f32),
            pltpu.VMEM((3, SIDE, SIDE), f32),
            pltpu.SemaphoreType.DMA,
            pltpu.SemaphoreType.DMA,
            pltpu.SemaphoreType.DMA((3, 3)),
            pltpu.SemaphoreType.DMA((3, 3, 2)),
            pltpu.SemaphoreType.DMA((2,)),
        ],
        compiler_params=pltpu.CompilerParams(vmem_limit_bytes=VMEM_LIMIT),
        name="merge_slots",
    )(new_counts, whole, outer)


def solution(mesh):
    return jax.shard_map(
        body,
        mesh=mesh,
        in_specs=(
            P("owner", None, None, None),
            P("owner"),
            P(),
            P(),
            P("owner", None, None),
            P(),
            P(),
        ),
        out_specs=P("owner", None, None, None),
        check_vma=False,
    )
```

```python
import functools

import jax
import jax.numpy as jnp
from jax import lax
from jax.experimental import pallas as pl
from jax.experimental.pallas import tpu as pltpu
from jax.sharding import PartitionSpec as P

SIDE = 256
HALF = 128
CLASSES = 11
PAD = 8
REACH = 6
VMEM_LIMIT = 62 * 1024 * 1024
WEIGHTS = (0.5, 0.5, 1.0, 1.0 / 6.0)
MESH = pl.DeviceIdType.MESH


def iota(shape, dim):
    return lax.broadcasted_iota(jnp.int32, shape, dim)


def phased(index):
    return 2 * (index & (HALF - 1)) + (index >> 7)


def prolong_weights(fine, coarse):
    near = fine >> 1
    second = jnp.clip(near + jnp.where((fine & 1) == 0, -1, 1), 0, HALF - 1)
    heavy = jnp.where(coarse == near, 0.75, 0.0)
    light = jnp.where(coarse == second, 0.25, 0.0)
    return (heavy + light).astype(jnp.bfloat16)


def split(block, axis):
    high = block.astype(jnp.bfloat16)
    low = (block - high.astype(jnp.float32)).astype(jnp.bfloat16)
    return jnp.concatenate([high, low], axis=axis)


def dot(a, b):
    return jnp.dot(a, b, preferred_element_type=jnp.float32)


def dot_t(a, b):
    return lax.dot_general(a, b, (((1,), (1,)), ((), ())), preferred_element_type=jnp.float32)


def table_of(ref):
    lane = iota((8, HALF), 1)
    table = jnp.zeros((8, HALF), jnp.float32)
    for number in range(CLASSES):
        table = jnp.where(lane == number, ref[number], table)
    return table


def pick_lanes(table, index):
    return jnp.take_along_axis(table, index, axis=1)


def look_up(classes, tables):
    index = classes.astype(jnp.int32)
    rows, columns = classes.shape
    found = []
    for table in tables:
        bands = []
        for r in range(0, rows, 8):
            blocks = [
                pick_lanes(table, index[r : r + 8, k : k + HALF]) for k in range(0, columns, HALF)
            ]
            bands.append(jnp.concatenate(blocks, axis=1))
        found.append(jnp.concatenate(bands, axis=0))
    return found


def scaled_rates(weight, x0, x1, x2, lap0, lap1, lap2, diffus, growth):
    dw = diffus * weight
    gw = growth * weight
    xw = x0 * weight
    r0 = dw * lap0 + (gw * x0) * (x1 - x0 - x2)
    r1 = (0.5 * dw) * lap1 + (0.4 * weight - x1 * (0.4 * weight + xw))
    r2 = dw * lap2 + (xw - (0.3 * weight) * x2)
    return r0, r1, r2


def combine(x, s2, s3, s4, rate):
    return (s2 + 2.0 * s3 + s4 - x) * (1.0 / 3.0) + rate


def kernel(
    owners,
    parents_hbm,
    counts_hbm,
    nb_hbm,
    diff_hbm,
    grow_hbm,
    coarse_ref,
    land_ref,
    result_out,
    ring_out,
    parents_ref,
    counts_ref,
    nb_ref,
    diff_ref,
    grow_ref,
    quads,
    land,
    x_buf,
    s2_buf,
    s3_buf,
    s4_buf,
    diffus_buf,
    growth_buf,
    result,
    ring,
    t0,
    t1,
    t2,
    t3,
    strip_diffus,
    strip_growth,
    wall_data,
    class_data,
    corner_data,
    h0,
    h1,
    h2,
    h3,
    outer_diffus,
    outer_growth,
    l0,
    l1,
    far_diffus,
    far_growth,
    k0,
    load_sem,
    small_sem,
    land_sem,
    face_send,
    face_recv,
    corner_send,
    corner_recv,
    pair_send,
    pair_recv,
    own_sem,
):
    me = lax.axis_index("owner")
    parity = me % 2
    partner = me + 1 - 2 * parity
    moving = 1 - parity
    steps = [by for far in range(1, REACH + 1) for by in (far, -far)]
    reach = [(me + by) % owners for by in steps]
    exists = [(me + by < owners) & (me + by >= 0) for by in steps]
    stages = (x_buf, s2_buf, s3_buf, s4_buf)
    strips = (t0, t1, t2, t3)
    outer = (h0, h1, h2, h3)

    loads = []
    for q in range(4):
        block = coarse_ref.at[0, :, pl.ds((q // 2) * HALF, HALF), pl.ds((q % 2) * HALF, HALF)]
        loads.append(pltpu.make_async_copy(block, quads.at[q], load_sem.at[q]))
    for load in loads:
        load.start()
    small = []
    pairs = (
        (parents_hbm, parents_ref),
        (counts_hbm, counts_ref),
        (nb_hbm, nb_ref),
        (diff_hbm, diff_ref),
        (grow_hbm, grow_ref),
    )
    for n, (src, dst) in enumerate(pairs):
        small.append(pltpu.make_async_copy(src, dst, small_sem.at[n]))
        small[n].start()
    land_load = pltpu.make_async_copy(land_ref, land.at[pl.ds(0, 3)], land_sem)
    land_load.start()
    barrier = pltpu.get_barrier_semaphore()
    for n in range(len(steps)):

        @pl.when(exists[n])
        def _(n=n):
            pl.semaphore_signal(barrier, inc=1, device_id=(reach[n],), device_id_type=MESH)


    shape = (SIDE, SIDE)
    columns_up = prolong_weights(iota(shape, 1), iota(shape, 0) & (HALF - 1))
    phases_across = prolong_weights(phased(iota(shape, 1)), iota(shape, 0) & (HALF - 1))
    phases_along = prolong_weights(phased(iota(shape, 0)), iota(shape, 1) & (HALF - 1))
    weave = jnp.where(phased(iota(shape, 0)) == iota(shape, 1), 1.0, 0.0).astype(jnp.bfloat16)
    unweave = jnp.where(phased(iota(shape, 1)) == iota(shape, 0), 1.0, 0.0).astype(jnp.bfloat16)
    edge = iota((16, SIDE), 0)
    edge = jnp.where(edge < 8, edge, SIDE + 7 - edge)
    edge_up = prolong_weights(edge, iota((16, SIDE), 1) & (HALF - 1))
    rim = iota((16, SIDE), 0)
    rim = jnp.where(rim < 8, rim, HALF + 7 - rim)
    rim_pick = jnp.where((iota((16, SIDE), 1) & (HALF - 1)) == rim, 1.0, 0.0).astype(jnp.bfloat16)
    edge_and_rim = jnp.concatenate([edge_up, rim_pick], axis=0)
    edge_pick = jnp.where(iota((16, SIDE), 1) == edge, 1.0, 0.0).astype(jnp.bfloat16)
    for buf in stages:
        for i in range(2):
            for c in range(3):
                for y in range(2):
                    for x in range(2):
                        buf[i, c, y, x, 0:PAD] = jnp.zeros((PAD, HALF), jnp.float32)
                        buf[i, c, y, x, PAD + HALF :] = jnp.zeros((PAD, HALF), jnp.float32)

    def face_copies(k):
        data = (wall_data, class_data)[k]
        ends = [
            (data.at[pl.ds(3, 2)], data.at[pl.ds(1, 2)]),
            (data.at[pl.ds(3, 2)], data.at[pl.ds(5, 2)]),
            (data.at[4], data.at[0]),
            (data.at[3], data.at[7]),
        ]
        made = []
        for n, (src, dst) in enumerate(ends):
            made.append(
                pltpu.make_async_remote_copy(
                    src_ref=src,
                    dst_ref=dst,
                    send_sem=face_send.at[k, n],
                    recv_sem=face_recv.at[k, n],
                    device_id=(reach[n],),
                    device_id_type=MESH,
                )
            )
        return made

    def corner_copies():
        made = []
        for n, by in enumerate(steps):
            made.append(
                pltpu.make_async_remote_copy(
                    src_ref=corner_data.at[REACH, pl.ds(0, 4)],
                    dst_ref=corner_data.at[REACH - by, pl.ds(0, 4)],
                    send_sem=corner_send.at[n],
                    recv_sem=corner_recv.at[n],
                    device_id=(reach[n],),
                    device_id_type=MESH,
                )
            )
        return made

    pl.semaphore_wait(barrier, sum(jnp.where(there, 1, 0) for there in exists))
    land_copy = pltpu.make_async_remote_copy(
        src_ref=land_ref.at[2 * (1 - parity)],
        dst_ref=land.at[3],
        send_sem=pair_send.at[0],
        recv_sem=pair_recv.at[0],
        device_id=(partner,),
        device_id_type=MESH,
    )
    land_copy.start()

    for load in loads + small:
        load.wait()
    parent = [parents_ref[i] % 4 for i in range(2)]
    edges = []
    for i in range(2):
        for c in range(3):
            block = quads[parent[i], c]
            across = dot_t(edge_and_rim, split(block, 1))
            along = dot(edge_and_rim, split(block, 0))
            edges += [across[0:16], along[0:16]]
            for f in range(4):
                rows = (across, along)[f // 2][16 + 8 * (f % 2) : 19 + 8 * (f % 2)]
                wall_data[3 + i, 9 * f + 3 * c : 9 * f + 3 * c + 3, :] = rows
    for n, copy in enumerate(face_copies(0)):
        pl.when(exists[n])(copy.start)
    edges = dot(split(jnp.concatenate(edges, axis=0), 1), columns_up).reshape(2, 3, 4, 8, SIDE)
    for c in range(3):
        t0[c] = jnp.concatenate([edges[0, c], edges[1, c]], axis=0)

    for i in range(2):
        for c in range(3):
            half_done = dot(split(quads[parent[i], c], 1), phases_across)
            fine = dot(phases_along, split(half_done, 0))
            for y in range(2):
                for x in range(2):
                    x_buf[i, c, y, x, PAD : PAD + HALF] = fine[
                        y * HALF : (y + 1) * HALF, x * HALF : (x + 1) * HALF
                    ]

    land_load.wait()
    land_copy.wait_recv()
    count = counts_ref[me]
    slots = []
    for i in range(2):
        even_slot = jnp.where(i >= count, 3, i)
        odd_slot = jnp.where(i - 2 + count < 0, 3, i - 2 + count)
        slots.append(jnp.where(parity == 0, even_slot, odd_slot))
    tables = (table_of(diff_ref), table_of(grow_ref))
    classes_of = []
    for i in range(2):
        classes = land[slots[i]].astype(jnp.float32).astype(jnp.bfloat16)
        classes_of.append(classes)
        rims = jnp.concatenate([dot_t(edge_pick, classes), dot(edge_pick, classes)], axis=0)
        d, g = look_up(rims, tables)
        for f in range(4):
            rows = slice(8 * f, 8 * f + 8)
            strip_diffus[4 * i + f] = d[rows]
            strip_growth[4 * i + f] = g[rows]
            for a in range(3):
                for j in range(2):
                    at = 6 * f + 2 * a + j
                    row = 8 * f + a
                    class_data[3 + i, at : at + 1, :] = rims[
                        row : row + 1, j * HALF : (j + 1) * HALF
                    ]

    lane8, sub8 = iota((8, HALF), 1), iota((8, HALF), 0)
    for i in range(2):
        for x in range(2):
            row = jnp.zeros((8, HALF), jnp.float32)
            for q in range(5):
                pf = 4 * i + x
                strip_of = t0[q, pf] if q < 3 else (strip_diffus, strip_growth)[q - 3][pf]
                for y in range(2):
                    cell = lane8 - (64 * y + 9 * q + 3 * sub8)
                    inside = (cell >= 0) & (cell < 3) & (sub8 < 3)
                    cell = jnp.clip(cell, 0, 2)
                    cell = HALF - 1 - cell if y else cell
                    part = pick_lanes(strip_of[:, y * HALF : (y + 1) * HALF], cell)
                    row = row + jnp.where(inside, part, 0.0)
            at = 2 * i + x
            corner_data[REACH, at : at + 1, :] = jnp.sum(row, axis=0, keepdims=True)

    for n, copy in enumerate(face_copies(1)):
        pl.when(exists[n])(copy.start)
    for n, copy in enumerate(corner_copies()):
        pl.when(exists[n])(copy.start)

    for i in range(2):
        classes = dot(classes_of[i], unweave).astype(jnp.bfloat16)
        for n in range(8):
            rows = slice(32 * n, 32 * n + 32)
            d, g = look_up(dot(weave[rows], classes), tables)
            y, m = n // 4, 32 * (n % 4)
            for x in range(2):
                diffus_buf[i, y, x, m : m + 32] = d[:, x * HALF : (x + 1) * HALF]
                growth_buf[i, y, x, m : m + 32] = g[:, x * HALF : (x + 1) * HALF]

    def cross(patch, face):
        value = nb_ref[face, patch]
        has = value >= 0
        return jnp.where(has, value, patch), jnp.where(has, face ^ 1, face)

    strip = (8, 8, SIDE)
    sub = iota(strip, 1)
    lane_half = iota((8, 8, HALF), 2)

    def gather_outer():
        first = [
            jnp.where(sub8 == 0, 1.0, jnp.where(sub8 == 1, 0.75, jnp.where(sub8 == 2, 0.25, 0.0))),
            jnp.where(sub8 == 0, 0.0, jnp.where(sub8 == 1, 0.25, 0.75)),
            jnp.where(sub8 >= 3, 0.25, 0.0),
        ]
        index = {}
        for kind in range(2):
            for e in range(2):
                b = jnp.minimum(lane8 if e else HALF - 1 - lane8, 2)
                a = jnp.minimum(sub8, 2)
                index[kind, e] = 3 * a + b if kind == 0 else 3 * b + a
        walls, classes = [], []
        for i in range(2):
            for f in range(4):
                patch, face = cross(2 * me + i, f)
                where = jnp.clip(patch - (2 * me - 3), 0, 7)
                for c in range(3):
                    parts = []
                    for a in range(3):
                        row = wall_data[where, pl.ds(9 * face + 3 * c + a, 1), :]
                        parts.append(first[a] * jnp.broadcast_to(row, (8, HALF)))
                    walls.append(parts[0] + parts[1] + parts[2])
                for j in range(2):
                    rows = []
                    for a in range(3):
                        row = class_data[where, pl.ds(6 * face + 2 * a + j, 1), :]
                        rows.append(jnp.broadcast_to(row, (8, HALF)))
                    classes.append(jnp.where(sub8 == 0, rows[0], jnp.where(sub8 == 1, rows[1], rows[2])))
        walls = dot(split(jnp.concatenate(walls, axis=0), 1), columns_up).reshape(8, 3, 8, SIDE)
        d, g = look_up(jnp.concatenate(classes, axis=0), tables)
        d, g = d.reshape(8, 2, 8, HALF), g.reshape(8, 2, 8, HALF)
        for c in range(3):
            h0[c, :, :, 0:SIDE] = walls[:, c]
        for j in range(2):
            at = slice(j * HALF, HALF + j * HALF)
            outer_diffus[:, :, at] = d[:, j]
            outer_growth[:, :, at] = g[:, j]

        low_half = lane8 < HALF // 2
        for i in range(2):
            for f in range(4):
                pf = 4 * i + f
                kind = f // 2
                start = cross(2 * me + i, f)
                chains = []
                for e in range(2):
                    patch, wall = start
                    side = 2 * (1 - kind) + e
                    chain = []
                    for step in range(3):
                        if step % 2 == 0:
                            patch, side = cross(patch, side)
                        else:
                            patch, wall = cross(patch, wall)
                        x = wall if kind == 0 else side
                        y = (side if kind == 0 else wall) - 2
                        window = jnp.clip((patch >> 1) - me + REACH, 0, 2 * REACH)
                        row = corner_data[window, pl.ds(2 * (patch & 1) + x, 1), :]
                        row = jnp.broadcast_to(row, (8, HALF))
                        chain.append(jnp.where(y == 1, pltpu.roll(row, 64, 1), row))
                    chains.append(chain)
                for step in range(3):
                    for q in range(5 if step < 2 else 3):
                        tiles = []
                        for e in range(2):
                            if step < 2:
                                at = index[kind, e] + 9 * q
                            else:
                                at = jnp.full((8, HALF), 9 * q, jnp.int32)
                            tiles.append(pick_lanes(chains[e][step], at))
                        if step < 2:
                            tile = jnp.where(low_half, tiles[1], tiles[0])
                        else:
                            tile = jnp.where(low_half, tiles[0], tiles[1])
                        if step == 0 and q < 3:
                            h0[q, pf, :, SIDE:] = tile
                        elif step == 0:
                            (outer_diffus, outer_growth)[q - 3][pf, :, SIDE:] = tile
                        elif step == 1 and q < 3:
                            l0[q, pf] = tile
                        elif step == 1:
                            (far_diffus, far_growth)[q - 3][pf] = tile
                        else:
                            k0[q, pf] = tile

    def rates_of(s, now, laps, diffus, growth):
        return scaled_rates(WEIGHTS[s], *now, *laps, diffus, growth)

    rising = iota((8, HALF), 0)
    falling = HALF - 1 - rising

    def strip_laplacian(now, beyond):
        ghost = jnp.broadcast_to(beyond[:, 0:1, :], strip)
        ends = []
        for e in range(2):
            columns = []
            for i in range(2):
                for f in range(4):
                    face = ghost[4 * i + (2 if f < 2 else 0) + e]
                    if f % 2:
                        columns.append(pick_lanes(face[:, HALF:], falling))
                    else:
                        columns.append(pick_lanes(face[:, :HALF], rising))
            ends.append(jnp.stack(columns, axis=0))
        above = jnp.where(sub == 0, ghost, pltpu.roll(now, 1, 1))
        below = pltpu.roll(now, 7, 1)
        rolled = pltpu.roll(now, 1, 2)
        left = jnp.where(lane_half == 0, ends[0], rolled[:, :, :HALF])
        left = jnp.concatenate([left, rolled[:, :, HALF:]], axis=2)
        rolled = pltpu.roll(now, SIDE - 1, 2)
        right = jnp.where(lane_half == HALF - 1, ends[1], rolled[:, :, HALF:])
        right = jnp.concatenate([rolled[:, :, :HALF], right], axis=2)
        return (left + right) + (below + above) - 4.0 * now

    def round_laplacian(now, facing):
        lanes = now.shape[2]
        above = jnp.where(iota(now.shape, 1) == 0, facing, pltpu.roll(now, 1, 1))
        below = pltpu.roll(now, 7, 1)
        sides = pltpu.roll(now, 1, 2) + pltpu.roll(now, lanes - 1, 2)
        return sides + (below + above) - 4.0 * now

    def strip_stage(s):
        inner = [strips[s][c] for c in range(3)]
        beyond = [outer[s][c, :, :, 0:SIDE] for c in range(3)]
        laps = [strip_laplacian(inner[c], beyond[c]) for c in range(3)]
        rates = rates_of(s, inner, laps, strip_diffus[...], strip_growth[...])
        if s == 3:
            for c in range(3):
                block = combine(t0[c], t1[c], t2[c], t3[c], rates[c])
                for i in range(2):
                    ring[i, c] = block[4 * i : 4 * i + 4]
                    for f in (1, 3):
                        for r in range(4):
                            ring[i, c, f, 7 - r : 8 - r, :] = block[4 * i + f, r : r + 1, :]
            return
        for c in range(3):
            strips[s + 1][c] = t0[c] + rates[c]
        if s == 2:
            laps = []
            for c in range(3):
                whole = outer[s][c]
                now = beyond[c]
                above = jnp.where(sub == 0, inner[c], pltpu.roll(now, 1, 1))
                sides = pltpu.roll(whole, 1, 2) + pltpu.roll(whole, SIDE + HALF - 1, 2)
                laps.append(sides[:, :, 0:SIDE] + (pltpu.roll(now, 7, 1) + above) - 4.0 * now)
            rates = rates_of(
                s, beyond, laps, outer_diffus[:, :, 0:SIDE], outer_growth[:, :, 0:SIDE]
            )
            for c in range(3):
                outer[3][c, :, :, 0:SIDE] = h0[c, :, :, 0:SIDE] + rates[c]
            return
        far = [(l0, l1)[s][c] for c in range(3)]
        now = [outer[s][c] for c in range(3)]
        laps = [
            round_laplacian(now[c], jnp.concatenate([inner[c], far[c]], axis=2)) for c in range(3)
        ]
        rates = rates_of(s, now, laps, outer_diffus[...], outer_growth[...])
        for c in range(3):
            outer[s + 1][c] = h0[c] + rates[c]
        if s == 0:
            laps = []
            for c in range(3):
                both = jnp.concatenate([far[c], k0[c]], axis=2)
                facing = jnp.concatenate([now[c][:, :, SIDE:], k0[c]], axis=2)
                laps.append(round_laplacian(both, facing)[:, :, :HALF])
            rates = rates_of(s, far, laps, far_diffus[...], far_growth[...])
            for c in range(3):
                l1[c] = far[c] + rates[c]

    def bulk_stage(i, s):
        src = stages[s]
        dst = stages[(s + 1) % 4] if s < 3 else s2_buf

        def step_rows(step, carry):
            r = pl.multiple_of(step * 8, 8)
            at = PAD + r
            here = pl.ds(at, 8)
            now = [[src[i, c, n // 2, n % 2, here, :] for n in range(4)] for c in range(3)]
            lap = [[None] * 4 for _ in range(3)]
            for c in range(3):
                for n in range(4):
                    y, x = n // 2, n % 2
                    beside = now[c][2 * y + 1 - x]
                    beyond = pltpu.roll(beside, HALF - 1 if x else 1, 1)
                    upright = now[c][2 * (1 - y) + x]
                    further = src[i, c, 1 - y, x, pl.ds(at + 2 * y - 1, 8), :]
                    lap[c][n] = (beside + beyond) + (upright + further) - 4.0 * now[c][n]
            for n in range(4):
                y, x = n // 2, n % 2
                rates = scaled_rates(
                    WEIGHTS[s],
                    *[now[c][n] for c in range(3)],
                    *[lap[c][n] for c in range(3)],
                    diffus_buf[i, y, x, pl.ds(r, 8), :],
                    growth_buf[i, y, x, pl.ds(r, 8), :],
                )
                for c in range(3):
                    base = now[c][n] if s == 0 else x_buf[i, c, y, x, here, :]
                    if s < 3:
                        value = base + rates[c]
                    else:
                        value = combine(
                            base,
                            s2_buf[i, c, y, x, here, :],
                            s3_buf[i, c, y, x, here, :],
                            now[c][n],
                            rates[c],
                        )
                    dst[i, c, y, x, here, :] = value
            return carry

        lax.fori_loop(0, HALF // 8, step_rows, 0, unroll=16)

    def bulk_weave(i):
        for c in range(3):
            for y in range(2):
                both = jnp.concatenate(
                    [s2_buf[i, c, y, x, PAD : PAD + HALF, :] for x in range(2)], axis=1
                )
                high = both.astype(jnp.bfloat16)
                low = (both - high.astype(jnp.float32)).astype(jnp.bfloat16)
                woven = dot(high, weave) + dot(low, weave)
                for j in range(2):
                    result[i, c, j, pl.ds(y, HALF, stride=2), :] = woven[:, j * HALF : (j + 1) * HALF]

    def to_partner(n, src, dst):
        return pltpu.make_async_remote_copy(
            src_ref=src.at[moving],
            dst_ref=dst.at[2],
            send_sem=pair_send.at[n],
            recv_sem=pair_recv.at[n],
            device_id=(partner,),
            device_id_type=MESH,
        )

    result_copy = to_partner(1, result, result_out)
    ring_copy = to_partner(2, ring, ring_out)
    own_copies = [
        pltpu.make_async_copy(result.at[moving], result_out.at[moving], own_sem.at[0]),
        pltpu.make_async_copy(ring, ring_out.at[pl.ds(0, 2)], own_sem.at[1]),
        pltpu.make_async_copy(result.at[parity], result_out.at[parity], own_sem.at[2]),
    ]
    for s in range(4):
        bulk_stage(moving, s)
    bulk_weave(moving)
    result_copy.start()
    own_copies[0].start()
    for s in range(4):
        bulk_stage(parity, s)
    for n, copy in enumerate(face_copies(0) + face_copies(1)):
        pl.when(exists[n % 4 ^ 1])(copy.wait_recv)
    for n, copy in enumerate(corner_copies()):
        pl.when(exists[n ^ 1])(copy.wait_recv)
    gather_outer()
    for s in range(4):
        strip_stage(s)
    ring_copy.start()
    own_copies[1].start()
    bulk_weave(parity)
    own_copies[2].start()
    for n, copy in enumerate(face_copies(0) + face_copies(1)):
        pl.when(exists[n % 4])(copy.wait_send)
    for n, copy in enumerate(corner_copies()):
        pl.when(exists[n])(copy.wait_send)
    land_copy.wait_send()
    for copy in own_copies:
        copy.wait()
    result_copy.wait()
    ring_copy.wait()


def merge_kernel(
    counts_hbm,
    result_hbm,
    ring_hbm,
    out_hbm,
    counts_ref,
    result,
    ring,
    zeros,
    count_sem,
    ring_sem,
    result_sem,
    out_sem,
    zero_sem,
):
    me = lax.axis_index("owner")
    even = me % 2 == 0
    count_copy = pltpu.make_async_copy(counts_hbm, counts_ref, count_sem)
    ring_copy = pltpu.make_async_copy(ring_hbm, ring, ring_sem)
    count_copy.start()
    ring_copy.start()

    def load(e, c):
        return pltpu.make_async_copy(result_hbm.at[e, c], result.at[e, c], result_sem.at[e, c])

    for e in range(3):
        for c in range(3):
            load(e, c).start()
    zeros[...] = jnp.zeros_like(zeros)
    count_copy.wait()
    count = counts_ref[me]
    empties = []
    for s in (1, 2):
        empties.append(pltpu.make_async_copy(zeros, out_hbm.at[s], zero_sem.at[s - 1]))
        pl.when(s >= count)(empties[-1].start)

    slots = []
    for e in range(3):
        slot = jnp.where(even, e, (e + 1) % 3 + count - 3)
        slots.append((slot, (slot >= 0) & (slot < count)))
    low_lanes = iota((8, HALF), 1) < 4
    high_lanes = iota((8, HALF), 1) >= HALF - 4
    sub_rows = iota((8, HALF), 0)
    ring_copy.wait()

    def stores(e, c):
        made = []
        for j in range(2):
            made.append(
                pltpu.make_async_copy(
                    result.at[e, c, j],
                    out_hbm.at[jnp.maximum(slots[e][0], 0), c, :, pl.ds(j * HALF, HALF)],
                    out_sem.at[e, c, j],
                )
            )
        return made

    for e in range(3):
        for c in range(3):
            gap = jnp.zeros((HALF - 16, SIDE), jnp.float32)
            block = jnp.concatenate([ring[e, c, 0], gap, ring[e, c, 1]], axis=0)
            sides = (block[:, :HALF].T, block[:, HALF:].T)
            load(e, c).wait()
            for j in range(2):
                lanes = high_lanes if j else low_lanes
                for t in range(SIDE // 8):
                    rows = slice(8 * t, 8 * t + 8)
                    within = slice(8 * t % HALF, 8 * t % HALF + 8)
                    value = jnp.where(lanes, sides[t // 16][within], result[e, c, j, rows, :])
                    if t == 0:
                        value = jnp.where(
                            sub_rows < 4, ring[e, c, 2, :, j * HALF : (j + 1) * HALF], value
                        )
                    if t == SIDE // 8 - 1:
                        value = jnp.where(
                            sub_rows >= 4, ring[e, c, 3, :, j * HALF : (j + 1) * HALF], value
                        )
                    result[e, c, j, rows, :] = value

            @pl.when(slots[e][1])
            def _(e=e, c=c):
                for copy in stores(e, c):
                    copy.start()

    for e in range(3):

        @pl.when(slots[e][1])
        def _(e=e):
            for c in range(3):
                for copy in stores(e, c):
                    copy.wait()

    for s in (1, 2):
        pl.when(s >= count)(empties[s - 1].wait)


def body(coarse, parents, new_counts, neighbours, land_cover, class_diffusivity, class_growth):
    owners = lax.axis_size("owner")
    f32 = jnp.float32
    hbm = pl.BlockSpec(memory_space=pltpu.HBM)
    stage_buf = pltpu.VMEM((2, 3, 2, 2, HALF + 2 * PAD, HALF), f32)
    strip_buf = pltpu.VMEM((3, 8, 8, SIDE), f32)
    outer_buf = pltpu.VMEM((3, 8, 8, SIDE + HALF), f32)
    far_buf = pltpu.VMEM((3, 8, 8, HALF), f32)
    results = jax.ShapeDtypeStruct((3, 3, 2, SIDE, HALF), f32)
    rings = jax.ShapeDtypeStruct((3, 3, 4, 8, SIDE), f32)
    whole, outer = pl.pallas_call(
        functools.partial(kernel, owners),
        out_shape=(results, rings),
        in_specs=[hbm] * 7,
        out_specs=(hbm, hbm),
        scratch_shapes=[
            pltpu.SMEM((2,), jnp.int32),
            pltpu.SMEM((owners,), jnp.int32),
            pltpu.SMEM((4, 2 * owners), jnp.int32),
            pltpu.SMEM((CLASSES,), f32),
            pltpu.SMEM((CLASSES,), f32),
            pltpu.VMEM((4, 3, HALF, HALF), f32),
            pltpu.VMEM((4, SIDE, SIDE), jnp.int32),
            stage_buf,
            stage_buf,
            stage_buf,
            stage_buf,
            pltpu.VMEM((2, 2, 2, HALF, HALF), f32),
            pltpu.VMEM((2, 2, 2, HALF, HALF), f32),
            pltpu.VMEM((2, 3, 2, SIDE, HALF), f32),
            pltpu.VMEM((2, 3, 4, 8, SIDE), f32),
            strip_buf,
            strip_buf,
            strip_buf,
            strip_buf,
            pltpu.VMEM((8, 8, SIDE), f32),
            pltpu.VMEM((8, 8, SIDE), f32),
            pltpu.VMEM((8, 36, HALF), f32),
            pltpu.VMEM((8, 24, HALF), f32),
            pltpu.VMEM((2 * REACH + 1, 8, HALF), f32),
            outer_buf,
            outer_buf,
            outer_buf,
            outer_buf,
            pltpu.VMEM((8, 8, SIDE + HALF), f32),
            pltpu.VMEM((8, 8, SIDE + HALF), f32),
            far_buf,
            far_buf,
            pltpu.VMEM((8, 8, HALF), f32),
            pltpu.VMEM((8, 8, HALF), f32),
            far_buf,
            pltpu.SemaphoreType.DMA((4,)),
            pltpu.SemaphoreType.DMA((5,)),
            pltpu.SemaphoreType.DMA,
            pltpu.SemaphoreType.DMA((2, 4)),
            pltpu.SemaphoreType.DMA((2, 4)),
            pltpu.SemaphoreType.DMA((2 * REACH,)),
            pltpu.SemaphoreType.DMA((2 * REACH,)),
            pltpu.SemaphoreType.DMA((3,)),
            pltpu.SemaphoreType.DMA((3,)),
            pltpu.SemaphoreType.DMA((3,)),
        ],
        compiler_params=pltpu.CompilerParams(
            collective_id=0, has_side_effects=True, vmem_limit_bytes=VMEM_LIMIT
        ),
        name="regrid_step",
    )(parents, new_counts, neighbours.T, class_diffusivity, class_growth, coarse, land_cover)
    return pl.pallas_call(
        merge_kernel,
        out_shape=jax.ShapeDtypeStruct((3, 3, SIDE, SIDE), f32),
        in_specs=[hbm] * 3,
        out_specs=hbm,
        scratch_shapes=[
            pltpu.SMEM((owners,), jnp.int32),
            pltpu.VMEM(results.shape, f32),
            pltpu.VMEM(rings.shape, f32),
            pltpu.VMEM((3, SIDE, SIDE), f32),
            pltpu.SemaphoreType.DMA,
            pltpu.SemaphoreType.DMA,
            pltpu.SemaphoreType.DMA((3, 3)),
            pltpu.SemaphoreType.DMA((3, 3, 2)),
            pltpu.SemaphoreType.DMA((2,)),
        ],
        compiler_params=pltpu.CompilerParams(vmem_limit_bytes=VMEM_LIMIT),
        name="merge_slots",
    )(new_counts, whole, outer)


def solution(mesh):
    return jax.shard_map(
        body,
        mesh=mesh,
        in_specs=(
            P("owner", None, None, None),
            P("owner"),
            P(),
            P(),
            P("owner", None, None),
            P(),
            P(),
        ),
        out_specs=P("owner", None, None, None),
        check_vma=False,
    )
```
